32 devices in a mesh: groups: 2 (over x), seq: 16 (over z, y, core).
Axes of the slice: x: 2, y: 2, z: 4, core: 2. Of those that a mesh axis runs over, the one named last changes fastest.
Arguments:
- x_in: bfloat16 [4096, 4096], P(('groups', 'seq')), parts along dimension 0, may hold values from -6 to 6
- bc_in: bfloat16 [4096, 1024], P(('groups', 'seq')), parts along dimension 0, may hold values from -6 to 6
- z_in: bfloat16 [4096, 4096], P(('groups', 'seq')), parts along dimension 0, may hold values from -6 to 6
- dt_in: bfloat16 [4096, 128], P(('groups', 'seq')), parts along dimension 0, may hold values from -4 to 4
- conv_weight: float32 [4, 5120], replicated, may hold values from -3 to 3
- conv_bias: float32 [5120], replicated, may hold values from -3 to 3
- dt_bias: float32 [128], replicated, may hold values from -4 to -2
- a_log: float32 [128], replicated, may hold values from -11.5 to 0
- d_skip: float32 [128], replicated, may hold values from 0.5 to 1.5
- norm_gain: float32 [4096], replicated, may hold values from 0.5 to 1.5
- conv_cache: bfloat16 [6, 5120], P('groups'), parts along dimension 0, may hold values from -6 to 6
- cache_state: float32 [256, 32, 64], P('groups'), parts along dimension 0, may hold values from -6 to 6
- lengths: int32 [2], P('groups'), parts along dimension 0, may hold values from 1924 to 2048
Outputs:
- mixed: bfloat16 [4096, 4096], P(('groups', 'seq')), parts along dimension 0
- final_state: float32 [256, 32, 64], P(('groups', 'seq')), parts along dimension 0
The draws below stay inside these ranges and needn't reach their ends.
There are 2 independent parts, one for each index of `groups`. The reference program is written for one: setup_inputs(seed, part) draws one part's arguments, and reference() takes and returns one part's arrays. A program takes and returns all parts, laid end to end along the dimension named above; an argument that names none is the same for every part. Nothing has to cross between parts.
All inputs are finite; a program needn't handle non-finite values.
Results may differ from the reference program's by a relative error of at most 0.0085.
Values may be sent and summed in bfloat16 or wider, within the bound.
No kernel may reach another device: no remote copies, remote signals or barrier semaphores. Data moves between devices by JAX's collectives and lax.ppermute only.
A program may use at most 64 MiB of HBM per device.

```python
import jax
import jax.numpy as jnp
from jax import lax

HEADS = 128
HEAD_DIM = 32
STATE = 64
GROUPS = 8
CONV_W = 4
TOK_DEV = 128
TOKENS = 2048
INNER = 4096
CONV_CH = 5120


def level_of(key, extent, split, smallest, top_value):
    level = 1.0
    for dim, shards_of in split:
        draws = jax.random.uniform(jax.random.fold_in(jax.random.fold_in(key, 6), dim), (shards_of,), jnp.float32, smallest / len(split), top_value / len(split))
        level = level * jnp.repeat(jnp.exp(draws), extent[dim] // shards_of).reshape((-1,) + (1,) * (len(extent) - 1 - dim))
    return level


def gaussian(key, dims, deviation, reach, shards=(), held_as=jnp.bfloat16):
    factor_of = level_of(key, dims, shards, -0.22, 0.18) if shards else 1.0
    array = jax.random.normal(key, dims, jnp.float32) * deviation * factor_of
    return jnp.minimum(jnp.maximum(array, -reach), reach).astype(held_as)


def setup_inputs(seed: int = 0, part: int = 0) -> dict:
    key_of = jax.random.split(jax.random.key(seed), 14)
    own_keys = jax.random.split(jax.random.fold_in(key_of[13], part), 14)
    return {
        "x_in": gaussian(own_keys[0], (TOKENS, INNER), 1.0, 6.0, ((0, 16),)),
        "bc_in": gaussian(own_keys[1], (TOKENS, 2 * GROUPS * STATE), 1.0, 6.0, ((0, 16),)),
        "z_in": gaussian(own_keys[2], (TOKENS, INNER), 1.0, 6.0, ((0, 16),)),
        "dt_in": gaussian(own_keys[3], (TOKENS, HEADS), 1.0, 4.0, ((0, 16),)),
        "conv_weight": gaussian(key_of[4], (CONV_W, CONV_CH), CONV_W ** -0.5, 3.0, (), jnp.float32),
        "conv_bias": gaussian(key_of[5], (CONV_CH,), 0.5, 3.0, (), jnp.float32),
        "dt_bias": jnp.clip(jax.random.uniform(key_of[6], (HEADS,), jnp.float32, -4.0, -2.0), -4.0, -2.0),
        "a_log": jnp.clip(jax.random.uniform(key_of[7], (HEADS,), jnp.float32, -11.5, 0.0), -11.5, 0.0),
        "d_skip": jnp.clip(jax.random.uniform(key_of[8], (HEADS,), jnp.float32, 0.5, 1.5), 0.5, 1.5),
        "norm_gain": jnp.clip(1.0 + 0.1 * jax.random.normal(key_of[9], (INNER,), jnp.float32), 0.5, 1.5),
        "conv_cache": gaussian(own_keys[10], (CONV_W - 1, CONV_CH), 1.0, 6.0),
        "cache_state": gaussian(own_keys[11], (HEADS, HEAD_DIM, STATE), 1.0, 6.0, (), jnp.float32),
        "lengths": jax.random.randint(own_keys[12], (1,), TOKENS - TOK_DEV + CONV_W, TOKENS + 1).astype(jnp.int32),
    }


def conv_silu(extended, conv_weight, conv_bias, count):
    total = jnp.zeros((count, extended.shape[1]), jnp.float32) + conv_bias[None, :]
    for offset in range(CONV_W):
        total = total + extended[offset:offset + count].astype(jnp.float32) * conv_weight[offset][None, :]
    return jax.nn.silu(total).astype(jnp.bfloat16)

def block_step(state, pieces, decay_rate, d_skip):
    x_block, b_block, c_block, dt_block = pieces
    per_group = HEADS // GROUPS
    block_len = x_block.shape[0]
    hi_prec = lax.Precision.HIGHEST
    cum_rate = jnp.cumsum(dt_block * decay_rate[None, :], axis=0)
    lower_mask = jnp.arange(block_len)[:, None] >= jnp.arange(block_len)[None, :]
    gap_rate = cum_rate.T[:, :, None] - cum_rate.T[:, None, :]
    decay = jnp.exp(jnp.where(lower_mask[None], gap_rate, -1e+30))
    c_dot_b = jnp.einsum('tgn,sgn->gts', c_block.astype(jnp.float32), b_block.astype(jnp.float32), precision=hi_prec)
    c_dot_b = jnp.repeat(c_dot_b, per_group, axis=0)
    weight = lax.optimization_barrier((c_dot_b * decay * dt_block.T[:, None, :]).astype(jnp.bfloat16))
    x_float = x_block.astype(jnp.float32)
    y_diag = jnp.einsum('hts,shp->thp', weight.astype(jnp.float32), x_float, precision=hi_prec)
    c_heads = jnp.repeat(c_block.astype(jnp.float32), per_group, axis=1)
    y_enter = jnp.exp(cum_rate)[:, :, None] * jnp.einsum('thn,hpn->thp', c_heads, state, precision=hi_prec)
    y_block = y_diag + y_enter + d_skip[None, :, None] * x_float
    tail = jnp.exp(cum_rate[-1][None, :] - cum_rate) * dt_block
    b_heads = jnp.repeat(b_block.astype(jnp.float32), per_group, axis=1)
    b_weighted = lax.optimization_barrier((b_heads * tail[:, :, None]).astype(jnp.bfloat16))
    local = jnp.einsum('shp,shn->hpn', x_float, b_weighted.astype(jnp.float32), precision=hi_prec)
    new_state = jnp.exp(cum_rate[-1])[:, None, None] * state + local
    return (new_state, y_block)

def reference(x_in, bc_in, z_in, dt_in, conv_weight, conv_bias, dt_bias, a_log, d_skip, norm_gain, conv_cache, cache_state, lengths):
    inputs = jnp.concatenate([x_in, bc_in], axis=1)
    extended = jnp.concatenate([conv_cache, inputs], axis=0)
    convolved = conv_silu(extended, conv_weight, conv_bias, TOKENS)
    x_conv = convolved[:, :INNER].reshape(TOKENS, HEADS, HEAD_DIM)
    b_conv = convolved[:, INNER:INNER + GROUPS * STATE].reshape(TOKENS, GROUPS, STATE)
    c_conv = convolved[:, INNER + GROUPS * STATE:].reshape(TOKENS, GROUPS, STATE)
    live = (jnp.arange(TOKENS) < lengths[0]).astype(jnp.float32)
    step_size = jax.nn.softplus(dt_in.astype(jnp.float32) + dt_bias[None, :]) * live[:, None]
    decay_rate = -jnp.exp(a_log)
    blocks = TOKENS // TOK_DEV
    pieces = (x_conv.reshape(blocks, TOK_DEV, HEADS, HEAD_DIM), b_conv.reshape(blocks, TOK_DEV, GROUPS, STATE), c_conv.reshape(blocks, TOK_DEV, GROUPS, STATE), step_size.reshape(blocks, TOK_DEV, HEADS))

    def scan_step(state, piece):
        return block_step(state, piece, decay_rate, d_skip)
    final_state, y_blocks = lax.scan(scan_step, cache_state, pieces)
    y_out = lax.optimization_barrier((y_blocks.reshape(TOKENS, INNER) * live[:, None]).astype(jnp.bfloat16))
    gated = y_out.astype(jnp.float32) * jax.nn.silu(z_in.astype(jnp.float32))
    grouped = gated.reshape(TOKENS, GROUPS, INNER // GROUPS)
    scale = lax.rsqrt(lax.optimization_barrier(jnp.mean(grouped * grouped, axis=-1, keepdims=True)) + 1e-05)
    mixed = (grouped * scale).reshape(TOKENS, INNER) * norm_gain[None, :]
    return (mixed.astype(jnp.bfloat16), final_state)
```

```python
import functools

import jax
import jax.numpy as jnp
from jax import lax
from jax.experimental import pallas as pl
from jax.experimental.pallas import tpu as pltpu
from jax.sharding import PartitionSpec as P

STATE = 64
GROUPS = 8
CONV_W = 4
RIM = CONV_W - 1
LOG2E = 1.4426950408889634
BF16 = jnp.bfloat16
F32 = jnp.float32
HI = lax.Precision.HIGHEST
SEQ = "seq"
PAIR = 2
TOP = 16


def silu(v):
    half = 0.5 * v
    return half + half * jnp.tanh(half)


def split2(v):
    hi = v.astype(BF16)
    return hi, (v - hi.astype(F32)).astype(BF16)


def grid_call(body, grid, in_specs, out_specs, out_shape, scratch=(), flops=0, nbytes=0, vmem=24):
    return pl.pallas_call(
        body,
        grid=grid,
        in_specs=in_specs,
        out_specs=out_specs,
        out_shape=out_shape,
        scratch_shapes=list(scratch),
        compiler_params=pltpu.CompilerParams(vmem_limit_bytes=vmem * 2**20),
        cost_estimate=pl.CostEstimate(flops=flops, bytes_accessed=nbytes, transcendentals=0),
    )


def conv_rows(ext, weights, bias, count, first, cols):
    total = jnp.broadcast_to(bias, (count, bias.shape[1]))
    for k in range(CONV_W):
        total = total + ext[pl.ds(first + k - RIM, count), cols] * weights[k : k + 1, :]
    return silu(total)


def conv_kernel(
    len_ref,
    x_ref,
    b_ref,
    c_ref,
    dt_ref,
    wx_ref,
    wb_ref,
    wc_ref,
    cx_ref,
    cb_ref,
    cc_ref,
    dtb_ref,
    alog_ref,
    xo_ref,
    bo_ref,
    co_ref,
    cum_ref,
    row_ref,
    tail_ref,
    ecum_ref,
    dec_ref,
    ext,
    *,
    heads,
    head_dim,
):
    step = pl.program_id(0)
    rows = x_ref.shape[0]
    per_step = heads // pl.num_programs(0)

    def conv(src, w, bias, dst):
        width = src.shape[1]
        for j in range(width // 128):
            cols = pl.ds(128 * j, 128)
            ext[8:, :] = src[:, cols].astype(F32)
            weights, offset = w[:, cols], bias[:, cols]
            dst[:, cols] = conv_rows(ext, weights, offset, rows, 8, slice(None)).astype(BF16)

    ext[0:8, :] = jnp.zeros((8, 128), F32)

    @pl.when(step == 0)
    def _():
        raw = dt_ref[...].astype(F32) + dtb_ref[...]
        soft = jnp.maximum(raw, 0.0) + jnp.log1p(jnp.exp(-jnp.abs(raw)))
        first = lax.axis_index(SEQ) * rows
        token = first + lax.broadcasted_iota(jnp.int32, (rows, heads), 0)
        dt = jnp.where(token < len_ref[0], soft, 0.0)
        rate = -jnp.exp(alog_ref[...]) * dt
        below = lax.broadcasted_iota(jnp.int32, (rows, rows), 0)
        across = lax.broadcasted_iota(jnp.int32, (rows, rows), 1)
        tri = (below >= across).astype(F32)
        cum = jnp.dot(tri, rate, precision=HI, preferred_element_type=F32)
        last = cum[rows - 1 : rows, :]
        tail = jnp.exp(last - cum) * dt
        ecum = jnp.exp(cum)
        cum_ref[...] = cum * LOG2E
        log_dt = jnp.where(dt > 0.0, jnp.log(jnp.maximum(dt, 1e-38)) * LOG2E, -1e30)
        row_ref[...] = (cum * LOG2E - log_dt).T
        tail_hi, tail_lo = split2(tail)
        ecum_hi, ecum_lo = split2(ecum)
        for i in range(heads // per_step):
            part = slice(i * per_step, (i + 1) * per_step)
            tail_ref[i] = jnp.concatenate([tail_hi[:, part], tail_lo[:, part]], axis=1)
            ecum_ref[i] = jnp.concatenate([ecum_hi[:, part], ecum_lo[:, part]], axis=1)
        steps = heads // per_step
        unit_heads = per_step // (2 * PAIR)
        unit_cols = unit_heads * head_dim
        owner = lax.broadcasted_iota(jnp.int32, (8, heads), 0)
        head = lax.broadcasted_iota(jnp.int32, (8, heads), 1)
        chosen = jnp.where(head // per_step == owner, jnp.exp(last), 0.0)
        head = lax.broadcasted_iota(jnp.int32, (heads, unit_cols), 0)
        lane = lax.broadcasted_iota(jnp.int32, (heads, unit_cols), 1)
        same = head % unit_heads == lane // head_dim
        for q in range(2 * PAIR):
            spread = jnp.where(same & ((head % per_step) // unit_heads == q), 1.0, 0.0)
            dec = jnp.dot(chosen, spread, precision=HI, preferred_element_type=F32)
            dec_ref[q] = pack_decay(dec)

    conv(x_ref, wx_ref, cx_ref, xo_ref)
    conv(b_ref, wb_ref, cb_ref, bo_ref)
    conv(c_ref, wc_ref, cc_ref, co_ref)


def pack_decay(dec):
    hi, lo = split2(dec)
    return jnp.concatenate([hi.astype(F32), lo.astype(F32)], axis=0).astype(BF16)


def unpack_decay(rows):
    both = rows.astype(F32)
    return both[0:8] + both[8:16]


def local_kernel(
    xc_ref,
    bc_ref,
    xtop_ref,
    btop_ref,
    ctop_ref,
    xrim_ref,
    brim_ref,
    crim_ref,
    xcache_ref,
    bcache_ref,
    ccache_ref,
    wx_ref,
    wb_ref,
    wc_ref,
    cx_ref,
    cb_ref,
    cc_ref,
    tail_ref,
    dec_ref,
    send_ref,
    keep_ref,
    xfix_ref,
    bfix_ref,
    cfix_ref,
    ext,
    *,
    head_dim,
):
    step = pl.program_id(0)
    steps = pl.num_programs(0)
    device = lax.axis_index(SEQ)
    core = device % 2
    rows, width = xc_ref.shape
    unit = width // (2 * PAIR)
    state_rows = steps * STATE

    def fix(top, rim, cache, w, bias, dst):
        cols = top.shape[1]
        ext[8 : 8 + TOP, 0:cols] = top[...].astype(F32)
        before = jnp.where(device == 0, cache[...].astype(F32), rim[...].astype(F32))
        ext[8 - RIM : 8, 0:cols] = before
        fixed = conv_rows(ext, w[...], bias[...], TOP, 8, pl.ds(0, cols)).astype(BF16)
        dst[...] = fixed
        return fixed

    xfix = fix(xtop_ref, xrim_ref, xcache_ref, wx_ref, cx_ref, xfix_ref)
    bfix = fix(btop_ref, brim_ref, bcache_ref, wb_ref, cb_ref, bfix_ref)
    fix(ctop_ref, crim_ref, ccache_ref, wc_ref, cc_ref, cfix_ref)
    b_all = jnp.concatenate([bfix, bc_ref[TOP:, :]], axis=0)
    b_turned = b_all.T
    per_step = tail_ref.shape[2] // 2
    head = lax.broadcasted_iota(jnp.int32, (2 * per_step, width), 0) % per_step
    lane = lax.broadcasted_iota(jnp.int32, (2 * per_step, width), 1)
    spread = jnp.where(head == lane // head_dim, 1.0, 0.0).astype(BF16)
    tail = jnp.dot(tail_ref[0], spread, preferred_element_type=F32)
    x_all = jnp.concatenate([xfix, xc_ref[TOP:, :]], axis=0)
    scaled = (x_all.astype(F32) * tail).astype(BF16)
    where = pl.ds(pl.multiple_of(step * STATE, STATE), STATE)
    for y in range(PAIR):
        lhs = b_turned[y * STATE : (y + 1) * STATE, :]
        both = jnp.dot(
            lhs, scaled[:, 2 * y * unit : 2 * (y + 1) * unit], preferred_element_type=F32
        ).astype(BF16)
        low, high = both[:, :unit], both[:, unit:]
        send_ref[y, where, :] = jnp.where(core == 0, high, low)
        keep_ref[y, where, :] = jnp.where(core == 0, low, high)

    @pl.when(step == 0)
    def _():
        for y in range(PAIR):
            send_ref[y, state_rows:, :] = dec_ref[2 * y + 1 - core]
            keep_ref[y, state_rows:, :] = dec_ref[2 * y + core]


def blocks_of(rows):
    return [(i, slice(i * STATE, (i + 1) * STATE)) for i in range(rows // STATE)]


def core_kernel(keep_ref, recv_ref, send_ref, own_ref):
    device = lax.axis_index(SEQ)
    core, side = device % 2, (device // 2) % 2
    rows = keep_ref.shape[1] - 16
    for out, pick in ((send_ref, 1 - side), (own_ref, side)):
        mine, other = keep_ref.at[pick], recv_ref.at[pick]
        join_totals(mine, other, core == 0, out, rows)


def join_totals(mine, other, mine_first, out, rows):
    d_mine = unpack_decay(mine[rows:, :])
    d_other = unpack_decay(other[rows:, :])
    d_later = jnp.where(mine_first, d_other, d_mine)
    f_mine = jnp.where(mine_first, d_later, 1.0)
    f_other = jnp.where(mine_first, 1.0, d_later)
    for i, part in blocks_of(rows):
        total = mine[part, :].astype(F32) * f_mine[i : i + 1] + other[part, :].astype(F32) * f_other[
            i : i + 1
        ]
        out[part, :] = total.astype(BF16)
    out[rows:, :] = pack_decay(d_mine * d_other)


def total_kernel(mine_ref, other_ref, out_ref, *, bit):
    device = lax.axis_index(SEQ)
    rows = mine_ref.shape[0] - 16
    join_totals(mine_ref, other_ref, (device // bit) % 2 == 0, out_ref, rows)


def prefix_kernel(mine_ref, other_ref, pre_ref, dpre_ref, out_ref, opre_ref, odpre_ref, *, bit):
    device = lax.axis_index(SEQ)
    rows = mine_ref.shape[0] - 16
    first = (device // bit) % 2 == 0
    join_totals(mine_ref, other_ref, first, out_ref, rows)
    d_other = unpack_decay(other_ref[rows:, :])
    d_pre = dpre_ref[...]
    gain = jnp.where(first, 0.0, d_pre)
    for i, part in blocks_of(rows):
        opre_ref[part, :] = pre_ref[part, :] + gain[i : i + 1] * other_ref[part, :].astype(F32)
    odpre_ref[...] = jnp.where(first, d_pre, d_pre * d_other)


def start_kernel(mine_ref, other_ref, out_ref, opre_ref, odpre_ref, *, bit):
    device = lax.axis_index(SEQ)
    rows = mine_ref.shape[0] - 16
    first = (device // bit) % 2 == 0
    join_totals(mine_ref, other_ref, first, out_ref, rows)
    d_other = unpack_decay(other_ref[rows:, :])
    opre_ref[...] = jnp.where(first, 0.0, other_ref[:rows, :].astype(F32))
    odpre_ref[...] = jnp.where(first, 1.0, d_other)


def enter_kernel(
    mine_ref, other_ref, pre_ref, dpre_ref, cache_ref, own_ref, recv_ref, send_ref, stay_ref, fin_ref, *, bit
):
    device = lax.axis_index(SEQ)
    side = (device // 2) % 2
    rows = mine_ref.shape[0] - 16
    first = (device // bit) % 2 == 0
    d_mine = unpack_decay(mine_ref[rows:, :])
    d_other = unpack_decay(other_ref[rows:, :])
    d_later = jnp.where(first, d_other, d_mine)
    f_mine = jnp.where(first, d_later, 1.0)
    f_other = jnp.where(first, 1.0, d_later)
    d_all = d_mine * d_other
    d_pre = dpre_ref[...]
    gain = jnp.where(first, 0.0, d_pre)
    d_before = jnp.where(first, d_pre, d_pre * d_other)
    d_first = jnp.where(side == 0, unpack_decay(own_ref[rows:, :]), unpack_decay(recv_ref[rows:, :]))
    for i, part in blocks_of(rows):
        cache = cache_ref[part, :]
        other = other_ref[part, :].astype(F32)
        mine = mine_ref[part, :].astype(F32)
        row = slice(i, i + 1)
        fin_ref[part, :] = d_all[row] * cache + mine * f_mine[row] + other * f_other[row]
        plane = d_before[row] * cache + pre_ref[part, :] + gain[row] * other
        t_first = jnp.where(side == 0, own_ref[part, :].astype(F32), recv_ref[part, :].astype(F32))
        second = d_first[row] * plane + t_first
        send_ref[part, :] = jnp.where(side == 0, second, plane).astype(BF16)
        stay_ref[part, :] = jnp.where(side == 0, plane, second).astype(BF16)


def chip_kernel(stay_ref, recv_ref, keep_ref, part_ref, send_ref, own_ref):
    device = lax.axis_index(SEQ)
    core, side = device % 2, (device // 2) % 2
    rows = stay_ref.shape[0]
    for y in range(PAIR):
        d_first = jnp.where(
            core == 0, unpack_decay(keep_ref[y, rows:, :]), unpack_decay(part_ref[y, rows:, :])
        )
        for i, part in blocks_of(rows):
            chip = jnp.where(side == y, stay_ref[part, :], recv_ref[part, :])
            local = jnp.where(core == 0, keep_ref[y, part, :], part_ref[y, part, :])
            second = (d_first[i : i + 1] * chip.astype(F32) + local.astype(F32)).astype(BF16)
            send_ref[y, part, :] = jnp.where(core == 0, second, chip)
            own_ref[y, part, :] = jnp.where(core == 0, chip, second)


def diag_kernel(
    xc_ref, xfix_ref, b_ref, bfix_ref, c_ref, cfix_ref, cum_ref, row_ref, skip_ref, out_ref, *, head_dim, first
):
    rows, width = xc_ref.shape
    per_group = width // head_dim // PAIR
    below = lax.broadcasted_iota(jnp.int32, (rows, rows), 0)
    across = lax.broadcasted_iota(jnp.int32, (rows, rows), 1)
    mask = below >= across
    b_all = jnp.concatenate([bfix_ref[...], b_ref[TOP:, :]], axis=0)
    c_all = jnp.concatenate([cfix_ref[...], c_ref[TOP:, :]], axis=0)
    b_turned = b_all.T
    quad = 128 // head_dim
    lane = lax.broadcasted_iota(jnp.int32, (rows, 128), 1) // head_dim
    heads = cum_ref.shape[1]
    base = (first + pl.program_id(0)) * PAIR * per_group
    cum = pltpu.roll(cum_ref[...], heads - base, axis=1)
    for y in range(PAIR):
        part = slice(y * STATE, (y + 1) * STATE)
        c_dot_b = jnp.dot(c_all[:, part], b_turned[part, :], preferred_element_type=F32)
        for q in range(per_group // quad):
            cols = pl.ds((y * per_group + q * quad) * head_dim, 128)
            x_quad = jnp.concatenate([xfix_ref[:, cols], xc_ref[TOP:, cols]], axis=0)
            lhs, rhs = [], []
            for k in range(quad):
                head = y * per_group + q * quad + k
                gap = cum[:, head : head + 1] - row_ref[head : head + 1, :]
                decay = jnp.exp2(jnp.where(mask, gap, -1e30))
                lhs.append((c_dot_b * decay).astype(BF16))
                rhs.append(jnp.where(lane == k, x_quad, jnp.zeros_like(x_quad)))
            inner = jnp.dot(
                jnp.concatenate(lhs, axis=1),
                jnp.concatenate(rhs, axis=0),
                preferred_element_type=F32,
            )
            out_ref[:, cols] = inner + skip_ref[:, cols] * x_quad.astype(F32)


def out_kernel(
    len_ref, diag_ref, c_ref, cfix_ref, ecum_ref, own_ref, recv_ref, z_ref, gain_ref, out_ref, *, head_dim
):
    device = lax.axis_index(SEQ)
    core = device % 2
    rows, width = diag_ref.shape
    unit = width // (2 * PAIR)
    c_all = jnp.concatenate([cfix_ref[...], c_ref[TOP:, :]], axis=0)
    per_step = ecum_ref.shape[2] // 2
    head = lax.broadcasted_iota(jnp.int32, (2 * per_step, width), 0) % per_step
    lane = lax.broadcasted_iota(jnp.int32, (2 * per_step, width), 1)
    spread = jnp.where(head == lane // head_dim, 1.0, 0.0).astype(BF16)
    grow = jnp.dot(ecum_ref[0], spread, preferred_element_type=F32)
    token = device * rows + lax.broadcasted_iota(jnp.int32, (rows, 1), 0)
    live = (token < len_ref[0]).astype(F32)
    for y in range(PAIR):
        own, recv = own_ref[y], recv_ref[y]
        state = jnp.concatenate(
            [jnp.where(core == 0, own, recv), jnp.where(core == 0, recv, own)], axis=1
        )
        cols = slice(2 * y * unit, 2 * (y + 1) * unit)
        entering = jnp.dot(
            c_all[:, y * STATE : (y + 1) * STATE], state, preferred_element_type=F32
        )
        y_all = (diag_ref[:, cols] + grow[:, cols] * entering) * live
        y_all = y_all.astype(BF16).astype(F32)
        gated = y_all * silu(z_ref[:, cols].astype(F32))
        scale = lax.rsqrt(jnp.mean(gated * gated, axis=1, keepdims=True) + 1e-05)
        out_ref[:, cols] = (gated * scale * gain_ref[:, cols]).astype(BF16)


def swap(value, mask):
    devices = range(lax.axis_size(SEQ))
    return lax.ppermute(value, SEQ, [(i, i ^ mask) for i in devices])


def whole(shape):
    return pl.BlockSpec(shape, lambda *_: (0,) * len(shape))


def plain_call(body, out_shape, *args, nbytes=2**20):
    return pl.pallas_call(
        body,
        out_shape=out_shape,
        in_specs=[pl.BlockSpec(memory_space=pltpu.VMEM)] * len(args),
        out_specs=jax.tree.map(lambda _: pl.BlockSpec(memory_space=pltpu.VMEM), out_shape),
        compiler_params=pltpu.CompilerParams(vmem_limit_bytes=12 * 2**20),
        cost_estimate=pl.CostEstimate(flops=0, bytes_accessed=nbytes, transcendentals=0),
    )(*args)


def body(
    x_in,
    bc_in,
    z_in,
    dt_in,
    conv_weight,
    conv_bias,
    dt_bias,
    a_log,
    d_skip,
    norm_gain,
    conv_cache,
    cache_state,
    lengths,
):
    rows, inner = x_in.shape
    heads = dt_in.shape[1]
    head_dim = inner // heads
    devices = lax.axis_size(SEQ)
    index = lax.axis_index(SEQ)
    share = heads // devices
    steps = GROUPS // PAIR
    per_step = heads // steps
    width = inner // steps
    bcw = PAIR * STATE
    b0, c0 = inner // bcw, inner // bcw + steps
    unit = width // (2 * PAIR)
    state_rows = steps * STATE
    msg_rows = state_rows + 16
    sds = jax.ShapeDtypeStruct
    smem = pl.BlockSpec(memory_space=pltpu.SMEM)

    bias2 = conv_bias.reshape(1, -1)
    rim = jnp.concatenate([x_in[rows - RIM :], bc_in[rows - RIM :]], axis=1)
    rim = lax.ppermute(rim, SEQ, [(i, (i + 1) % devices) for i in range(devices)])

    def at(r, c, off):
        return pl.BlockSpec((r, c), lambda i: (0, i + off))

    def lead(shape):
        return pl.BlockSpec((1,) + shape, lambda i: (i,) + (0,) * len(shape))

    weight_specs = [at(CONV_W, width, 0), at(CONV_W, bcw, b0), at(CONV_W, bcw, c0)]
    bias_specs = [at(1, width, 0), at(1, bcw, b0), at(1, bcw, c0)]
    xc, bc, cc, cum, row, tail, ecum, dec = grid_call(
        functools.partial(conv_kernel, heads=heads, head_dim=head_dim),
        (steps,),
        [smem, at(rows, width, 0), at(rows, bcw, 0), at(rows, bcw, steps), whole((rows, heads))]
        + weight_specs
        + bias_specs
        + [whole((1, heads))] * 2,
        [
            at(rows, width, 0),
            at(rows, bcw, 0),
            at(rows, bcw, 0),
            whole((rows, heads)),
            whole((heads, rows)),
            whole((steps, rows, 2 * per_step)),
            whole((steps, rows, 2 * per_step)),
            whole((2 * PAIR, 16, unit)),
        ],
        [
            sds((rows, inner), BF16),
            sds((rows, GROUPS * STATE), BF16),
            sds((rows, GROUPS * STATE), BF16),
            sds((rows, heads), F32),
            sds((heads, rows), F32),
            sds((steps, rows, 2 * per_step), BF16),
            sds((steps, rows, 2 * per_step), BF16),
            sds((2 * PAIR, 16, unit), BF16),
        ],
        scratch=[pltpu.VMEM((8 + rows, 128), F32)],
        nbytes=4 * 2**20,
    )(
        lengths,
        x_in,
        bc_in,
        bc_in,
        dt_in,
        conv_weight,
        conv_weight,
        conv_weight,
        bias2,
        bias2,
        bias2,
        dt_bias.reshape(1, -1),
        a_log.reshape(1, -1),
    )

    send, keep, xfix, bfix, cfix = grid_call(
        functools.partial(local_kernel, head_dim=head_dim),
        (steps,),
        [at(rows, width, 0), at(rows, bcw, 0)]
        + [at(TOP, width, 0), at(TOP, bcw, 0), at(TOP, bcw, steps)]
        + [at(RIM, width, 0), at(RIM, bcw, b0), at(RIM, bcw, c0)] * 2
        + weight_specs
        + bias_specs
        + [lead((rows, 2 * per_step)), whole((2 * PAIR, 16, unit))],
        [
            whole((PAIR, msg_rows, unit)),
            whole((PAIR, msg_rows, unit)),
            at(TOP, width, 0),
            at(TOP, bcw, 0),
            at(TOP, bcw, 0),
        ],
        [
            sds((PAIR, msg_rows, unit), BF16),
            sds((PAIR, msg_rows, unit), BF16),
            sds((TOP, inner), BF16),
            sds((TOP, GROUPS * STATE), BF16),
            sds((TOP, GROUPS * STATE), BF16),
        ],
        scratch=[pltpu.VMEM((8 + TOP, width), F32)],
        nbytes=2 * 2**20,
    )(
        xc,
        bc,
        x_in,
        bc_in,
        bc_in,
        rim,
        rim,
        rim,
        conv_cache,
        conv_cache,
        conv_cache,
        conv_weight,
        conv_weight,
        conv_weight,
        bias2,
        bias2,
        bias2,
        tail,
        dec,
    )

    message = sds((msg_rows, unit), BF16)
    part = swap(send, 1)
    send_y, own = plain_call(core_kernel, (message, message), keep, part)
    recv = swap(send_y, 2)
    total = plain_call(functools.partial(total_kernel, bit=2), message, own, recv)
    pre = None
    bit = 4
    pre_shape = (sds((state_rows, unit), F32), sds((8, unit), F32))
    while 2 * bit < devices:
        other = swap(total, 2 * bit - 4)
        if pre is None:
            total, *pre = plain_call(
                functools.partial(start_kernel, bit=bit), (message,) + pre_shape, total, other
            )
        else:
            total, *pre = plain_call(
                functools.partial(prefix_kernel, bit=bit), (message,) + pre_shape, total, other, *pre
            )
        bit *= 2
    if pre is None:
        pre = [jnp.zeros((state_rows, unit), F32), jnp.ones((8, unit), F32)]
    other = swap(total, 2 * bit - 4)
    quarter = index % (2 * PAIR)
    cache = cache_state.reshape(steps, 2 * PAIR, unit, STATE)
    cache = lax.dynamic_index_in_dim(cache, quarter, 1, keepdims=False)
    cache = cache.transpose(0, 2, 1).reshape(state_rows, unit)
    state_out = sds((state_rows, unit), BF16)
    send_y, stay, final = plain_call(
        functools.partial(enter_kernel, bit=bit),
        (state_out, state_out, sds((state_rows, unit), F32)),
        total,
        other,
        *pre,
        cache,
        own,
        recv,
    )
    recv_y = swap(send_y, 2)
    half = sds((PAIR, state_rows, unit), BF16)
    send_c, enter_own = plain_call(chip_kernel, (half, half), stay, recv_y, keep, part)
    enter_recv = swap(send_c, 1)

    diag = grid_call(
        functools.partial(diag_kernel, head_dim=head_dim, first=0),
        (steps,),
        [
            at(rows, width, 0),
            at(TOP, width, 0),
            at(rows, bcw, 0),
            at(TOP, bcw, 0),
            at(rows, bcw, 0),
            at(TOP, bcw, 0),
            whole((rows, heads)),
            pl.BlockSpec((per_step, rows), lambda i: (i, 0)),
            at(1, width, 0),
        ],
        at(rows, width, 0),
        sds((rows, inner), F32),
        nbytes=8 * 2**20,
    )(xc, xfix, bc, bfix, cc, cfix, cum, row, jnp.repeat(d_skip, head_dim).reshape(1, -1))

    def mid(shape):
        return pl.BlockSpec(shape, lambda i: (0, i, 0))

    mixed = grid_call(
        functools.partial(out_kernel, head_dim=head_dim),
        (steps,),
        [
            smem,
            at(rows, width, 0),
            at(rows, bcw, 0),
            at(TOP, bcw, 0),
            lead((rows, 2 * per_step)),
            mid((PAIR, STATE, unit)),
            mid((PAIR, STATE, unit)),
            at(rows, width, 0),
            at(1, width, 0),
        ],
        at(rows, width, 0),
        sds((rows, inner), BF16),
        nbytes=4 * 2**20,
    )(lengths, diag, cc, cfix, ecum, enter_own, enter_recv, z_in, norm_gain.reshape(1, -1))

    final = final.reshape(steps, STATE, unit)
    if share * head_dim == unit and devices == 2 * PAIR * steps:
        mine = lax.dynamic_index_in_dim(final, index // (2 * PAIR), 0, keepdims=False)
        mine = mine.T.reshape(share, head_dim, STATE)
    else:
        around = [[4 * i + j for j in range(4)] for i in range(devices // 4)]
        every = lax.all_gather(final, SEQ, axis=1, axis_index_groups=around)
        every = every.reshape(steps * 2 * PAIR, STATE, unit).transpose(0, 2, 1)
        every = every.reshape(heads, head_dim, STATE)
        mine = lax.dynamic_slice_in_dim(every, index * share, share, 0)
    return (mixed, mine)


def solution(mesh):
    in_specs = (
        P(("groups", "seq"), None),
        P(("groups", "seq"), None),
        P(("groups", "seq"), None),
        P(("groups", "seq"), None),
        P(),
        P(),
        P(),
        P(),
        P(),
        P(),
        P("groups", None),
        P("groups", None, None),
        P("groups"),
    )
    out_specs = (P(("groups", "seq"), None), P(("groups", "seq"), None, None))
    return jax.shard_map(body, mesh=mesh, in_specs=in_specs, out_specs=out_specs, check_vma=False)
```

```python
import functools

import jax
import jax.numpy as jnp
from jax import lax
from jax.experimental import pallas as pl
from jax.experimental.pallas import tpu as pltpu
from jax.sharding import PartitionSpec as P

STATE = 64
GROUPS = 8
CONV_W = 4
RIM = CONV_W - 1
LOG2E = 1.4426950408889634
BF16 = jnp.bfloat16
F32 = jnp.float32
HI = lax.Precision.HIGHEST
SEQ = "seq"
PAIR = 2
TOP = 16


def silu(v):
    half = 0.5 * v
    return half + half * jnp.tanh(half)


def split2(v):
    hi = v.astype(BF16)
    return hi, (v - hi.astype(F32)).astype(BF16)


def grid_call(body, grid, in_specs, out_specs, out_shape, scratch=(), flops=0, nbytes=0, vmem=24):
    return pl.pallas_call(
        body,
        grid=grid,
        in_specs=in_specs,
        out_specs=out_specs,
        out_shape=out_shape,
        scratch_shapes=list(scratch),
        compiler_params=pltpu.CompilerParams(vmem_limit_bytes=vmem * 2**20),
        cost_estimate=pl.CostEstimate(flops=flops, bytes_accessed=nbytes, transcendentals=0),
    )


def rim_kernel(x_ref, bc_ref, out_ref, x_rows, bc_rows, sems):
    rows, inner = x_ref.shape
    copies = [
        pltpu.make_async_copy(x_ref.at[pl.ds(rows - TOP, TOP), :], x_rows, sems.at[0]),
        pltpu.make_async_copy(bc_ref.at[pl.ds(rows - TOP, TOP), :], bc_rows, sems.at[1]),
    ]
    for copy in copies:
        copy.start()
    for copy in copies:
        copy.wait()
    out_ref[:, :inner] = x_rows[...].astype(F32)[TOP - RIM :, :].astype(BF16)
    out_ref[:, inner:] = bc_rows[...].astype(F32)[TOP - RIM :, :].astype(BF16)


def pack_decay(dec):
    hi, lo = split2(dec)
    return jnp.concatenate([hi.astype(F32), lo.astype(F32)], axis=0).astype(BF16)


def unpack_decay(rows):
    both = rows.astype(F32)
    return both[0:8] + both[8:16]


def conv_kernel(
    len_ref,
    x_ref,
    b_ref,
    c_ref,
    dt_ref,
    wx_ref,
    wb_ref,
    wc_ref,
    cx_ref,
    cb_ref,
    cc_ref,
    dtb_ref,
    alog_ref,
    after_ref,
    xo_ref,
    bo_ref,
    co_ref,
    prex_ref,
    preb_ref,
    prec_ref,
    cum_ref,
    row_ref,
    ecum_ref,
    dec_ref,
    top_ref,
    local_ref,
    ext,
    tails,
    scaled,
    *,
    heads,
    head_dim,
):
    step = pl.program_id(0)
    rows = x_ref.shape[0]
    per_step = heads // pl.num_programs(0)

    def conv(src, w, bias, cols):
        ext[8:, :] = src[:, cols].astype(F32)
        total = jnp.broadcast_to(bias[:, cols], (rows, 128))
        for k in range(CONV_W):
            total = total + ext[pl.ds(8 + k - RIM, rows), :] * w[k : k + 1, cols]
        return total[0:8], silu(total).astype(BF16)

    ext[0:8, :] = jnp.zeros((8, 128), F32)

    @pl.when(step == 0)
    def _():
        raw = dt_ref[...].astype(F32) + dtb_ref[...]
        soft = jnp.maximum(raw, 0.0) + jnp.log1p(jnp.exp(-jnp.abs(raw)))
        first = lax.axis_index(SEQ) * rows
        token = first + lax.broadcasted_iota(jnp.int32, (rows, heads), 0)
        dt = jnp.where(token < len_ref[0], soft, 0.0)
        rate = -jnp.exp(alog_ref[...]) * dt
        below = lax.broadcasted_iota(jnp.int32, (rows, rows), 0)
        across = lax.broadcasted_iota(jnp.int32, (rows, rows), 1)
        tri = (below >= across).astype(F32)
        cum = jnp.dot(tri, rate, precision=HI, preferred_element_type=F32)
        last = cum[rows - 1 : rows, :]
        tail = jnp.exp(last - cum) * dt
        ecum = jnp.exp(cum)
        cum_ref[...] = cum * LOG2E
        log_dt = jnp.where(dt > 0.0, jnp.log(jnp.maximum(dt, 1e-38)) * LOG2E, -1e30)
        row_ref[...] = (cum * LOG2E - log_dt).T
        tail_hi, tail_lo = split2(tail)
        ecum_hi, ecum_lo = split2(ecum)
        for i in range(heads // per_step):
            part = slice(i * per_step, (i + 1) * per_step)
            tails[i] = jnp.concatenate([tail_hi[:, part], tail_lo[:, part]], axis=1)
            ecum_ref[i] = jnp.concatenate([ecum_hi[:, part], ecum_lo[:, part]], axis=1)
        unit_heads = per_step // (2 * PAIR)
        unit_cols = unit_heads * head_dim
        owner = lax.broadcasted_iota(jnp.int32, (8, heads), 0)
        head = lax.broadcasted_iota(jnp.int32, (8, heads), 1)
        chosen = jnp.where(head // per_step == owner, jnp.exp(last), 0.0)
        head = lax.broadcasted_iota(jnp.int32, (heads, unit_cols), 0)
        lane = lax.broadcasted_iota(jnp.int32, (heads, unit_cols), 1)
        same = head % unit_heads == lane // head_dim
        for q in range(2 * PAIR):
            spread = jnp.where(same & ((head % per_step) // unit_heads == q), 1.0, 0.0)
            dec = jnp.dot(chosen, spread, precision=HI, preferred_element_type=F32)
            dec_ref[q] = pack_decay(dec)

    for src, w, bias, dst, pre in (
        (b_ref, wb_ref, cb_ref, bo_ref, preb_ref),
        (c_ref, wc_ref, cc_ref, co_ref, prec_ref),
    ):
        pre[...], dst[...] = conv(src, w, bias, slice(None))
    early = lax.broadcasted_iota(jnp.int32, (8, 128), 0) < RIM
    head = lax.broadcasted_iota(jnp.int32, (2 * per_step, 128), 0) % per_step
    lane = lax.broadcasted_iota(jnp.int32, (2 * per_step, 128), 1) // head_dim
    for j in range(x_ref.shape[1] // 128):
        cols = pl.ds(128 * j, 128)
        prex_ref[:, cols], xj = conv(x_ref, wx_ref, cx_ref, cols)
        xo_ref[:, cols] = xj
        spread = jnp.where(head == lane + j * (128 // head_dim), 1.0, 0.0).astype(BF16)
        tail = jnp.dot(tails[step], spread, preferred_element_type=F32)
        top_ref[:, cols] = jnp.where(early, tail[0:8], 0.0)
        tail = jnp.concatenate([jnp.where(early, 0.0, tail[0:8]), tail[8:]], axis=0)
        scaled[:, cols] = (xj.astype(F32) * tail).astype(BF16)
    b_turned = bo_ref[...].T
    group = x_ref.shape[1] // PAIR
    for y in range(PAIR):
        local_ref[y] = jnp.dot(
            b_turned[y * STATE : (y + 1) * STATE, :],
            scaled[:, y * group : (y + 1) * group],
            preferred_element_type=F32,
        )


def fix_kernel(
    rim_ref,
    cache_ref,
    w_ref,
    prex_ref,
    preb_ref,
    prec_ref,
    xc_ref,
    bc_ref,
    cc_ref,
    top_ref,
    local_ref,
    dec_ref,
    send_ref,
    keep_ref,
    xfix_ref,
    bfix_ref,
    cfix_ref,
    ext,
):
    device = lax.axis_index(SEQ)
    core = device % 2
    inner = xc_ref.shape[1]
    side = bc_ref.shape[1]
    ext[8:, :] = jnp.zeros((8, ext.shape[1]), F32)
    ext[8 - RIM : 8, :] = jnp.where(
        device == 0, cache_ref[...].astype(F32), rim_ref[...].astype(F32)
    )

    def fix(pre, old, dst, first, count):
        cols = pl.ds(first, count)
        total = pre[...]
        for k in range(RIM):
            total = total + ext[pl.ds(8 - RIM + k, 8), cols] * w_ref[k : k + 1, cols]
        fixed = silu(total)
        dst[...] = jnp.concatenate([fixed, old[0:TOP, :].astype(F32)[8:, :]], axis=0).astype(BF16)
        return fixed.astype(BF16).astype(F32)

    x_top = fix(prex_ref, xc_ref, xfix_ref, 0, inner)
    b_top = fix(preb_ref, bc_ref, bfix_ref, inner, side)
    fix(prec_ref, cc_ref, cfix_ref, inner + side, side)
    scaled = x_top * top_ref[...]
    scaled = jnp.concatenate([scaled, jnp.zeros_like(scaled)], axis=0).astype(BF16)
    b_top = jnp.concatenate([b_top, jnp.zeros_like(b_top)], axis=0)
    b_turned = b_top.T.astype(BF16)
    groups, _, width = local_ref.shape
    unit = width // 2
    for g in range(groups):
        extra = jnp.dot(
            b_turned[g * STATE : (g + 1) * STATE, :],
            scaled[:, g * width : (g + 1) * width],
            preferred_element_type=F32,
        )
        whole_state = local_ref[g] + extra
        low, high = whole_state[:, :unit], whole_state[:, unit:]
        where = pl.ds((g // PAIR) * STATE, STATE)
        send_ref[g % PAIR, where, :] = jnp.where(core == 0, high, low).astype(BF16)
        keep_ref[g % PAIR, where, :] = jnp.where(core == 0, low, high).astype(BF16)
    where = pl.ds(groups // PAIR * STATE, 16)
    for y in range(PAIR):
        send_ref[y, where, :] = dec_ref[2 * y + 1 - core]
        keep_ref[y, where, :] = dec_ref[2 * y + core]


def cache_kernel(state_ref, after_ref, out_ref, held, *, unit_heads):
    step = pl.program_id(0)
    channels, size, heads = state_ref.shape
    per_tile = 128 // unit_heads
    quarters = 2 * PAIR
    steps = heads // (quarters * unit_heads)
    quarter = lax.axis_index(SEQ) % quarters
    lane = lax.broadcasted_iota(jnp.int32, (size, 128), 1) // unit_heads
    for k in range(channels):
        channel = step * channels + k
        tile, place = channel // per_tile, channel % per_tile
        value = state_ref[k]
        for i in range(steps):
            start = (i * quarters + quarter) * unit_heads
            moved = pltpu.roll(value, (place * unit_heads - start + heads) % heads, axis=1)
            held[tile, i] = jnp.where(lane == place, moved, held[tile, i])

    @pl.when(step == pl.num_programs(0) - 1)
    def _():
        unit = out_ref.shape[1]
        dim = unit // unit_heads
        source = lax.broadcasted_iota(jnp.int32, (unit, unit), 0)
        target = lax.broadcasted_iota(jnp.int32, (unit, unit), 1)
        chosen = source == (target % dim) * unit_heads + target // dim
        order = jnp.where(chosen, 1.0, 0.0).astype(BF16)
        for i in range(steps):
            value = jnp.concatenate([held[t, i] for t in range(unit // 128)], axis=1)
            hi = value.astype(BF16)
            rest = value - hi.astype(F32)
            mid = rest.astype(BF16)
            low = (rest - mid.astype(F32)).astype(BF16)
            parts = jnp.dot(
                jnp.concatenate([hi, mid, low], axis=0), order, preferred_element_type=F32
            )
            out_ref[i * size : (i + 1) * size, :] = (
                parts[:size] + parts[size : 2 * size] + parts[2 * size :]
            )


def blocks_of(rows):
    return [(i, slice(i * STATE, (i + 1) * STATE)) for i in range(rows // STATE)]


def core_kernel(keep_ref, recv_ref, send_ref, own_ref):
    device = lax.axis_index(SEQ)
    core, side = device % 2, (device // 2) % 2
    rows = keep_ref.shape[1] - 16
    for out, pick in ((send_ref, 1 - side), (own_ref, side)):
        mine, other = keep_ref.at[pick], recv_ref.at[pick]
        join_totals(mine, other, core == 0, out, rows)


def join_totals(mine, other, mine_first, out, rows):
    d_mine = unpack_decay(mine[rows:, :])
    d_other = unpack_decay(other[rows:, :])
    d_later = jnp.where(mine_first, d_other, d_mine)
    f_mine = jnp.where(mine_first, d_later, 1.0)
    f_other = jnp.where(mine_first, 1.0, d_later)
    for i, part in blocks_of(rows):
        total = mine[part, :].astype(F32) * f_mine[i : i + 1] + other[part, :].astype(F32) * f_other[
            i : i + 1
        ]
        out[part, :] = total.astype(BF16)
    out[rows:, :] = pack_decay(d_mine * d_other)


def total_kernel(mine_ref, other_ref, after_ref, out_ref, *, bit):
    device = lax.axis_index(SEQ)
    rows = mine_ref.shape[0] - 16
    join_totals(mine_ref, other_ref, (device // bit) % 2 == 0, out_ref, rows)


def prefix_kernel(mine_ref, other_ref, pre_ref, dpre_ref, out_ref, opre_ref, odpre_ref, *, bit):
    device = lax.axis_index(SEQ)
    rows = mine_ref.shape[0] - 16
    first = (device // bit) % 2 == 0
    join_totals(mine_ref, other_ref, first, out_ref, rows)
    d_other = unpack_decay(other_ref[rows:, :])
    d_pre = dpre_ref[...]
    gain = jnp.where(first, 0.0, d_pre)
    for i, part in blocks_of(rows):
        opre_ref[part, :] = pre_ref[part, :] + gain[i : i + 1] * other_ref[part, :].astype(F32)
    odpre_ref[...] = jnp.where(first, d_pre, d_pre * d_other)


def start_kernel(mine_ref, other_ref, out_ref, opre_ref, odpre_ref, *, bit):
    device = lax.axis_index(SEQ)
    rows = mine_ref.shape[0] - 16
    first = (device // bit) % 2 == 0
    join_totals(mine_ref, other_ref, first, out_ref, rows)
    d_other = unpack_decay(other_ref[rows:, :])
    opre_ref[...] = jnp.where(first, 0.0, other_ref[:rows, :].astype(F32))
    odpre_ref[...] = jnp.where(first, 1.0, d_other)


def enter_kernel(
    mine_ref,
    other_ref,
    pre_ref,
    dpre_ref,
    cache_ref,
    own_ref,
    recv_ref,
    after_ref,
    send_ref,
    stay_ref,
    fin_ref,
    *,
    bit,
):
    device = lax.axis_index(SEQ)
    side = (device // 2) % 2
    rows = mine_ref.shape[0] - 16
    first = (device // bit) % 2 == 0
    d_mine = unpack_decay(mine_ref[rows:, :])
    d_other = unpack_decay(other_ref[rows:, :])
    d_later = jnp.where(first, d_other, d_mine)
    f_mine = jnp.where(first, d_later, 1.0)
    f_other = jnp.where(first, 1.0, d_later)
    d_all = d_mine * d_other
    d_pre = dpre_ref[...]
    gain = jnp.where(first, 0.0, d_pre)
    d_before = jnp.where(first, d_pre, d_pre * d_other)
    d_first = jnp.where(side == 0, unpack_decay(own_ref[rows:, :]), unpack_decay(recv_ref[rows:, :]))
    for i, part in blocks_of(rows):
        cache = cache_ref[part, :]
        other = other_ref[part, :].astype(F32)
        mine = mine_ref[part, :].astype(F32)
        row = slice(i, i + 1)
        fin_ref[part, :] = d_all[row] * cache + mine * f_mine[row] + other * f_other[row]
        plane = d_before[row] * cache + pre_ref[part, :] + gain[row] * other
        t_first = jnp.where(side == 0, own_ref[part, :].astype(F32), recv_ref[part, :].astype(F32))
        second = d_first[row] * plane + t_first
        send_ref[part, :] = jnp.where(side == 0, second, plane).astype(BF16)
        stay_ref[part, :] = jnp.where(side == 0, plane, second).astype(BF16)


def chip_kernel(stay_ref, recv_ref, keep_ref, part_ref, after_ref, send_ref):
    enter_block(stay_ref, recv_ref, keep_ref, part_ref, send_ref, lax.axis_index(SEQ) % 2 == 1)


def block_kernel(stay_ref, recv_ref, keep_ref, part_ref, after_ref, own_ref):
    enter_block(stay_ref, recv_ref, keep_ref, part_ref, own_ref, lax.axis_index(SEQ) % 2 == 0)


def enter_block(stay_ref, recv_ref, keep_ref, part_ref, out_ref, first):
    device = lax.axis_index(SEQ)
    core, side = device % 2, (device // 2) % 2
    rows = stay_ref.shape[0]

    def fill(values):
        for y in range(PAIR):
            for mine, source in ((True, stay_ref), (False, recv_ref)):

                @pl.when((side == y) == mine)
                def _(y=y, source=source):
                    values(y, source)

    @pl.when(first)
    def _():
        def values(y, source):
            out_ref[y] = source[...]

        fill(values)

    for kept, local in ((0, keep_ref), (1, part_ref)):

        @pl.when(jnp.logical_not(first) & (core == kept))
        def _(local=local):
            def values(y, source):
                decay = unpack_decay(local[y, rows:, :])
                for i, part in blocks_of(rows):
                    entered = decay[i : i + 1] * source[part, :].astype(F32)
                    out_ref[y, part, :] = (entered + local[y, part, :].astype(F32)).astype(BF16)

            fill(values)


def diag_kernel(
    xc_ref,
    xfix_ref,
    b_ref,
    bfix_ref,
    c_ref,
    cfix_ref,
    cum_ref,
    row_ref,
    skip_ref,
    after_ref,
    out_ref,
    *,
    head_dim,
):
    rows, width = xc_ref.shape
    per_group = width // head_dim // PAIR
    below = lax.broadcasted_iota(jnp.int32, (rows, rows), 0)
    across = lax.broadcasted_iota(jnp.int32, (rows, rows), 1)
    mask = below >= across
    b_all = jnp.concatenate([bfix_ref[...], b_ref[TOP:, :]], axis=0)
    c_all = jnp.concatenate([cfix_ref[...], c_ref[TOP:, :]], axis=0)
    b_turned = b_all.T
    quad = 128 // head_dim
    lane = lax.broadcasted_iota(jnp.int32, (rows, 128), 1) // head_dim
    heads = cum_ref.shape[1]
    base = pl.program_id(0) * PAIR * per_group
    cum = pltpu.roll(cum_ref[...], heads - base, axis=1)
    for y in range(PAIR):
        part = slice(y * STATE, (y + 1) * STATE)
        c_dot_b = jnp.dot(c_all[:, part], b_turned[part, :], preferred_element_type=F32)
        for q in range(per_group // quad):
            cols = pl.ds((y * per_group + q * quad) * head_dim, 128)
            x_quad = jnp.concatenate([xfix_ref[:, cols], xc_ref[TOP:, cols]], axis=0)
            lhs, rhs = [], []
            for k in range(quad):
                head = y * per_group + q * quad + k
                gap = cum[:, head : head + 1] - row_ref[head : head + 1, :]
                decay = jnp.exp2(jnp.where(mask, gap, -1e30))
                lhs.append((c_dot_b * decay).astype(BF16))
                rhs.append(jnp.where(lane == k, x_quad, jnp.zeros_like(x_quad)))
            inner = jnp.dot(
                jnp.concatenate(lhs, axis=1),
                jnp.concatenate(rhs, axis=0),
                preferred_element_type=F32,
            )
            out_ref[:, cols] = inner + skip_ref[:, cols] * x_quad.astype(F32)


def gate_kernel(len_ref, z_ref, ecum_ref, final_ref, gate_ref, grow_ref, mine_ref, *, head_dim):
    device = lax.axis_index(SEQ)
    rows, width = z_ref.shape
    per_step = ecum_ref.shape[2] // 2
    token = device * rows + lax.broadcasted_iota(jnp.int32, (rows, 128), 0)
    live = token < len_ref[0]
    head = lax.broadcasted_iota(jnp.int32, (2 * per_step, width), 0) % per_step
    lane = lax.broadcasted_iota(jnp.int32, (2 * per_step, width), 1)
    spread = jnp.where(head == lane // head_dim, 1.0, 0.0).astype(BF16)
    grow_ref[...] = jnp.dot(ecum_ref[0], spread, preferred_element_type=F32)
    for j in range(width // 128):
        cols = pl.ds(128 * j, 128)
        gate_ref[:, cols] = jnp.where(live, silu(z_ref[:, cols].astype(F32)), 0.0)

    @pl.when(pl.program_id(0) == 0)
    def _():
        step = (device // (2 * PAIR)) % (final_ref.shape[0] // STATE)
        mine = final_ref[pl.ds(pl.multiple_of(step * STATE, STATE), STATE), :]
        mine_ref[...] = mine.T


def out_kernel(
    diag_ref, gate_ref, grow_ref, c_ref, cfix_ref, own_ref, recv_ref, gain_ref, out_ref, held, sems
):
    core = lax.axis_index(SEQ) % 2
    steps, _, width = held.shape
    unit = width // (2 * PAIR)
    side = PAIR * STATE
    copies = []
    for i in range(steps):
        c_all = jnp.concatenate(
            [cfix_ref[:, i * side : (i + 1) * side], c_ref[TOP:, i * side : (i + 1) * side]], axis=0
        )
        for y in range(PAIR):
            own = own_ref[y, i * STATE : (i + 1) * STATE, :]
            recv = recv_ref[y, i * STATE : (i + 1) * STATE, :]
            state = jnp.concatenate(
                [jnp.where(core == 0, own, recv), jnp.where(core == 0, recv, own)], axis=1
            )
            first = i * width + 2 * y * unit
            cols = slice(first, first + 2 * unit)
            entering = jnp.dot(
                c_all[:, y * STATE : (y + 1) * STATE], state, preferred_element_type=F32
            )
            y_all = (diag_ref[:, cols] + grow_ref[:, cols] * entering).astype(BF16).astype(F32)
            gated = y_all * gate_ref[:, cols]
            scale = lax.rsqrt(jnp.mean(gated * gated, axis=1, keepdims=True) + 1e-05)
            held[i, :, 2 * y * unit : 2 * (y + 1) * unit] = (
                gated * scale * gain_ref[:, cols]
            ).astype(BF16)
        copy = pltpu.make_async_copy(
            held.at[i], out_ref.at[:, pl.ds(i * width, width)], sems.at[i]
        )
        copy.start()
        copies.append(copy)
    for copy in copies:
        copy.wait()


def swap(value, mask):
    devices = range(lax.axis_size(SEQ))
    return lax.ppermute(value, SEQ, [(i, i ^ mask) for i in devices])


def whole(shape):
    return pl.BlockSpec(shape, lambda *_: (0,) * len(shape))


def near(shape, dtype):
    return pltpu.VMEM(shape, dtype)


def far(value):
    return pltpu.with_memory_space_constraint(value, pltpu.HBM)


VMEM_SPEC = pl.BlockSpec(memory_space=pltpu.VMEM)
ANY_SPEC = pl.BlockSpec(memory_space=pl.ANY)


def plain_call(body, out_shape, *args, after=(), nbytes=2**20, scratch=()):
    return pl.pallas_call(
        body,
        out_shape=out_shape,
        in_specs=[VMEM_SPEC] * len(args) + [ANY_SPEC] * len(after),
        out_specs=jax.tree.map(lambda _: VMEM_SPEC, out_shape),
        scratch_shapes=list(scratch),
        compiler_params=pltpu.CompilerParams(vmem_limit_bytes=12 * 2**20),
        cost_estimate=pl.CostEstimate(flops=0, bytes_accessed=nbytes, transcendentals=0),
    )(*args, *after)


def body(
    x_in,
    bc_in,
    z_in,
    dt_in,
    conv_weight,
    conv_bias,
    dt_bias,
    a_log,
    d_skip,
    norm_gain,
    conv_cache,
    cache_state,
    lengths,
):
    rows, inner = x_in.shape
    heads = dt_in.shape[1]
    head_dim = inner // heads
    devices = lax.axis_size(SEQ)
    index = lax.axis_index(SEQ)
    share = heads // devices
    steps = GROUPS // PAIR
    per_step = heads // steps
    width = inner // steps
    side = GROUPS * STATE
    bcw = PAIR * STATE
    b0, c0 = inner // bcw, inner // bcw + steps
    unit = width // (2 * PAIR)
    unit_heads = unit // head_dim
    state_rows = steps * STATE
    msg_rows = state_rows + 16
    smem = pl.BlockSpec(memory_space=pltpu.SMEM)

    def at(r, c, off):
        return pl.BlockSpec((r, c), lambda i: (0, i + off))

    def lead(*shape):
        return pl.BlockSpec(shape, lambda i: (i,) + (0,) * (len(shape) - 1))

    rim = pl.pallas_call(
        rim_kernel,
        out_shape=near((RIM, inner + 2 * side), BF16),
        in_specs=[ANY_SPEC, ANY_SPEC],
        out_specs=VMEM_SPEC,
        scratch_shapes=[
            pltpu.VMEM((TOP, inner), BF16),
            pltpu.VMEM((TOP, 2 * side), BF16),
            pltpu.SemaphoreType.DMA((2,)),
        ],
        compiler_params=pltpu.CompilerParams(vmem_limit_bytes=4 * 2**20),
    )(far(x_in), far(bc_in))
    rim_recv = lax.ppermute(rim, SEQ, [(i, (i + 1) % devices) for i in range(devices)])

    bias2 = far(conv_bias.reshape(1, -1))
    weight = far(conv_weight)
    weight_specs = [at(CONV_W, width, 0), at(CONV_W, bcw, b0), at(CONV_W, bcw, c0)]
    bias_specs = [at(1, width, 0), at(1, bcw, b0), at(1, bcw, c0)]
    xc, bc, cc, prex, preb, prec, cum, row, ecum, dec, top, local = grid_call(
        functools.partial(conv_kernel, heads=heads, head_dim=head_dim),
        (steps,),
        [smem, at(rows, width, 0), at(rows, bcw, 0), at(rows, bcw, steps), whole((rows, heads))]
        + weight_specs
        + bias_specs
        + [whole((1, heads))] * 2
        + [ANY_SPEC],
        [
            at(rows, width, 0),
            at(rows, bcw, 0),
            at(rows, bcw, 0),
            at(8, width, 0),
            at(8, bcw, 0),
            at(8, bcw, 0),
            whole((rows, heads)),
            whole((heads, rows)),
            whole((steps, rows, 2 * per_step)),
            whole((2 * PAIR, 16, unit)),
            at(8, width, 0),
            lead(PAIR, STATE, width // PAIR),
        ],
        [
            near((rows, inner), BF16),
            near((rows, side), BF16),
            near((rows, side), BF16),
            near((8, inner), F32),
            near((8, side), F32),
            near((8, side), F32),
            near((rows, heads), F32),
            near((heads, rows), F32),
            near((steps, rows, 2 * per_step), BF16),
            near((2 * PAIR, 16, unit), BF16),
            near((8, inner), F32),
            near((GROUPS, STATE, width // PAIR), F32),
        ],
        scratch=[
            pltpu.VMEM((8 + rows, 128), F32),
            pltpu.VMEM((steps, rows, 2 * per_step), BF16),
            pltpu.VMEM((rows, width), BF16),
        ],
        nbytes=4 * 2**20,
    )(
        lengths,
        far(x_in),
        far(bc_in),
        far(bc_in),
        far(dt_in),
        weight,
        weight,
        weight,
        bias2,
        bias2,
        bias2,
        far(dt_bias.reshape(1, -1)),
        far(a_log.reshape(1, -1)),
        rim,
    )

    pair_msg = near((PAIR, msg_rows, unit), BF16)
    send, keep, xfix, bfix, cfix = plain_call(
        fix_kernel,
        (pair_msg, pair_msg, near((TOP, inner), BF16), near((TOP, side), BF16), near((TOP, side), BF16)),
        rim_recv,
        conv_cache,
        conv_weight,
        prex,
        preb,
        prec,
        xc,
        bc,
        cc,
        top,
        local,
        dec,
        scratch=[pltpu.VMEM((16, inner + 2 * side), F32)],
    )

    message = near((msg_rows, unit), BF16)
    part = swap(send, 1)
    send_y, own = plain_call(core_kernel, (message, message), keep, part)
    recv = swap(send_y, 2)
    cache_steps = 4
    cache = grid_call(
        functools.partial(cache_kernel, unit_heads=unit_heads),
        (cache_steps,),
        [lead(head_dim // cache_steps, STATE, heads), ANY_SPEC],
        whole((state_rows, unit)),
        near((state_rows, unit), F32),
        scratch=[pltpu.VMEM((unit // 128, steps, STATE, 128), F32)],
        nbytes=2 * 2**20,
    )(far(cache_state.transpose(1, 2, 0)), own)
    total = plain_call(
        functools.partial(total_kernel, bit=2), message, own, recv, after=(cache,)
    )
    pre = None
    bit = 4
    pre_shape = (near((state_rows, unit), F32), near((8, unit), F32))
    while 2 * bit < devices:
        other = swap(total, 2 * bit - 4)
        if pre is None:
            total, *pre = plain_call(
                functools.partial(start_kernel, bit=bit), (message,) + pre_shape, total, other
            )
        else:
            total, *pre = plain_call(
                functools.partial(prefix_kernel, bit=bit), (message,) + pre_shape, total, other, *pre
            )
        bit *= 2
    if pre is None:
        pre = [jnp.zeros((state_rows, unit), F32), jnp.ones((8, unit), F32)]
    other = swap(total, 2 * bit - 4)
    diag = grid_call(
        functools.partial(diag_kernel, head_dim=head_dim),
        (steps,),
        [
            at(rows, width, 0),
            at(TOP, width, 0),
            at(rows, bcw, 0),
            at(TOP, bcw, 0),
            at(rows, bcw, 0),
            at(TOP, bcw, 0),
            whole((rows, heads)),
            pl.BlockSpec((per_step, rows), lambda i: (i, 0)),
            at(1, width, 0),
            ANY_SPEC,
        ],
        at(rows, width, 0),
        near((rows, inner), F32),
        nbytes=8 * 2**20,
    )(xc, xfix, bc, bfix, cc, cfix, cum, row, jnp.repeat(d_skip, head_dim).reshape(1, -1), total)
    state_out = near((state_rows, unit), BF16)
    send_y, stay, final = plain_call(
        functools.partial(enter_kernel, bit=bit),
        (state_out, state_out, near((state_rows, unit), F32)),
        total,
        other,
        *pre,
        cache,
        own,
        recv,
        after=(diag,),
    )
    recv_y = swap(send_y, 2)
    gate, grow, mine = grid_call(
        functools.partial(gate_kernel, head_dim=head_dim),
        (steps,),
        [smem, at(rows, width, 0), lead(1, rows, 2 * per_step), whole((state_rows, unit))],
        [at(rows, width, 0), at(rows, width, 0), whole((unit, STATE))],
        [
            near((rows, inner), F32),
            near((rows, inner), F32),
            jax.ShapeDtypeStruct((unit, STATE), F32),
        ],
        nbytes=5 * 2**20,
    )(lengths, far(z_in), ecum, final)
    half = near((PAIR, state_rows, unit), BF16)
    send_c = plain_call(chip_kernel, half, stay, recv_y, keep, part, after=(gate,))
    enter_recv = swap(send_c, 1)
    enter_own = plain_call(block_kernel, half, stay, recv_y, keep, part, after=(send_c,))

    mixed = pl.pallas_call(
        out_kernel,
        out_shape=jax.ShapeDtypeStruct((rows, inner), BF16),
        in_specs=[VMEM_SPEC] * 8,
        out_specs=ANY_SPEC,
        scratch_shapes=[
            pltpu.VMEM((steps, rows, width), BF16),
            pltpu.SemaphoreType.DMA((steps,)),
        ],
        compiler_params=pltpu.CompilerParams(vmem_limit_bytes=16 * 2**20),
        cost_estimate=pl.CostEstimate(flops=0, bytes_accessed=4 * 2**20, transcendentals=0),
    )(diag, gate, grow, cc, cfix, enter_own, enter_recv, norm_gain.reshape(1, -1))

    if share * head_dim == unit and devices == 2 * PAIR * steps:
        mine = mine.reshape(share, head_dim, STATE)
    else:
        around = [[4 * i + j for j in range(4)] for i in range(devices // 4)]
        every = final.reshape(steps, STATE, unit)
        every = lax.all_gather(every, SEQ, axis=1, axis_index_groups=around)
        every = every.reshape(steps * 2 * PAIR, STATE, unit).transpose(0, 2, 1)
        every = every.reshape(heads, head_dim, STATE)
        mine = lax.dynamic_slice_in_dim(every, index * share, share, 0)
    return (mixed, mine)


def solution(mesh):
    in_specs = (
        P(("groups", "seq"), None),
        P(("groups", "seq"), None),
        P(("groups", "seq"), None),
        P(("groups", "seq"), None),
        P(),
        P(),
        P(),
        P(),
        P(),
        P(),
        P("groups", None),
        P("groups", None, None),
        P("groups"),
    )
    out_specs = (P(("groups", "seq"), None), P(("groups", "seq"), None, None))
    return jax.shard_map(body, mesh=mesh, in_specs=in_specs, out_specs=out_specs, check_vma=False)
```

```python
import functools

import jax
import jax.numpy as jnp
from jax import lax
from jax.experimental import pallas as pl
from jax.experimental.pallas import tpu as pltpu
from jax.sharding import PartitionSpec as P

STATE = 64
GROUPS = 8
CONV_W = 4
RIM = CONV_W - 1
LOG2E = 1.4426950408889634
BF16 = jnp.bfloat16
F32 = jnp.float32
HI = lax.Precision.HIGHEST
SEQ = "seq"
PAIR = 2
TOP = 16


def silu(v):
    half = 0.5 * v
    return half + half * jnp.tanh(half)


def split2(v):
    hi = v.astype(BF16)
    return hi, (v - hi.astype(F32)).astype(BF16)


def rim_kernel(*refs, count):
    x_ref, bc_ref = refs[:2]
    sources, out_ref, refs = refs[2 : 2 + count], refs[2 + count], refs[3 + count :]
    targets, (x_rows, bc_rows, sems) = refs[: count + 1], refs[count + 1 :]
    rows, inner = x_ref.shape
    pairs = [
        (x_ref.at[pl.ds(rows - TOP, TOP), :], x_rows),
        (bc_ref.at[pl.ds(rows - TOP, TOP), :], bc_rows),
        (x_ref.at[:, pl.ds(0, targets[0].shape[1])], targets[0]),
    ] + list(zip(sources, targets[1:]))
    copies = [pltpu.make_async_copy(a, b, sems.at[k]) for k, (a, b) in enumerate(pairs)]
    for copy in copies:
        copy.start()
    for copy in copies[:2]:
        copy.wait()
    out_ref[:, :inner] = x_rows[...].astype(F32)[TOP - RIM :, :].astype(BF16)
    out_ref[:, inner:] = bc_rows[...].astype(F32)[TOP - RIM :, :].astype(BF16)
    for copy in copies[2:]:
        copy.wait()


def pack_decay(dec):
    hi, lo = split2(dec)
    return jnp.concatenate([hi.astype(F32), lo.astype(F32)], axis=0).astype(BF16)


def unpack_decay(rows):
    both = rows.astype(F32)
    return both[0:8] + both[8:16]


def convolve(values, w_ref, bias_ref, first, ext, rows):
    cols = pl.ds(first, 128)
    ext[8:, :] = values.astype(F32)
    total = jnp.broadcast_to(bias_ref[:, cols], (rows, 128))
    for k in range(CONV_W):
        total = total + ext[pl.ds(8 + k - RIM, rows), :] * w_ref[k : k + 1, cols]
    return total


def conv_kernel(
    len_ref,
    x_hbm,
    x0_ref,
    bc_ref,
    w_ref,
    bias_ref,
    dt_ref,
    dtb_ref,
    alog_ref,
    after_ref,
    xo_ref,
    bo_ref,
    prex_ref,
    preb_ref,
    cum_ref,
    step_ref,
    dec_ref,
    top_ref,
    local_ref,
    x_ref,
    ext,
    tails,
    scaled,
    sems,
    *,
    heads,
    head_dim,
):
    more, rows, width = x_ref.shape
    steps = more + 1
    per_step = heads // steps
    side = bo_ref.shape[1]
    inner = steps * width
    copies = [
        pltpu.make_async_copy(
            x_hbm.at[:, pl.ds((i + 1) * width, width)], x_ref.at[i], sems.at[i]
        )
        for i in range(more)
    ]
    for copy in copies:
        copy.start()
    spare = ext.shape[0]
    for k in range(spare):
        ext[k, 0:8, :] = jnp.zeros((8, 128), F32)

    raw = dt_ref[...].astype(F32) + dtb_ref[...]
    soft = jnp.maximum(raw, 0.0) + jnp.log1p(jnp.exp(-jnp.abs(raw)))
    token = lax.axis_index(SEQ) * rows + lax.broadcasted_iota(jnp.int32, (rows, heads), 0)
    dt = jnp.where(token < len_ref[0], soft, 0.0)
    step_ref[...] = dt
    rate = -jnp.exp(alog_ref[...]) * dt
    below = lax.broadcasted_iota(jnp.int32, (rows, rows), 0)
    across = lax.broadcasted_iota(jnp.int32, (rows, rows), 1)
    tri = jnp.where(below >= across, 1.0, 0.0).astype(BF16)
    hi, rest = split2(rate)
    mid, low = split2(rate - hi.astype(F32))
    sums = jnp.dot(tri, jnp.concatenate([hi, mid, low], axis=1), preferred_element_type=F32)
    cum = sums[:, :heads] + (sums[:, heads : 2 * heads] + sums[:, 2 * heads :])
    cum_ref[...] = cum

    for j in range(side // 128):
        cols = pl.ds(128 * j, 128)
        total = convolve(bc_ref[:, cols], w_ref, bias_ref, inner + 128 * j, ext.at[j % spare], rows)
        preb_ref[:, cols] = total[0:8]
        bo_ref[:, cols] = silu(total).astype(BF16)

    last = cum[rows - 1 : rows, :]
    tail_hi, tail_lo = split2(jnp.exp(last - cum) * dt)
    unit_heads = per_step // (2 * PAIR)
    unit_cols = unit_heads * head_dim
    owner = lax.broadcasted_iota(jnp.int32, (8, heads), 0)
    head = lax.broadcasted_iota(jnp.int32, (8, heads), 1)
    dec_hi, dec_lo = split2(jnp.exp(last))
    chosen = jnp.concatenate(
        [jnp.where(head // per_step == owner, v.astype(F32), 0.0) for v in (dec_hi, dec_lo)], axis=0
    ).astype(BF16)
    head = lax.broadcasted_iota(jnp.int32, (heads, unit_cols), 0)
    lane = lax.broadcasted_iota(jnp.int32, (heads, unit_cols), 1)
    same = head % unit_heads == lane // head_dim
    for q in range(2 * PAIR):
        spread = jnp.where(same & ((head % per_step) // unit_heads == q), 1.0, 0.0).astype(BF16)
        dec_ref[q] = jnp.dot(chosen, spread, preferred_element_type=F32).astype(BF16)

    head = lax.broadcasted_iota(jnp.int32, (2 * per_step, width), 0) % per_step
    lane = lax.broadcasted_iota(jnp.int32, (2 * per_step, width), 1) // head_dim
    spread = jnp.where(head == lane, 1.0, 0.0).astype(BF16)

    def widen(i):
        part = slice(i * per_step, (i + 1) * per_step)
        both = jnp.concatenate([tail_hi[:, part], tail_lo[:, part]], axis=1)
        tails[i % 2] = jnp.dot(both, spread, preferred_element_type=F32)

    early = lax.broadcasted_iota(jnp.int32, (8, 128), 0) < RIM
    group = width // PAIR
    widen(0)
    for i in range(steps):
        if i:
            copies[i - 1].wait()
        if i + 1 < steps:
            widen(i + 1)
        for j in range(width // 128):
            cols, lanes = pl.ds(i * width + 128 * j, 128), slice(128 * j, 128 * (j + 1))
            values = x_ref[i - 1, :, lanes] if i else x0_ref[:, lanes]
            total = convolve(
                values, w_ref, bias_ref, i * width + 128 * j, ext.at[j % spare], rows
            )
            prex_ref[:, cols] = total[0:8]
            xj = silu(total).astype(BF16)
            xo_ref[:, cols] = xj
            tail = tails[i % 2, :, lanes]
            top_ref[:, cols] = jnp.where(early, tail[0:8], 0.0)
            tail = jnp.concatenate([jnp.where(early, 0.0, tail[0:8]), tail[8:]], axis=0)
            scaled[i % 2, :, lanes] = (xj.astype(F32) * tail).astype(BF16)
        b_turned = bo_ref[:, i * PAIR * STATE : (i + 1) * PAIR * STATE].T
        for y in range(PAIR):
            local_ref[PAIR * i + y] = jnp.dot(
                b_turned[y * STATE : (y + 1) * STATE, :],
                scaled[i % 2, :, y * group : (y + 1) * group],
                preferred_element_type=F32,
            )


def before_block(near_rim, core_rim, cache):
    device = lax.axis_index(SEQ)
    rim = jnp.where(device % 2 == 1, core_rim.astype(F32), near_rim.astype(F32))
    return jnp.where(device == 0, cache.astype(F32), rim)


def side_kernel(
    bc_ref,
    w_ref,
    bias_ref,
    near_ref,
    core_ref,
    cache_ref,
    cum_ref,
    step_ref,
    after_ref,
    co_ref,
    log_ref,
    row_ref,
    ecum_ref,
    ext,
):
    rows, heads = cum_ref.shape
    side = co_ref.shape[1]
    first = w_ref.shape[1] - side
    spare = ext.shape[0]
    for j in range(side // 128):
        cols = pl.ds(first + 128 * j, 128)
        ext[j % spare, 8 - RIM : 8, :] = before_block(
            near_ref[:, cols], core_ref[:, cols], cache_ref[:, cols]
        )
        values = bc_ref[:, pl.ds(side + 128 * j, 128)]
        total = convolve(values, w_ref, bias_ref, first + 128 * j, ext.at[j % spare], rows)
        co_ref[:, pl.ds(128 * j, 128)] = silu(total).astype(BF16)
    cum, dt = cum_ref[...], step_ref[...]
    log_ref[...] = cum * LOG2E
    log_dt = jnp.where(dt > 0.0, jnp.log(jnp.maximum(dt, 1e-38)) * LOG2E, -1e30)
    row_ref[...] = (cum * LOG2E - log_dt).T
    ecum_hi, ecum_lo = split2(jnp.exp(cum))
    steps, _, twice = ecum_ref.shape
    for i in range(steps):
        part = slice(i * twice // 2, (i + 1) * twice // 2)
        ecum_ref[i] = jnp.concatenate([ecum_hi[:, part], ecum_lo[:, part]], axis=1)


def fix_kernel(
    near_ref,
    core_ref,
    cache_ref,
    w_ref,
    prex_ref,
    preb_ref,
    xc_ref,
    bc_ref,
    top_ref,
    local_ref,
    dec_ref,
    send_ref,
    keep_ref,
    xfix_ref,
    bfix_ref,
    ext,
):
    device = lax.axis_index(SEQ)
    core = device % 2
    inner = xc_ref.shape[1]
    side = bc_ref.shape[1]
    ext[8:, :] = jnp.zeros((8, ext.shape[1]), F32)
    cols = pl.ds(0, ext.shape[1])
    ext[8 - RIM : 8, :] = before_block(near_ref[:, cols], core_ref[:, cols], cache_ref[:, cols])

    def fix(pre, old, dst, first, count):
        cols = pl.ds(first, count)
        total = pre[...]
        for k in range(RIM):
            total = total + ext[pl.ds(8 - RIM + k, 8), cols] * w_ref[k : k + 1, cols]
        fixed = silu(total)
        dst[...] = jnp.concatenate([fixed, old[0:TOP, :].astype(F32)[8:, :]], axis=0).astype(BF16)
        return fixed.astype(BF16).astype(F32)

    x_top = fix(prex_ref, xc_ref, xfix_ref, 0, inner)
    b_top = fix(preb_ref, bc_ref, bfix_ref, inner, side)
    scaled = x_top * top_ref[...]
    scaled = jnp.concatenate([scaled, jnp.zeros_like(scaled)], axis=0).astype(BF16)
    b_top = jnp.concatenate([b_top, jnp.zeros_like(b_top)], axis=0)
    b_turned = b_top.T.astype(BF16)
    groups, _, width = local_ref.shape
    unit = width // 2
    for g in range(groups):
        extra = jnp.dot(
            b_turned[g * STATE : (g + 1) * STATE, :],
            scaled[:, g * width : (g + 1) * width],
            preferred_element_type=F32,
        )
        whole_state = local_ref[g] + extra
        low, high = whole_state[:, :unit], whole_state[:, unit:]
        where = pl.ds((g // PAIR) * STATE, STATE)
        send_ref[g % PAIR, where, :] = jnp.where(core == 0, high, low).astype(BF16)
        keep_ref[g % PAIR, where, :] = jnp.where(core == 0, low, high).astype(BF16)
    where = pl.ds(groups // PAIR * STATE, 16)
    for y in range(PAIR):
        send_ref[y, where, :] = dec_ref[2 * y + 1 - core]
        keep_ref[y, where, :] = dec_ref[2 * y + core]


def cache_kernel(state_hbm, after_ref, out_ref, state_ref, held, sems, *, unit_heads):
    channels, size, heads = state_hbm.shape
    chunks = sems.shape[0]
    count = channels // chunks
    copies = []
    for c in range(chunks):
        part = pl.ds(c * count, count)
        copies.append(pltpu.make_async_copy(state_hbm.at[part], state_ref.at[part], sems.at[c]))
        copies[c].start()
    per_tile = 128 // unit_heads
    quarters = 2 * PAIR
    steps = heads // (quarters * unit_heads)
    quarter = lax.axis_index(SEQ) % quarters
    lane = lax.broadcasted_iota(jnp.int32, (size, 128), 1) // unit_heads
    for channel in range(channels):
        if channel % count == 0:
            copies[channel // count].wait()
        tile, place = channel // per_tile, channel % per_tile
        value = state_ref[channel]
        for i in range(steps):
            start = (i * quarters + quarter) * unit_heads
            moved = pltpu.roll(value, (place * unit_heads - start + heads) % heads, axis=1)
            if place == 0:
                held[tile, i] = moved
            else:
                held[tile, i] = jnp.where(lane == place, moved, held[tile, i])
    unit = out_ref.shape[1]
    dim = unit // unit_heads
    source = lax.broadcasted_iota(jnp.int32, (unit, unit), 0)
    target = lax.broadcasted_iota(jnp.int32, (unit, unit), 1)
    chosen = source == (target % dim) * unit_heads + target // dim
    order = jnp.where(chosen, 1.0, 0.0).astype(BF16)
    for i in range(steps):
        value = jnp.concatenate([held[t, i] for t in range(unit // 128)], axis=1)
        hi = value.astype(BF16)
        rest = value - hi.astype(F32)
        mid = rest.astype(BF16)
        low = (rest - mid.astype(F32)).astype(BF16)
        parts = jnp.dot(
            jnp.concatenate([hi, mid, low], axis=0), order, preferred_element_type=F32
        )
        out_ref[i * size : (i + 1) * size, :] = (
            parts[:size] + parts[size : 2 * size] + parts[2 * size :]
        )


def blocks_of(rows):
    return [(i, slice(i * STATE, (i + 1) * STATE)) for i in range(rows // STATE)]


def core_kernel(keep_ref, recv_ref, send_ref, own_ref):
    device = lax.axis_index(SEQ)
    core, side = device % 2, (device // 2) % 2
    rows = keep_ref.shape[1] - 16
    for out, pick in ((send_ref, 1 - side), (own_ref, side)):
        mine, other = keep_ref.at[pick], recv_ref.at[pick]
        join_totals(mine, other, core == 0, out, rows)


def join_totals(mine, other, mine_first, out, rows):
    d_mine = unpack_decay(mine[rows:, :])
    d_other = unpack_decay(other[rows:, :])
    d_later = jnp.where(mine_first, d_other, d_mine)
    f_mine = jnp.where(mine_first, d_later, 1.0)
    f_other = jnp.where(mine_first, 1.0, d_later)
    for i, part in blocks_of(rows):
        total = mine[part, :].astype(F32) * f_mine[i : i + 1] + other[part, :].astype(F32) * f_other[
            i : i + 1
        ]
        out[part, :] = total.astype(BF16)
    out[rows:, :] = pack_decay(d_mine * d_other)


def total_kernel(mine_ref, other_ref, cache_ref, c_ref, out_ref, *, bit):
    device = lax.axis_index(SEQ)
    rows = mine_ref.shape[0] - 16
    join_totals(mine_ref, other_ref, (device // bit) % 2 == 0, out_ref, rows)


def prefix_kernel(mine_ref, other_ref, pre_ref, dpre_ref, out_ref, opre_ref, odpre_ref, *, bit):
    device = lax.axis_index(SEQ)
    rows = mine_ref.shape[0] - 16
    first = (device // bit) % 2 == 0
    join_totals(mine_ref, other_ref, first, out_ref, rows)
    d_other = unpack_decay(other_ref[rows:, :])
    d_pre = dpre_ref[...]
    gain = jnp.where(first, 0.0, d_pre)
    for i, part in blocks_of(rows):
        opre_ref[part, :] = pre_ref[part, :] + gain[i : i + 1] * other_ref[part, :].astype(F32)
    odpre_ref[...] = jnp.where(first, d_pre, d_pre * d_other)


def start_kernel(mine_ref, other_ref, after_ref, out_ref, opre_ref, odpre_ref, *, bit):
    device = lax.axis_index(SEQ)
    rows = mine_ref.shape[0] - 16
    first = (device // bit) % 2 == 0
    join_totals(mine_ref, other_ref, first, out_ref, rows)
    d_other = unpack_decay(other_ref[rows:, :])
    opre_ref[...] = jnp.where(first, 0.0, other_ref[:rows, :].astype(F32))
    odpre_ref[...] = jnp.where(first, 1.0, d_other)


def enter_kernel(
    mine_ref,
    other_ref,
    pre_ref,
    dpre_ref,
    cache_ref,
    own_ref,
    recv_ref,
    after_ref,
    send_ref,
    stay_ref,
    fin_ref,
    *,
    bit,
):
    device = lax.axis_index(SEQ)
    side = (device // 2) % 2
    rows = mine_ref.shape[0] - 16
    first = (device // bit) % 2 == 0
    d_mine = unpack_decay(mine_ref[rows:, :])
    d_other = unpack_decay(other_ref[rows:, :])
    d_later = jnp.where(first, d_other, d_mine)
    f_mine = jnp.where(first, d_later, 1.0)
    f_other = jnp.where(first, 1.0, d_later)
    d_all = d_mine * d_other
    d_pre = dpre_ref[...]
    gain = jnp.where(first, 0.0, d_pre)
    d_before = jnp.where(first, d_pre, d_pre * d_other)
    d_first = jnp.where(side == 0, unpack_decay(own_ref[rows:, :]), unpack_decay(recv_ref[rows:, :]))
    for i, part in blocks_of(rows):
        cache = cache_ref[part, :]
        other = other_ref[part, :].astype(F32)
        mine = mine_ref[part, :].astype(F32)
        row = slice(i, i + 1)
        fin_ref[part, :] = d_all[row] * cache + mine * f_mine[row] + other * f_other[row]
        plane = d_before[row] * cache + pre_ref[part, :] + gain[row] * other
        t_first = jnp.where(side == 0, own_ref[part, :].astype(F32), recv_ref[part, :].astype(F32))
        second = d_first[row] * plane + t_first
        send_ref[part, :] = jnp.where(side == 0, second, plane).astype(BF16)
        stay_ref[part, :] = jnp.where(side == 0, plane, second).astype(BF16)


def chip_kernel(stay_ref, recv_ref, keep_ref, part_ref, gate_ref, grow_ref, send_ref):
    enter_block(stay_ref, recv_ref, keep_ref, part_ref, send_ref, lax.axis_index(SEQ) % 2 == 1)


def block_kernel(stay_ref, recv_ref, keep_ref, part_ref, after_ref, own_ref):
    enter_block(stay_ref, recv_ref, keep_ref, part_ref, own_ref, lax.axis_index(SEQ) % 2 == 0)


def enter_block(stay_ref, recv_ref, keep_ref, part_ref, out_ref, first):
    device = lax.axis_index(SEQ)
    core, side = device % 2, (device // 2) % 2
    rows = stay_ref.shape[0]

    def fill(values):
        for y in range(PAIR):
            for mine, source in ((True, stay_ref), (False, recv_ref)):

                @pl.when((side == y) == mine)
                def _(y=y, source=source):
                    values(y, source)

    @pl.when(first)
    def _():
        def values(y, source):
            out_ref[y] = source[...]

        fill(values)

    for kept, local in ((0, keep_ref), (1, part_ref)):

        @pl.when(jnp.logical_not(first) & (core == kept))
        def _(local=local):
            def values(y, source):
                decay = unpack_decay(local[y, rows:, :])
                for i, part in blocks_of(rows):
                    entered = decay[i : i + 1] * source[part, :].astype(F32)
                    out_ref[y, part, :] = (entered + local[y, part, :].astype(F32)).astype(BF16)

            fill(values)


def diag_kernel(
    xc_ref,
    xfix_ref,
    b_ref,
    bfix_ref,
    c_ref,
    cum_ref,
    row_ref,
    skip_ref,
    after_ref,
    out_ref,
    *,
    head_dim,
    first,
):
    rows = xc_ref.shape[0]
    heads = cum_ref.shape[1]
    per_group = heads // GROUPS
    below = lax.broadcasted_iota(jnp.int32, (rows, rows), 0)
    across = lax.broadcasted_iota(jnp.int32, (rows, rows), 1)
    mask = below >= across
    quad = 128 // head_dim
    lane = lax.broadcasted_iota(jnp.int32, (rows, 128), 1) // head_dim
    for g in range(out_ref.shape[1] // (per_group * head_dim)):
        part = slice((first + g) * STATE, (first + g + 1) * STATE)
        b_all = jnp.concatenate([bfix_ref[:, part], b_ref[TOP:, part]], axis=0)
        c_dot_b = lax.dot_general(
            c_ref[:, part], b_all, (((1,), (1,)), ((), ())), preferred_element_type=F32
        )
        for q in range(per_group // quad):
            base = (first + g) * per_group + q * quad
            cols = pl.ds(base * head_dim, 128)
            x_quad = jnp.concatenate([xfix_ref[:, cols], xc_ref[TOP:, cols]], axis=0)
            lhs, rhs = [], []
            for k in range(quad):
                head = base + k
                gap = cum_ref[:, head : head + 1] - row_ref[head : head + 1, :]
                decay = jnp.exp2(jnp.where(mask, gap, -1e30))
                lhs.append((c_dot_b * decay).astype(BF16))
                rhs.append(jnp.where(lane == k, x_quad, jnp.zeros_like(x_quad)))
            skip = skip_ref[:, base : base + 1]
            for k in range(1, quad):
                skip = jnp.where(lane[0:1] == k, skip_ref[:, base + k : base + k + 1], skip)
            inner = jnp.dot(
                jnp.concatenate(lhs, axis=1),
                jnp.concatenate(rhs, axis=0),
                preferred_element_type=F32,
            )
            out = pl.ds((g * per_group + q * quad) * head_dim, 128)
            out_ref[:, out] = inner + skip * x_quad.astype(F32)


def gate_kernel(len_ref, z_ref, after_ref, gate_ref):
    rows, width = z_ref.shape
    first = lax.axis_index(SEQ) * rows
    live = first + lax.broadcasted_iota(jnp.int32, (rows, 128), 0) < len_ref[0]
    for j in range(width // 128):
        cols = pl.ds(128 * j, 128)
        gate_ref[:, cols] = jnp.where(live, silu(z_ref[:, cols].astype(F32)), 0.0)


def grow_kernel(ecum_ref, final_ref, grow_ref, mine_ref, *, head_dim):
    steps = ecum_ref.shape[0]
    per_step = ecum_ref.shape[2] // 2
    width = per_step * head_dim
    head = lax.broadcasted_iota(jnp.int32, (2 * per_step, width), 0) % per_step
    lane = lax.broadcasted_iota(jnp.int32, (2 * per_step, width), 1)
    spread = jnp.where(head == lane // head_dim, 1.0, 0.0).astype(BF16)
    for i in range(steps):
        grow_ref[:, i * width : (i + 1) * width] = jnp.dot(
            ecum_ref[i], spread, preferred_element_type=F32
        )
    step = (lax.axis_index(SEQ) // (2 * PAIR)) % (final_ref.shape[0] // STATE)
    mine = final_ref[pl.ds(pl.multiple_of(step * STATE, STATE), STATE), :]
    mine_ref[...] = mine.T


def out_kernel(
    *refs,
    parts,
):
    diag_refs, refs = refs[:parts], refs[parts:]
    gate_ref, grow_ref, c_ref, own_ref, recv_ref, gain_ref, out_ref, held, sems = refs
    core = lax.axis_index(SEQ) % 2
    steps, _, width = held.shape
    unit = width // (2 * PAIR)
    side = PAIR * STATE
    copies = []
    for i in range(steps):
        c_all = c_ref[:, i * side : (i + 1) * side]
        for y in range(PAIR):
            own = own_ref[y, i * STATE : (i + 1) * STATE, :]
            recv = recv_ref[y, i * STATE : (i + 1) * STATE, :]
            state = jnp.concatenate(
                [jnp.where(core == 0, own, recv), jnp.where(core == 0, recv, own)], axis=1
            )
            first = i * width + 2 * y * unit
            cols = slice(first, first + 2 * unit)
            entering = jnp.dot(
                c_all[:, y * STATE : (y + 1) * STATE], state, preferred_element_type=F32
            )
            held_cols = diag_refs[0].shape[1]
            diag = diag_refs[first // held_cols]
            first = first % held_cols
            y_all = diag[:, first : first + 2 * unit] + grow_ref[:, cols] * entering
            gated = y_all.astype(BF16).astype(F32) * gate_ref[:, cols]
            scale = lax.rsqrt(jnp.mean(gated * gated, axis=1, keepdims=True) + 1e-05)
            held[i, :, 2 * y * unit : 2 * (y + 1) * unit] = (
                gated * scale * gain_ref[:, cols]
            ).astype(BF16)
        copy = pltpu.make_async_copy(
            held.at[i], out_ref.at[:, pl.ds(i * width, width)], sems.at[i]
        )
        copy.start()
        copies.append(copy)
    for copy in copies:
        copy.wait()


def swap(value, mask):
    devices = range(lax.axis_size(SEQ))
    return lax.ppermute(value, SEQ, [(i, i ^ mask) for i in devices])


def chip_route(count):
    route = {i: i + 1 for i in range(1, count - 1, 2)}
    route.update({i: i - 1 for i in range(4, count - 2, 2)})
    route.update({2: 0, 0: 1, count - 2: count - 1, count - 1: count - 3})
    return sorted(route.items())


def near(shape, dtype):
    return pltpu.VMEM(shape, dtype)


VMEM_SPEC = pl.BlockSpec(memory_space=pltpu.VMEM)
ANY_SPEC = pl.BlockSpec(memory_space=pl.ANY)


def plain_call(
    body, out_shape, *args, smem=(), far=(), after=(), mib=12, nbytes=2**20, scratch=(), out_specs=None
):
    return pl.pallas_call(
        body,
        out_shape=out_shape,
        in_specs=[pl.BlockSpec(memory_space=pltpu.SMEM)] * len(smem)
        + [ANY_SPEC] * len(far)
        + [VMEM_SPEC] * len(args) + [ANY_SPEC] * len(after),
        out_specs=out_specs or jax.tree.map(lambda _: VMEM_SPEC, out_shape),
        scratch_shapes=list(scratch),
        compiler_params=pltpu.CompilerParams(vmem_limit_bytes=mib * 2**20),
        cost_estimate=pl.CostEstimate(flops=0, bytes_accessed=nbytes, transcendentals=0),
    )(*smem, *[pltpu.with_memory_space_constraint(a, pltpu.HBM) for a in far], *args, *after)


def body(
    x_in,
    bc_in,
    z_in,
    dt_in,
    conv_weight,
    conv_bias,
    dt_bias,
    a_log,
    d_skip,
    norm_gain,
    conv_cache,
    cache_state,
    lengths,
):
    rows, inner = x_in.shape
    heads = dt_in.shape[1]
    head_dim = inner // heads
    devices = lax.axis_size(SEQ)
    index = lax.axis_index(SEQ)
    share = heads // devices
    steps = GROUPS // PAIR
    per_step = heads // steps
    width = inner // steps
    side = GROUPS * STATE
    unit = width // (2 * PAIR)
    unit_heads = unit // head_dim
    state_rows = steps * STATE
    msg_rows = state_rows + 16
    dma = pltpu.SemaphoreType.DMA

    fetched = [
        bc_in,
        conv_weight,
        conv_bias.reshape(1, -1),
        dt_in,
        dt_bias.reshape(1, -1),
        a_log.reshape(1, -1),
    ]
    rim, *ready = plain_call(
        functools.partial(rim_kernel, count=len(fetched)),
        [near((RIM, inner + 2 * side), BF16), near((rows, width), BF16)]
        + [near(a.shape, a.dtype) for a in fetched],
        far=(x_in, bc_in, *fetched),
        mib=4,
        scratch=[
            pltpu.VMEM((TOP, inner), BF16),
            pltpu.VMEM((TOP, 2 * side), BF16),
            dma((3 + len(fetched),)),
        ],
    )
    near_rim = lax.ppermute(rim, SEQ, chip_route(devices))
    core_rim = swap(rim, 1)

    xc, bc, prex, preb, cum, step_size, dec, top, local = plain_call(
        functools.partial(conv_kernel, heads=heads, head_dim=head_dim),
        (
            near((rows, inner), BF16),
            near((rows, side), BF16),
            near((8, inner), F32),
            near((8, side), F32),
            near((rows, heads), F32),
            near((rows, heads), F32),
            near((2 * PAIR, 16, unit), BF16),
            near((8, inner), F32),
            near((GROUPS, STATE, width // PAIR), F32),
        ),
        *ready,
        smem=(lengths,),
        far=(x_in,),
        after=(rim,),
        scratch=[
            pltpu.VMEM((steps - 1, rows, width), BF16),
            pltpu.VMEM((4, 8 + rows, 128), F32),
            pltpu.VMEM((2, rows, width), F32),
            pltpu.VMEM((2, rows, width), BF16),
            dma((steps - 1,)),
        ],
        mib=16,
        nbytes=4 * 2**20,
    )

    pair_msg = near((PAIR, msg_rows, unit), BF16)
    send, keep, xfix, bfix = plain_call(
        fix_kernel,
        (pair_msg, pair_msg, near((TOP, inner), BF16), near((TOP, side), BF16)),
        near_rim,
        core_rim,
        conv_cache,
        ready[2],
        prex,
        preb,
        xc,
        bc,
        top,
        local,
        dec,
        scratch=[pltpu.VMEM((16, inner + side), F32)],
    )

    message = near((msg_rows, unit), BF16)
    part = swap(send, 1)
    send_y, own = plain_call(core_kernel, (message, message), keep, part)
    recv = swap(send_y, 2)
    chunks = 4
    cache = plain_call(
        functools.partial(cache_kernel, unit_heads=unit_heads),
        near((state_rows, unit), F32),
        far=(cache_state.transpose(1, 2, 0),),
        after=(own,),
        scratch=[
            pltpu.VMEM((head_dim, STATE, heads), F32),
            pltpu.VMEM((unit // 128, steps, STATE, 128), F32),
            dma((chunks,)),
        ],
        nbytes=2 * 2**20,
    )
    cc, log_cum, row, ecum = plain_call(
        side_kernel,
        (
            near((rows, side), BF16),
            near((rows, heads), F32),
            near((heads, rows), F32),
            near((steps, rows, 2 * per_step), BF16),
        ),
        ready[1],
        ready[2],
        ready[3],
        near_rim,
        core_rim,
        conv_cache,
        cum,
        step_size,
        after=(own,),
        scratch=[pltpu.VMEM((4, 8 + rows, 128), F32)],
    )
    total = plain_call(
        functools.partial(total_kernel, bit=2), message, own, recv, after=(cache, cc)
    )

    def diag_part(k, order):
        return plain_call(
            functools.partial(diag_kernel, head_dim=head_dim, first=k * GROUPS // 2),
            near((rows, inner // 2), F32),
            xc,
            xfix,
            bc,
            bfix,
            cc,
            log_cum,
            row,
            d_skip.reshape(1, -1),
            after=(order,),
            nbytes=4 * 2**20,
        )

    diags = [diag_part(0, total)]
    pre = None
    bit = 4
    pre_shape = (near((state_rows, unit), F32), near((8, unit), F32))
    while 2 * bit < devices:
        other = swap(total, 2 * bit - 4)
        if pre is None:
            total, *pre = plain_call(
                functools.partial(start_kernel, bit=bit),
                (message,) + pre_shape,
                total,
                other,
                after=(diags[0],),
            )
        else:
            total, *pre = plain_call(
                functools.partial(prefix_kernel, bit=bit), (message,) + pre_shape, total, other, *pre
            )
        bit *= 2
    if pre is None:
        pre = [jnp.zeros((state_rows, unit), F32), jnp.ones((8, unit), F32)]
    last = total
    other = swap(last, 2 * bit - 4)
    diags.append(diag_part(1, last))
    state_out = near((state_rows, unit), BF16)
    send_y, stay, final = plain_call(
        functools.partial(enter_kernel, bit=bit),
        (state_out, state_out, near((state_rows, unit), F32)),
        total,
        other,
        *pre,
        cache,
        own,
        recv,
        after=(diags[1],),
    )
    recv_y = swap(send_y, 2)
    grow, mine = plain_call(
        functools.partial(grow_kernel, head_dim=head_dim),
        (near((rows, inner), F32), jax.ShapeDtypeStruct((unit, STATE), F32)),
        ecum,
        final,
        nbytes=5 * 2**20,
    )
    gate = plain_call(
        gate_kernel, near((rows, inner), F32), z_in, smem=(lengths,), after=(final,)
    )
    half = near((PAIR, state_rows, unit), BF16)
    send_c = plain_call(chip_kernel, half, stay, recv_y, keep, part, after=(gate, grow))
    enter_recv = swap(send_c, 1)
    enter_own = plain_call(block_kernel, half, stay, recv_y, keep, part, after=(send_c,))

    mixed = plain_call(
        functools.partial(out_kernel, parts=len(diags)),
        jax.ShapeDtypeStruct((rows, inner), BF16),
        *diags,
        gate,
        grow,
        cc,
        enter_own,
        enter_recv,
        norm_gain.reshape(1, -1),
        out_specs=ANY_SPEC,
        scratch=[pltpu.VMEM((steps, rows, width), BF16), dma((steps,))],
        mib=16,
        nbytes=4 * 2**20,
    )

    if share * head_dim == unit and devices == 2 * PAIR * steps:
        mine = mine.reshape(share, head_dim, STATE)
    else:
        around = [[4 * i + j for j in range(4)] for i in range(devices // 4)]
        every = final.reshape(steps, STATE, unit)
        every = lax.all_gather(every, SEQ, axis=1, axis_index_groups=around)
        every = every.reshape(steps * 2 * PAIR, STATE, unit).transpose(0, 2, 1)
        every = every.reshape(heads, head_dim, STATE)
        mine = lax.dynamic_slice_in_dim(every, index * share, share, 0)
    return (mixed, mine)


def solution(mesh):
    in_specs = (
        P(("groups", "seq"), None),
        P(("groups", "seq"), None),
        P(("groups", "seq"), None),
        P(("groups", "seq"), None),
        P(),
        P(),
        P(),
        P(),
        P(),
        P(),
        P("groups", None),
        P("groups", None, None),
        P("groups"),
    )
    out_specs = (P(("groups", "seq"), None), P(("groups", "seq"), None, None))
    return jax.shard_map(body, mesh=mesh, in_specs=in_specs, out_specs=out_specs, check_vma=False)
```

```python
import functools

import jax
import jax.numpy as jnp
from jax import lax
from jax.experimental import pallas as pl
from jax.experimental.pallas import tpu as pltpu
from jax.sharding import PartitionSpec as P

STATE = 64
GROUPS = 8
CONV_W = 4
RIM = CONV_W - 1
LOG2E = 1.4426950408889634
BF16 = jnp.bfloat16
F32 = jnp.float32
HI = lax.Precision.HIGHEST
SEQ = "seq"
PAIR = 2
TOP = 16


def silu(v):
    half = 0.5 * v
    return half + half * jnp.tanh(half)


def split2(v):
    hi = v.astype(BF16)
    return hi, (v - hi.astype(F32)).astype(BF16)


def rim_kernel(*refs, count):
    x_ref, bc_ref = refs[:2]
    sources, out_ref, refs = refs[:count], refs[count], refs[count + 1 :]
    targets, (x_rows, bc_rows, sems) = refs[:count], refs[count:]
    rows, inner = x_ref.shape
    pairs = [
        (x_ref.at[pl.ds(rows - TOP, TOP), :], x_rows),
        (bc_ref.at[pl.ds(rows - TOP, TOP), :], bc_rows),
    ] + list(zip(sources, targets))
    copies = [pltpu.make_async_copy(a, b, sems.at[k]) for k, (a, b) in enumerate(pairs)]
    for copy in copies:
        copy.start()
    for copy in copies[:2]:
        copy.wait()
    out_ref[:, :inner] = x_rows[...].astype(F32)[TOP - RIM :, :].astype(BF16)
    out_ref[:, inner:] = bc_rows[...].astype(F32)[TOP - RIM :, :].astype(BF16)
    for copy in copies[2:]:
        copy.wait()


def pack_decay(dec):
    hi, lo = split2(dec)
    return jnp.concatenate([hi.astype(F32), lo.astype(F32)], axis=0).astype(BF16)


def unpack_decay(rows):
    both = rows.astype(F32)
    return both[0:8] + both[8:16]


def convolve(values, w_ref, bias_ref, first, ext, rows):
    cols = pl.ds(first, 128)
    ext[8:, :] = values.astype(F32)
    total = jnp.broadcast_to(bias_ref[:, cols], (rows, 128))
    for k in range(CONV_W):
        total = total + ext[pl.ds(8 + k - RIM, rows), :] * w_ref[k : k + 1, cols]
    return total


def conv_kernel(
    len_ref,
    x_ref,
    bc_ref,
    w_ref,
    bias_ref,
    dt_ref,
    dtb_ref,
    alog_ref,
    after_ref,
    xo_ref,
    bo_ref,
    prex_ref,
    preb_ref,
    cum_ref,
    step_ref,
    dec_ref,
    top_ref,
    local_ref,
    ext,
    tails,
    scaled,
    *,
    heads,
    head_dim,
):
    _, rows, width = tails.shape
    side = bo_ref.shape[1]
    inner = x_ref.shape[1]
    steps = inner // width
    per_step = heads // steps
    spare = ext.shape[0]
    for k in range(spare):
        ext[k, 0:8, :] = jnp.zeros((8, 128), F32)

    raw = dt_ref[...].astype(F32) + dtb_ref[...]
    soft = jnp.maximum(raw, 0.0) + jnp.log1p(jnp.exp(-jnp.abs(raw)))
    token = lax.axis_index(SEQ) * rows + lax.broadcasted_iota(jnp.int32, (rows, heads), 0)
    dt = jnp.where(token < len_ref[0], soft, 0.0)
    step_ref[...] = dt
    rate = -jnp.exp(alog_ref[...]) * dt
    below = lax.broadcasted_iota(jnp.int32, (rows, rows), 0)
    across = lax.broadcasted_iota(jnp.int32, (rows, rows), 1)
    tri = jnp.where(below >= across, 1.0, 0.0).astype(BF16)
    hi, rest = split2(rate)
    mid, low = split2(rate - hi.astype(F32))
    sums = jnp.dot(tri, jnp.concatenate([hi, mid, low], axis=1), preferred_element_type=F32)
    cum = sums[:, :heads] + (sums[:, heads : 2 * heads] + sums[:, 2 * heads :])
    cum_ref[...] = cum

    for j in range(side // 128):
        cols = pl.ds(128 * j, 128)
        total = convolve(bc_ref[:, cols], w_ref, bias_ref, inner + 128 * j, ext.at[j % spare], rows)
        preb_ref[:, cols] = total[0:8]
        bo_ref[:, cols] = silu(total).astype(BF16)

    last = cum[rows - 1 : rows, :]
    tail_hi, tail_lo = split2(jnp.exp(last - cum) * dt)
    unit_heads = per_step // (2 * PAIR)
    unit_cols = unit_heads * head_dim
    owner = lax.broadcasted_iota(jnp.int32, (8, heads), 0)
    head = lax.broadcasted_iota(jnp.int32, (8, heads), 1)
    dec_hi, dec_lo = split2(jnp.exp(last))
    chosen = jnp.concatenate(
        [jnp.where(head // per_step == owner, v.astype(F32), 0.0) for v in (dec_hi, dec_lo)], axis=0
    ).astype(BF16)
    head = lax.broadcasted_iota(jnp.int32, (heads, unit_cols), 0)
    lane = lax.broadcasted_iota(jnp.int32, (heads, unit_cols), 1)
    same = head % unit_heads == lane // head_dim
    for q in range(2 * PAIR):
        spread = jnp.where(same & ((head % per_step) // unit_heads == q), 1.0, 0.0).astype(BF16)
        dec_ref[q] = jnp.dot(chosen, spread, preferred_element_type=F32).astype(BF16)

    head = lax.broadcasted_iota(jnp.int32, (2 * per_step, width), 0) % per_step
    lane = lax.broadcasted_iota(jnp.int32, (2 * per_step, width), 1) // head_dim
    spread = jnp.where(head == lane, 1.0, 0.0).astype(BF16)

    def widen(i):
        part = slice(i * per_step, (i + 1) * per_step)
        both = jnp.concatenate([tail_hi[:, part], tail_lo[:, part]], axis=1)
        tails[i % 2] = jnp.dot(both, spread, preferred_element_type=F32)

    early = lax.broadcasted_iota(jnp.int32, (8, 128), 0) < RIM
    group = width // PAIR
    widen(0)
    for i in range(steps):
        if i + 1 < steps:
            widen(i + 1)
        for j in range(width // 128):
            cols, lanes = pl.ds(i * width + 128 * j, 128), slice(128 * j, 128 * (j + 1))
            total = convolve(
                x_ref[:, cols], w_ref, bias_ref, i * width + 128 * j, ext.at[j % spare], rows
            )
            prex_ref[:, cols] = total[0:8]
            xj = silu(total).astype(BF16)
            xo_ref[:, cols] = xj
            tail = tails[i % 2, :, lanes]
            top_ref[:, cols] = jnp.where(early, tail[0:8], 0.0)
            tail = jnp.concatenate([jnp.where(early, 0.0, tail[0:8]), tail[8:]], axis=0)
            scaled[i % 2, :, lanes] = (xj.astype(F32) * tail).astype(BF16)
        b_turned = bo_ref[:, i * PAIR * STATE : (i + 1) * PAIR * STATE].T
        for y in range(PAIR):
            local_ref[PAIR * i + y] = jnp.dot(
                b_turned[y * STATE : (y + 1) * STATE, :],
                scaled[i % 2, :, y * group : (y + 1) * group],
                preferred_element_type=F32,
            )


def before_block(near_rim, core_rim, cache):
    device = lax.axis_index(SEQ)
    rim = jnp.where(device % 2 == 1, core_rim.astype(F32), near_rim.astype(F32))
    return jnp.where(device == 0, cache.astype(F32), rim)


def side_kernel(
    bc_ref,
    w_ref,
    bias_ref,
    near_ref,
    core_ref,
    cache_ref,
    cum_ref,
    step_ref,
    after_ref,
    co_ref,
    log_ref,
    row_ref,
    ecum_ref,
    ext,
):
    rows, heads = cum_ref.shape
    side = co_ref.shape[1]
    first = w_ref.shape[1] - side
    spare = ext.shape[0]
    for j in range(side // 128):
        cols = pl.ds(first + 128 * j, 128)
        ext[j % spare, 8 - RIM : 8, :] = before_block(
            near_ref[:, cols], core_ref[:, cols], cache_ref[:, cols]
        )
        values = bc_ref[:, pl.ds(side + 128 * j, 128)]
        total = convolve(values, w_ref, bias_ref, first + 128 * j, ext.at[j % spare], rows)
        co_ref[:, pl.ds(128 * j, 128)] = silu(total).astype(BF16)
    cum, dt = cum_ref[...], step_ref[...]
    log_ref[...] = cum * LOG2E
    log_dt = jnp.where(dt > 0.0, jnp.log(jnp.maximum(dt, 1e-38)) * LOG2E, -1e30)
    row_ref[...] = (cum * LOG2E - log_dt).T
    ecum_hi, ecum_lo = split2(jnp.exp(cum))
    steps, _, twice = ecum_ref.shape
    for i in range(steps):
        part = slice(i * twice // 2, (i + 1) * twice // 2)
        ecum_ref[i] = jnp.concatenate([ecum_hi[:, part], ecum_lo[:, part]], axis=1)


def fix_kernel(
    near_ref,
    core_ref,
    cache_ref,
    w_ref,
    prex_ref,
    preb_ref,
    xc_ref,
    bc_ref,
    top_ref,
    local_ref,
    dec_ref,
    send_ref,
    keep_ref,
    xfix_ref,
    bfix_ref,
    ext,
):
    device = lax.axis_index(SEQ)
    core = device % 2
    inner = xc_ref.shape[1]
    side = bc_ref.shape[1]
    ext[8:, :] = jnp.zeros((8, ext.shape[1]), F32)
    cols = pl.ds(0, ext.shape[1])
    ext[8 - RIM : 8, :] = before_block(near_ref[:, cols], core_ref[:, cols], cache_ref[:, cols])

    def fix(pre, old, dst, first, count):
        cols = pl.ds(first, count)
        total = pre[...]
        for k in range(RIM):
            total = total + ext[pl.ds(8 - RIM + k, 8), cols] * w_ref[k : k + 1, cols]
        fixed = silu(total)
        dst[...] = jnp.concatenate([fixed, old[0:TOP, :].astype(F32)[8:, :]], axis=0).astype(BF16)
        return fixed.astype(BF16).astype(F32)

    x_top = fix(prex_ref, xc_ref, xfix_ref, 0, inner)
    b_top = fix(preb_ref, bc_ref, bfix_ref, inner, side)
    scaled = x_top * top_ref[...]
    scaled = jnp.concatenate([scaled, jnp.zeros_like(scaled)], axis=0).astype(BF16)
    b_top = jnp.concatenate([b_top, jnp.zeros_like(b_top)], axis=0)
    b_turned = b_top.T.astype(BF16)
    groups, _, width = local_ref.shape
    unit = width // 2
    for g in range(groups):
        extra = jnp.dot(
            b_turned[g * STATE : (g + 1) * STATE, :],
            scaled[:, g * width : (g + 1) * width],
            preferred_element_type=F32,
        )
        whole_state = local_ref[g] + extra
        low, high = whole_state[:, :unit], whole_state[:, unit:]
        where = pl.ds((g // PAIR) * STATE, STATE)
        send_ref[g % PAIR, where, :] = jnp.where(core == 0, high, low).astype(BF16)
        keep_ref[g % PAIR, where, :] = jnp.where(core == 0, low, high).astype(BF16)
    where = pl.ds(groups // PAIR * STATE, 16)
    for y in range(PAIR):
        send_ref[y, where, :] = dec_ref[2 * y + 1 - core]
        keep_ref[y, where, :] = dec_ref[2 * y + core]


def cache_kernel(state_hbm, after_ref, out_ref, state_ref, held, sems, *, unit_heads):
    channels, size, heads = state_hbm.shape
    chunks = sems.shape[0]
    count = channels // chunks
    copies = []
    for c in range(chunks):
        part = pl.ds(c * count, count)
        copies.append(pltpu.make_async_copy(state_hbm.at[part], state_ref.at[part], sems.at[c]))
        copies[c].start()
    per_tile = 128 // unit_heads
    quarters = 2 * PAIR
    steps = heads // (quarters * unit_heads)
    quarter = lax.axis_index(SEQ) % quarters
    lane = lax.broadcasted_iota(jnp.int32, (size, 128), 1) // unit_heads
    for channel in range(channels):
        if channel % count == 0:
            copies[channel // count].wait()
        tile, place = channel // per_tile, channel % per_tile
        value = state_ref[channel]
        for i in range(steps):
            start = (i * quarters + quarter) * unit_heads
            moved = pltpu.roll(value, (place * unit_heads - start + heads) % heads, axis=1)
            if place == 0:
                held[tile, i] = moved
            else:
                held[tile, i] = jnp.where(lane == place, moved, held[tile, i])
    unit = out_ref.shape[1]
    dim = unit // unit_heads
    source = lax.broadcasted_iota(jnp.int32, (unit, unit), 0)
    target = lax.broadcasted_iota(jnp.int32, (unit, unit), 1)
    chosen = source == (target % dim) * unit_heads + target // dim
    order = jnp.where(chosen, 1.0, 0.0).astype(BF16)
    for i in range(steps):
        value = jnp.concatenate([held[t, i] for t in range(unit // 128)], axis=1)
        hi = value.astype(BF16)
        rest = value - hi.astype(F32)
        mid = rest.astype(BF16)
        low = (rest - mid.astype(F32)).astype(BF16)
        parts = jnp.dot(
            jnp.concatenate([hi, mid, low], axis=0), order, preferred_element_type=F32
        )
        out_ref[i * size : (i + 1) * size, :] = (
            parts[:size] + parts[size : 2 * size] + parts[2 * size :]
        )


def blocks_of(rows):
    return [(i, slice(i * STATE, (i + 1) * STATE)) for i in range(rows // STATE)]


def core_kernel(keep_ref, recv_ref, send_ref, own_ref):
    device = lax.axis_index(SEQ)
    core, side = device % 2, (device // 2) % 2
    rows = keep_ref.shape[1] - 16
    for out, pick in ((send_ref, 1 - side), (own_ref, side)):
        mine, other = keep_ref.at[pick], recv_ref.at[pick]
        join_totals(mine, other, core == 0, out, rows)


def join_totals(mine, other, mine_first, out, rows):
    d_mine = unpack_decay(mine[rows:, :])
    d_other = unpack_decay(other[rows:, :])
    d_later = jnp.where(mine_first, d_other, d_mine)
    f_mine = jnp.where(mine_first, d_later, 1.0)
    f_other = jnp.where(mine_first, 1.0, d_later)
    for i, part in blocks_of(rows):
        total = mine[part, :].astype(F32) * f_mine[i : i + 1] + other[part, :].astype(F32) * f_other[
            i : i + 1
        ]
        out[part, :] = total.astype(BF16)
    out[rows:, :] = pack_decay(d_mine * d_other)


def total_kernel(mine_ref, other_ref, cache_ref, c_ref, out_ref, *, bit):
    device = lax.axis_index(SEQ)
    rows = mine_ref.shape[0] - 16
    join_totals(mine_ref, other_ref, (device // bit) % 2 == 0, out_ref, rows)


def prefix_kernel(mine_ref, other_ref, pre_ref, dpre_ref, out_ref, opre_ref, odpre_ref, *, bit):
    device = lax.axis_index(SEQ)
    rows = mine_ref.shape[0] - 16
    first = (device // bit) % 2 == 0
    join_totals(mine_ref, other_ref, first, out_ref, rows)
    d_other = unpack_decay(other_ref[rows:, :])
    d_pre = dpre_ref[...]
    gain = jnp.where(first, 0.0, d_pre)
    for i, part in blocks_of(rows):
        opre_ref[part, :] = pre_ref[part, :] + gain[i : i + 1] * other_ref[part, :].astype(F32)
    odpre_ref[...] = jnp.where(first, d_pre, d_pre * d_other)


def start_kernel(mine_ref, other_ref, after_ref, out_ref, opre_ref, odpre_ref, *, bit):
    device = lax.axis_index(SEQ)
    rows = mine_ref.shape[0] - 16
    first = (device // bit) % 2 == 0
    join_totals(mine_ref, other_ref, first, out_ref, rows)
    d_other = unpack_decay(other_ref[rows:, :])
    opre_ref[...] = jnp.where(first, 0.0, other_ref[:rows, :].astype(F32))
    odpre_ref[...] = jnp.where(first, 1.0, d_other)


def enter_kernel(
    mine_ref,
    other_ref,
    pre_ref,
    dpre_ref,
    cache_ref,
    own_ref,
    recv_ref,
    after_ref,
    send_ref,
    stay_ref,
    fin_ref,
    *,
    bit,
):
    device = lax.axis_index(SEQ)
    side = (device // 2) % 2
    rows = mine_ref.shape[0] - 16
    first = (device // bit) % 2 == 0
    d_mine = unpack_decay(mine_ref[rows:, :])
    d_other = unpack_decay(other_ref[rows:, :])
    d_later = jnp.where(first, d_other, d_mine)
    f_mine = jnp.where(first, d_later, 1.0)
    f_other = jnp.where(first, 1.0, d_later)
    d_all = d_mine * d_other
    d_pre = dpre_ref[...]
    gain = jnp.where(first, 0.0, d_pre)
    d_before = jnp.where(first, d_pre, d_pre * d_other)
    d_first = jnp.where(side == 0, unpack_decay(own_ref[rows:, :]), unpack_decay(recv_ref[rows:, :]))
    for i, part in blocks_of(rows):
        cache = cache_ref[part, :]
        other = other_ref[part, :].astype(F32)
        mine = mine_ref[part, :].astype(F32)
        row = slice(i, i + 1)
        fin_ref[part, :] = d_all[row] * cache + mine * f_mine[row] + other * f_other[row]
        plane = d_before[row] * cache + pre_ref[part, :] + gain[row] * other
        t_first = jnp.where(side == 0, own_ref[part, :].astype(F32), recv_ref[part, :].astype(F32))
        second = d_first[row] * plane + t_first
        send_ref[part, :] = jnp.where(side == 0, second, plane).astype(BF16)
        stay_ref[part, :] = jnp.where(side == 0, plane, second).astype(BF16)


def chip_kernel(stay_ref, recv_ref, keep_ref, part_ref, gate_ref, grow_ref, send_ref):
    enter_block(stay_ref, recv_ref, keep_ref, part_ref, send_ref, lax.axis_index(SEQ) % 2 == 1)


def enter_block(stay_ref, recv_ref, keep_ref, part_ref, out_ref, first):
    device = lax.axis_index(SEQ)
    core, side = device % 2, (device // 2) % 2
    rows = stay_ref.shape[0]

    def fill(values):
        for y in range(PAIR):
            for mine, source in ((True, stay_ref), (False, recv_ref)):

                @pl.when((side == y) == mine)
                def _(y=y, source=source):
                    values(y, source)

    @pl.when(first)
    def _():
        def values(y, source):
            out_ref[y] = source[...]

        fill(values)

    for kept, local in ((0, keep_ref), (1, part_ref)):

        @pl.when(jnp.logical_not(first) & (core == kept))
        def _(local=local):
            def values(y, source):
                decay = unpack_decay(local[y, rows:, :])
                for i, part in blocks_of(rows):
                    entered = decay[i : i + 1] * source[part, :].astype(F32)
                    out_ref[y, part, :] = (entered + local[y, part, :].astype(F32)).astype(BF16)

            fill(values)


def diag_kernel(
    xc_ref,
    xfix_ref,
    b_ref,
    bfix_ref,
    c_ref,
    cum_ref,
    row_ref,
    skip_ref,
    after_ref,
    out_ref,
    *,
    head_dim,
    first,
):
    rows = xc_ref.shape[0]
    heads = cum_ref.shape[1]
    per_group = heads // GROUPS
    below = lax.broadcasted_iota(jnp.int32, (rows, rows), 0)
    across = lax.broadcasted_iota(jnp.int32, (rows, rows), 1)
    mask = below >= across
    quad = 128 // head_dim
    lane = lax.broadcasted_iota(jnp.int32, (rows, 128), 1) // head_dim
    for g in range(out_ref.shape[1] // (per_group * head_dim)):
        part = slice((first + g) * STATE, (first + g + 1) * STATE)
        b_all = jnp.concatenate([bfix_ref[:, part], b_ref[TOP:, part]], axis=0)
        c_dot_b = lax.dot_general(
            c_ref[:, part], b_all, (((1,), (1,)), ((), ())), preferred_element_type=F32
        )
        for q in range(per_group // quad):
            base = (first + g) * per_group + q * quad
            cols = pl.ds(base * head_dim, 128)
            x_quad = jnp.concatenate([xfix_ref[:, cols], xc_ref[TOP:, cols]], axis=0)
            lhs, rhs = [], []
            for k in range(quad):
                head = base + k
                gap = cum_ref[:, head : head + 1] - row_ref[head : head + 1, :]
                decay = jnp.exp2(jnp.where(mask, gap, -1e30))
                lhs.append((c_dot_b * decay).astype(BF16))
                rhs.append(jnp.where(lane == k, x_quad, jnp.zeros_like(x_quad)))
            skip = skip_ref[:, base : base + 1]
            for k in range(1, quad):
                skip = jnp.where(lane[0:1] == k, skip_ref[:, base + k : base + k + 1], skip)
            inner = jnp.dot(
                jnp.concatenate(lhs, axis=1),
                jnp.concatenate(rhs, axis=0),
                preferred_element_type=F32,
            )
            out = pl.ds((g * per_group + q * quad) * head_dim, 128)
            out_ref[:, out] = inner + skip * x_quad.astype(F32)


def gate_kernel(len_ref, z_ref, after_ref, gate_ref):
    rows, width = z_ref.shape
    first = lax.axis_index(SEQ) * rows
    live = first + lax.broadcasted_iota(jnp.int32, (rows, 128), 0) < len_ref[0]
    for j in range(width // 128):
        cols = pl.ds(128 * j, 128)
        gate_ref[:, cols] = jnp.where(live, silu(z_ref[:, cols].astype(F32)), 0.0)


def grow_kernel(ecum_ref, final_ref, grow_ref, mine_ref, *, head_dim):
    steps = ecum_ref.shape[0]
    per_step = ecum_ref.shape[2] // 2
    width = per_step * head_dim
    head = lax.broadcasted_iota(jnp.int32, (2 * per_step, width), 0) % per_step
    lane = lax.broadcasted_iota(jnp.int32, (2 * per_step, width), 1)
    spread = jnp.where(head == lane // head_dim, 1.0, 0.0).astype(BF16)
    for i in range(steps):
        grow_ref[:, i * width : (i + 1) * width] = jnp.dot(
            ecum_ref[i], spread, preferred_element_type=F32
        )
    step = (lax.axis_index(SEQ) // (2 * PAIR)) % (final_ref.shape[0] // STATE)
    mine = final_ref[pl.ds(pl.multiple_of(step * STATE, STATE), STATE), :]
    mine_ref[...] = mine.T


def gated_part(parts, gate_ref, grow_ref, c_ref, state, group, half):
    width = gate_ref.shape[1] // GROUPS
    unit = width // 2
    per_part = GROUPS // len(parts)
    inside = pl.ds(pl.multiple_of((group % per_part) * width + half * unit, 128), unit)
    cols = pl.ds(pl.multiple_of(group * width + half * unit, 128), unit)
    entering = jnp.dot(
        c_ref[:, group * STATE : (group + 1) * STATE], state, preferred_element_type=F32
    )
    y_all = parts[group // per_part][:, inside] + grow_ref[:, cols] * entering
    return y_all.astype(BF16).astype(F32) * gate_ref[:, cols], cols


def own_kernel(*refs, parts):
    diag_refs, refs = refs[:parts], refs[parts:]
    gate_ref, grow_ref, c_ref, stay_ref, recv_ref, keep_ref, part_ref, after_ref, out_ref, own_ref = refs
    core = lax.axis_index(SEQ) % 2
    enter_block(stay_ref, recv_ref, keep_ref, part_ref, own_ref, core == 0)
    for g in range(GROUPS):
        i, y = g // PAIR, g % PAIR
        state = own_ref[y, i * STATE : (i + 1) * STATE, :]
        out_ref[g], _ = gated_part(diag_refs, gate_ref, grow_ref, c_ref, state, g, core)


def out_kernel(*refs, parts):
    diag_refs, refs = refs[:parts], refs[parts:]
    gate_ref, grow_ref, c_ref, own_ref, recv_ref, gain_ref, out_ref, held, sems = refs
    core = lax.axis_index(SEQ) % 2
    unit = own_ref.shape[2]
    width = 2 * unit
    copies = []
    for g in range(GROUPS):
        i, y = g // PAIR, g % PAIR
        state = recv_ref[y, i * STATE : (i + 1) * STATE, :]
        other, cols = gated_part(diag_refs, gate_ref, grow_ref, c_ref, state, g, 1 - core)
        own = own_ref[g]
        squares = jnp.sum(own * own + other * other, axis=1, keepdims=True)
        scale = lax.rsqrt(squares * (1.0 / width) + 1e-05)
        for half, value in ((core, own), (1 - core, other)):
            cols = pl.ds(pl.multiple_of(g * width + half * unit, 128), unit)
            lanes = pl.ds(pl.multiple_of(half * unit, 128), unit)
            held[g, :, lanes] = (value * scale * gain_ref[:, cols]).astype(BF16)
        copy = pltpu.make_async_copy(
            held.at[g], out_ref.at[:, pl.ds(g * width, width)], sems.at[g]
        )
        copy.start()
        copies.append(copy)
    for copy in copies:
        copy.wait()


def swap(value, mask):
    devices = range(lax.axis_size(SEQ))
    return lax.ppermute(value, SEQ, [(i, i ^ mask) for i in devices])


def chip_route(count):
    route = {i: i + 1 for i in range(1, count - 1, 2)}
    route.update({i: i - 1 for i in range(4, count - 2, 2)})
    route.update({2: 0, 0: 1, count - 2: count - 1, count - 1: count - 3})
    return sorted(route.items())


def near(shape, dtype):
    return pltpu.VMEM(shape, dtype)


VMEM_SPEC = pl.BlockSpec(memory_space=pltpu.VMEM)
ANY_SPEC = pl.BlockSpec(memory_space=pl.ANY)


def plain_call(
    body, out_shape, *args, smem=(), far=(), after=(), mib=12, nbytes=2**20, scratch=(), out_specs=None
):
    return pl.pallas_call(
        body,
        out_shape=out_shape,
        in_specs=[pl.BlockSpec(memory_space=pltpu.SMEM)] * len(smem)
        + [ANY_SPEC] * len(far)
        + [VMEM_SPEC] * len(args) + [ANY_SPEC] * len(after),
        out_specs=out_specs or jax.tree.map(lambda _: VMEM_SPEC, out_shape),
        scratch_shapes=list(scratch),
        compiler_params=pltpu.CompilerParams(vmem_limit_bytes=mib * 2**20),
        cost_estimate=pl.CostEstimate(flops=0, bytes_accessed=nbytes, transcendentals=0),
    )(*smem, *[pltpu.with_memory_space_constraint(a, pltpu.HBM) for a in far], *args, *after)


def body(
    x_in,
    bc_in,
    z_in,
    dt_in,
    conv_weight,
    conv_bias,
    dt_bias,
    a_log,
    d_skip,
    norm_gain,
    conv_cache,
    cache_state,
    lengths,
):
    rows, inner = x_in.shape
    heads = dt_in.shape[1]
    head_dim = inner // heads
    devices = lax.axis_size(SEQ)
    index = lax.axis_index(SEQ)
    share = heads // devices
    steps = GROUPS // PAIR
    per_step = heads // steps
    width = inner // steps
    side = GROUPS * STATE
    unit = width // (2 * PAIR)
    unit_heads = unit // head_dim
    state_rows = steps * STATE
    msg_rows = state_rows + 16
    dma = pltpu.SemaphoreType.DMA

    fetched = [
        x_in,
        bc_in,
        conv_weight,
        conv_bias.reshape(1, -1),
        dt_in,
        dt_bias.reshape(1, -1),
        a_log.reshape(1, -1),
    ]
    rim, *ready = plain_call(
        functools.partial(rim_kernel, count=len(fetched)),
        [near((RIM, inner + 2 * side), BF16)] + [near(a.shape, a.dtype) for a in fetched],
        far=fetched,
        mib=4,
        scratch=[
            pltpu.VMEM((TOP, inner), BF16),
            pltpu.VMEM((TOP, 2 * side), BF16),
            dma((2 + len(fetched),)),
        ],
    )
    near_rim = lax.ppermute(rim, SEQ, chip_route(devices))
    core_rim = swap(rim, 1)

    xc, bc, prex, preb, cum, step_size, dec, top, local = plain_call(
        functools.partial(conv_kernel, heads=heads, head_dim=head_dim),
        (
            near((rows, inner), BF16),
            near((rows, side), BF16),
            near((8, inner), F32),
            near((8, side), F32),
            near((rows, heads), F32),
            near((rows, heads), F32),
            near((2 * PAIR, 16, unit), BF16),
            near((8, inner), F32),
            near((GROUPS, STATE, width // PAIR), F32),
        ),
        *ready,
        smem=(lengths,),
        after=(rim,),
        scratch=[
            pltpu.VMEM((4, 8 + rows, 128), F32),
            pltpu.VMEM((2, rows, width), F32),
            pltpu.VMEM((2, rows, width), BF16),
        ],
        mib=16,
        nbytes=4 * 2**20,
    )

    pair_msg = near((PAIR, msg_rows, unit), BF16)
    send, keep, xfix, bfix = plain_call(
        fix_kernel,
        (pair_msg, pair_msg, near((TOP, inner), BF16), near((TOP, side), BF16)),
        near_rim,
        core_rim,
        conv_cache,
        ready[2],
        prex,
        preb,
        xc,
        bc,
        top,
        local,
        dec,
        scratch=[pltpu.VMEM((16, inner + side), F32)],
    )

    message = near((msg_rows, unit), BF16)
    part = swap(send, 1)
    send_y, own = plain_call(core_kernel, (message, message), keep, part)
    recv = swap(send_y, 2)
    chunks = 4
    cache = plain_call(
        functools.partial(cache_kernel, unit_heads=unit_heads),
        near((state_rows, unit), F32),
        far=(cache_state.transpose(1, 2, 0),),
        after=(own,),
        scratch=[
            pltpu.VMEM((head_dim, STATE, heads), F32),
            pltpu.VMEM((unit // 128, steps, STATE, 128), F32),
            dma((chunks,)),
        ],
        nbytes=2 * 2**20,
    )
    cc, log_cum, row, ecum = plain_call(
        side_kernel,
        (
            near((rows, side), BF16),
            near((rows, heads), F32),
            near((heads, rows), F32),
            near((steps, rows, 2 * per_step), BF16),
        ),
        ready[1],
        ready[2],
        ready[3],
        near_rim,
        core_rim,
        conv_cache,
        cum,
        step_size,
        after=(own,),
        scratch=[pltpu.VMEM((4, 8 + rows, 128), F32)],
    )
    total = plain_call(
        functools.partial(total_kernel, bit=2), message, own, recv, after=(cache, cc)
    )

    def diag_part(k, order):
        return plain_call(
            functools.partial(diag_kernel, head_dim=head_dim, first=k * GROUPS // 2),
            near((rows, inner // 2), F32),
            xc,
            xfix,
            bc,
            bfix,
            cc,
            log_cum,
            row,
            d_skip.reshape(1, -1),
            after=(order,),
            nbytes=4 * 2**20,
        )

    diags = [diag_part(0, total)]
    pre = None
    bit = 4
    pre_shape = (near((state_rows, unit), F32), near((8, unit), F32))
    while 2 * bit < devices:
        other = swap(total, 2 * bit - 4)
        if pre is None:
            total, *pre = plain_call(
                functools.partial(start_kernel, bit=bit),
                (message,) + pre_shape,
                total,
                other,
                after=(diags[0],),
            )
        else:
            total, *pre = plain_call(
                functools.partial(prefix_kernel, bit=bit), (message,) + pre_shape, total, other, *pre
            )
        bit *= 2
    if pre is None:
        pre = [jnp.zeros((state_rows, unit), F32), jnp.ones((8, unit), F32)]
    last = total
    other = swap(last, 2 * bit - 4)
    diags.append(diag_part(1, last))
    state_out = near((state_rows, unit), BF16)
    send_y, stay, final = plain_call(
        functools.partial(enter_kernel, bit=bit),
        (state_out, state_out, near((state_rows, unit), F32)),
        total,
        other,
        *pre,
        cache,
        own,
        recv,
        after=(diags[1],),
    )
    recv_y = swap(send_y, 2)
    grow, mine = plain_call(
        functools.partial(grow_kernel, head_dim=head_dim),
        (near((rows, inner), F32), jax.ShapeDtypeStruct((unit, STATE), F32)),
        ecum,
        final,
        nbytes=5 * 2**20,
    )
    gate = plain_call(
        gate_kernel, near((rows, inner), F32), z_in, smem=(lengths,), after=(final,)
    )
    half = near((PAIR, state_rows, unit), BF16)
    send_c = plain_call(chip_kernel, half, stay, recv_y, keep, part, after=(gate, grow))
    enter_recv = swap(send_c, 1)
    gated_own = plain_call(
        functools.partial(own_kernel, parts=len(diags)),
        near((GROUPS, rows, unit), F32),
        *diags,
        gate,
        grow,
        cc,
        stay,
        recv_y,
        keep,
        part,
        after=(send_c,),
        scratch=[pltpu.VMEM((PAIR, state_rows, unit), BF16)],
    )

    mixed = plain_call(
        functools.partial(out_kernel, parts=len(diags)),
        jax.ShapeDtypeStruct((rows, inner), BF16),
        *diags,
        gate,
        grow,
        cc,
        gated_own,
        enter_recv,
        norm_gain.reshape(1, -1),
        out_specs=ANY_SPEC,
        scratch=[pltpu.VMEM((GROUPS, rows, 2 * unit), BF16), dma((GROUPS,))],
        mib=16,
        nbytes=4 * 2**20,
    )

    if share * head_dim == unit and devices == 2 * PAIR * steps:
        mine = mine.reshape(share, head_dim, STATE)
    else:
        around = [[4 * i + j for j in range(4)] for i in range(devices // 4)]
        every = final.reshape(steps, STATE, unit)
        every = lax.all_gather(every, SEQ, axis=1, axis_index_groups=around)
        every = every.reshape(steps * 2 * PAIR, STATE, unit).transpose(0, 2, 1)
        every = every.reshape(heads, head_dim, STATE)
        mine = lax.dynamic_slice_in_dim(every, index * share, share, 0)
    return (mixed, mine)


def solution(mesh):
    in_specs = (
        P(("groups", "seq"), None),
        P(("groups", "seq"), None),
        P(("groups", "seq"), None),
        P(("groups", "seq"), None),
        P(),
        P(),
        P(),
        P(),
        P(),
        P(),
        P("groups", None),
        P("groups", None, None),
        P("groups"),
    )
    out_specs = (P(("groups", "seq"), None), P(("groups", "seq"), None, None))
    return jax.shard_map(body, mesh=mesh, in_specs=in_specs, out_specs=out_specs, check_vma=False)
```

```python
import functools

import jax
import jax.numpy as jnp
from jax import lax
from jax.experimental import pallas as pl
from jax.experimental.pallas import tpu as pltpu
from jax.sharding import PartitionSpec as P

STATE = 64
GROUPS = 8
CONV_W = 4
RIM = CONV_W - 1
LOG2E = 1.4426950408889634
BF16 = jnp.bfloat16
F32 = jnp.float32
HI = lax.Precision.HIGHEST
SEQ = "seq"
PAIR = 2
TOP = 16


def silu(v):
    return silu_of_twice(0.5 * v)


def silu_of_twice(half):
    return half + half * jnp.tanh(half)


def split2(v):
    hi = v.astype(BF16)
    return hi, (v - hi.astype(F32)).astype(BF16)


def rim_kernel(*refs, count):
    x_ref, bc_ref = refs[:2]
    sources, out_ref, refs = refs[:count], refs[count], refs[count + 1 :]
    targets, (x_rows, bc_rows, sems) = refs[:count], refs[count:]
    rows, inner = x_ref.shape
    pairs = [
        (x_ref.at[pl.ds(rows - TOP, TOP), :], x_rows),
        (bc_ref.at[pl.ds(rows - TOP, TOP), :], bc_rows),
    ] + list(zip(sources, targets))
    copies = [pltpu.make_async_copy(a, b, sems.at[k]) for k, (a, b) in enumerate(pairs)]
    for copy in copies:
        copy.start()
    for copy in copies[:2]:
        copy.wait()
    out_ref[:, :inner] = x_rows[...].astype(F32)[TOP - RIM :, :].astype(BF16)
    out_ref[:, inner:] = bc_rows[...].astype(F32)[TOP - RIM :, :].astype(BF16)
    for copy in copies[2:]:
        copy.wait()


def pack_decay(dec):
    hi, lo = split2(dec)
    return jnp.concatenate([hi.astype(F32), lo.astype(F32)], axis=0).astype(BF16)


def unpack_decay(rows):
    both = rows.astype(F32)
    return both[0:8] + both[8:16]


def convolve(values, w_ref, bias_ref, first, ext, rows):
    cols = pl.ds(first, 128)
    ext[8:, :] = values.astype(F32)
    total = jnp.broadcast_to(0.5 * bias_ref[:, cols], (rows, 128))
    for k in range(CONV_W):
        total = total + ext[pl.ds(8 + k - RIM, rows), :] * (0.5 * w_ref[k : k + 1, cols])
    return total


def conv_kernel(
    len_ref,
    x_ref,
    bc_ref,
    w_ref,
    bias_ref,
    dt_ref,
    dtb_ref,
    alog_ref,
    after_ref,
    xo_ref,
    bo_ref,
    prex_ref,
    preb_ref,
    cum_ref,
    step_ref,
    dec_ref,
    top_ref,
    local_ref,
    ext,
    tails,
    scaled,
    *,
    heads,
    head_dim,
):
    _, rows, width = tails.shape
    side = bo_ref.shape[1]
    inner = x_ref.shape[1]
    steps = inner // width
    per_step = heads // steps
    spare = ext.shape[0]
    for k in range(spare):
        ext[k, 0:8, :] = jnp.zeros((8, 128), F32)

    raw = dt_ref[...].astype(F32) + dtb_ref[...]
    soft = jnp.maximum(raw, 0.0) + jnp.log1p(jnp.exp(-jnp.abs(raw)))
    token = lax.axis_index(SEQ) * rows + lax.broadcasted_iota(jnp.int32, (rows, heads), 0)
    dt = jnp.where(token < len_ref[0], soft, 0.0)
    step_ref[...] = dt
    rate = -jnp.exp(alog_ref[...]) * dt
    below = lax.broadcasted_iota(jnp.int32, (rows, rows), 0)
    across = lax.broadcasted_iota(jnp.int32, (rows, rows), 1)
    tri = jnp.where(below >= across, 1.0, 0.0).astype(BF16)
    hi, rest = split2(rate)
    mid, low = split2(rate - hi.astype(F32))
    sums = jnp.dot(tri, jnp.concatenate([hi, mid, low], axis=1), preferred_element_type=F32)
    cum = sums[:, :heads] + (sums[:, heads : 2 * heads] + sums[:, 2 * heads :])
    cum_ref[...] = cum

    for j in range(side // 128):
        cols = pl.ds(128 * j, 128)
        total = convolve(bc_ref[:, cols], w_ref, bias_ref, inner + 128 * j, ext.at[j % spare], rows)
        preb_ref[:, cols] = total[0:8]
        bo_ref[:, cols] = silu_of_twice(total).astype(BF16)

    last = cum[rows - 1 : rows, :]
    tail_hi, tail_lo = split2(jnp.exp(last - cum) * dt)
    unit_heads = per_step // (2 * PAIR)
    unit_cols = unit_heads * head_dim
    owner = lax.broadcasted_iota(jnp.int32, (8, heads), 0)
    head = lax.broadcasted_iota(jnp.int32, (8, heads), 1)
    dec_hi, dec_lo = split2(jnp.exp(last))
    chosen = jnp.concatenate(
        [jnp.where(head // per_step == owner, v.astype(F32), 0.0) for v in (dec_hi, dec_lo)], axis=0
    ).astype(BF16)
    head = lax.broadcasted_iota(jnp.int32, (heads, unit_cols), 0)
    lane = lax.broadcasted_iota(jnp.int32, (heads, unit_cols), 1)
    same = head % unit_heads == lane // head_dim
    for q in range(2 * PAIR):
        spread = jnp.where(same & ((head % per_step) // unit_heads == q), 1.0, 0.0).astype(BF16)
        dec_ref[q] = jnp.dot(chosen, spread, preferred_element_type=F32).astype(BF16)

    head = lax.broadcasted_iota(jnp.int32, (2 * per_step, width), 0) % per_step
    lane = lax.broadcasted_iota(jnp.int32, (2 * per_step, width), 1) // head_dim
    spread = jnp.where(head == lane, 1.0, 0.0).astype(BF16)

    def widen(i):
        part = slice(i * per_step, (i + 1) * per_step)
        both = jnp.concatenate([tail_hi[:, part], tail_lo[:, part]], axis=1)
        tails[i % 2] = jnp.dot(both, spread, preferred_element_type=F32)

    early = lax.broadcasted_iota(jnp.int32, (8, 128), 0) < RIM
    group = width // PAIR
    widen(0)
    for i in range(steps):
        if i + 1 < steps:
            widen(i + 1)
        for j in range(width // 128):
            cols, lanes = pl.ds(i * width + 128 * j, 128), slice(128 * j, 128 * (j + 1))
            total = convolve(
                x_ref[:, cols], w_ref, bias_ref, i * width + 128 * j, ext.at[j % spare], rows
            )
            prex_ref[:, cols] = total[0:8]
            xj = silu_of_twice(total).astype(BF16)
            xo_ref[:, cols] = xj
            tail = tails[i % 2, :, lanes]
            top_ref[:, cols] = jnp.where(early, tail[0:8], 0.0)
            tail = jnp.concatenate([jnp.where(early, 0.0, tail[0:8]), tail[8:]], axis=0)
            scaled[i % 2, :, lanes] = (xj.astype(F32) * tail).astype(BF16)
        b_turned = bo_ref[:, i * PAIR * STATE : (i + 1) * PAIR * STATE].T
        for y in range(PAIR):
            local_ref[PAIR * i + y] = jnp.dot(
                b_turned[y * STATE : (y + 1) * STATE, :],
                scaled[i % 2, :, y * group : (y + 1) * group],
                preferred_element_type=F32,
            )


def before_block(near_rim, core_rim, cache):
    device = lax.axis_index(SEQ)
    rim = jnp.where(device % 2 == 1, core_rim.astype(F32), near_rim.astype(F32))
    return jnp.where(device == 0, cache.astype(F32), rim)


def side_kernel(
    bc_ref,
    w_ref,
    bias_ref,
    near_ref,
    core_ref,
    cache_ref,
    cum_ref,
    step_ref,
    after_ref,
    co_ref,
    log_ref,
    row_ref,
    ecum_ref,
    ext,
):
    rows, heads = cum_ref.shape
    side = co_ref.shape[1]
    first = w_ref.shape[1] - side
    spare = ext.shape[0]
    for j in range(side // 128):
        cols = pl.ds(first + 128 * j, 128)
        ext[j % spare, 8 - RIM : 8, :] = before_block(
            near_ref[:, cols], core_ref[:, cols], cache_ref[:, cols]
        )
        values = bc_ref[:, pl.ds(side + 128 * j, 128)]
        total = convolve(values, w_ref, bias_ref, first + 128 * j, ext.at[j % spare], rows)
        co_ref[:, pl.ds(128 * j, 128)] = silu_of_twice(total).astype(BF16)
    cum, dt = cum_ref[...], step_ref[...]
    log_ref[...] = cum * LOG2E
    log_dt = jnp.where(dt > 0.0, jnp.log(jnp.maximum(dt, 1e-38)) * LOG2E, -1e30)
    row_ref[...] = (cum * LOG2E - log_dt).T
    ecum_hi, ecum_lo = split2(jnp.exp(cum))
    steps, _, twice = ecum_ref.shape
    for i in range(steps):
        part = slice(i * twice // 2, (i + 1) * twice // 2)
        ecum_ref[i] = jnp.concatenate([ecum_hi[:, part], ecum_lo[:, part]], axis=1)


def fix_kernel(
    near_ref,
    core_ref,
    cache_ref,
    w_ref,
    prex_ref,
    preb_ref,
    xc_ref,
    bc_ref,
    top_ref,
    local_ref,
    dec_ref,
    send_ref,
    keep_ref,
    xfix_ref,
    bfix_ref,
    ext,
):
    device = lax.axis_index(SEQ)
    core = device % 2
    inner = xc_ref.shape[1]
    side = bc_ref.shape[1]
    ext[8:, :] = jnp.zeros((8, ext.shape[1]), F32)
    cols = pl.ds(0, ext.shape[1])
    ext[8 - RIM : 8, :] = before_block(near_ref[:, cols], core_ref[:, cols], cache_ref[:, cols])

    def fix(pre, old, dst, first, count):
        cols = pl.ds(first, count)
        total = pre[...]
        for k in range(RIM):
            total = total + ext[pl.ds(8 - RIM + k, 8), cols] * (0.5 * w_ref[k : k + 1, cols])
        fixed = silu_of_twice(total)
        dst[...] = jnp.concatenate([fixed, old[0:TOP, :].astype(F32)[8:, :]], axis=0).astype(BF16)
        return fixed.astype(BF16).astype(F32)

    x_top = fix(prex_ref, xc_ref, xfix_ref, 0, inner)
    b_top = fix(preb_ref, bc_ref, bfix_ref, inner, side)
    scaled = x_top * top_ref[...]
    scaled = jnp.concatenate([scaled, jnp.zeros_like(scaled)], axis=0).astype(BF16)
    b_top = jnp.concatenate([b_top, jnp.zeros_like(b_top)], axis=0)
    b_turned = b_top.T.astype(BF16)
    groups, _, width = local_ref.shape
    unit = width // 2
    for g in range(groups):
        extra = jnp.dot(
            b_turned[g * STATE : (g + 1) * STATE, :],
            scaled[:, g * width : (g + 1) * width],
            preferred_element_type=F32,
        )
        whole_state = local_ref[g] + extra
        low, high = whole_state[:, :unit], whole_state[:, unit:]
        where = pl.ds((g // PAIR) * STATE, STATE)
        send_ref[g % PAIR, where, :] = jnp.where(core == 0, high, low).astype(BF16)
        keep_ref[g % PAIR, where, :] = jnp.where(core == 0, low, high).astype(BF16)
    where = pl.ds(groups // PAIR * STATE, 16)
    for y in range(PAIR):
        send_ref[y, where, :] = dec_ref[2 * y + 1 - core]
        keep_ref[y, where, :] = dec_ref[2 * y + core]


def cache_kernel(state_hbm, after_ref, out_ref, state_ref, held, sems, *, unit_heads):
    channels, size, heads = state_hbm.shape
    chunks = sems.shape[0]
    count = channels // chunks
    copies = []
    for c in range(chunks):
        part = pl.ds(c * count, count)
        copies.append(pltpu.make_async_copy(state_hbm.at[part], state_ref.at[part], sems.at[c]))
        copies[c].start()
    per_tile = 128 // unit_heads
    quarters = 2 * PAIR
    steps = heads // (quarters * unit_heads)
    quarter = lax.axis_index(SEQ) % quarters
    lane = lax.broadcasted_iota(jnp.int32, (size, 128), 1) // unit_heads
    for channel in range(channels):
        if channel % count == 0:
            copies[channel // count].wait()
        tile, place = channel // per_tile, channel % per_tile
        value = state_ref[channel]
        for i in range(steps):
            start = (i * quarters + quarter) * unit_heads
            moved = pltpu.roll(value, (place * unit_heads - start + heads) % heads, axis=1)
            if place == 0:
                held[tile, i] = moved
            else:
                held[tile, i] = jnp.where(lane == place, moved, held[tile, i])
    unit = out_ref.shape[1]
    dim = unit // unit_heads
    source = lax.broadcasted_iota(jnp.int32, (unit, unit), 0)
    target = lax.broadcasted_iota(jnp.int32, (unit, unit), 1)
    chosen = source == (target % dim) * unit_heads + target // dim
    order = jnp.where(chosen, 1.0, 0.0).astype(BF16)
    for i in range(steps):
        value = jnp.concatenate([held[t, i] for t in range(unit // 128)], axis=1)
        hi = value.astype(BF16)
        rest = value - hi.astype(F32)
        mid = rest.astype(BF16)
        low = (rest - mid.astype(F32)).astype(BF16)
        parts = jnp.dot(
            jnp.concatenate([hi, mid, low], axis=0), order, preferred_element_type=F32
        )
        out_ref[i * size : (i + 1) * size, :] = (
            parts[:size] + parts[size : 2 * size] + parts[2 * size :]
        )


def blocks_of(rows):
    return [(i, slice(i * STATE, (i + 1) * STATE)) for i in range(rows // STATE)]


def core_kernel(keep_ref, recv_ref, send_ref, own_ref):
    device = lax.axis_index(SEQ)
    core, side = device % 2, (device // 2) % 2
    rows = keep_ref.shape[1] - 16
    for out, pick in ((send_ref, 1 - side), (own_ref, side)):
        mine, other = keep_ref.at[pick], recv_ref.at[pick]
        join_totals(mine, other, core == 0, out, rows)


def join_totals(mine, other, mine_first, out, rows):
    d_mine = unpack_decay(mine[rows:, :])
    d_other = unpack_decay(other[rows:, :])
    d_later = jnp.where(mine_first, d_other, d_mine)
    f_mine = jnp.where(mine_first, d_later, 1.0)
    f_other = jnp.where(mine_first, 1.0, d_later)
    for i, part in blocks_of(rows):
        total = mine[part, :].astype(F32) * f_mine[i : i + 1] + other[part, :].astype(F32) * f_other[
            i : i + 1
        ]
        out[part, :] = total.astype(BF16)
    out[rows:, :] = pack_decay(d_mine * d_other)


def total_kernel(mine_ref, other_ref, cache_ref, c_ref, out_ref, *, bit):
    device = lax.axis_index(SEQ)
    rows = mine_ref.shape[0] - 16
    join_totals(mine_ref, other_ref, (device // bit) % 2 == 0, out_ref, rows)


def prefix_kernel(mine_ref, other_ref, pre_ref, dpre_ref, out_ref, opre_ref, odpre_ref, *, bit):
    device = lax.axis_index(SEQ)
    rows = mine_ref.shape[0] - 16
    first = (device // bit) % 2 == 0
    join_totals(mine_ref, other_ref, first, out_ref, rows)
    d_other = unpack_decay(other_ref[rows:, :])
    d_pre = dpre_ref[...]
    gain = jnp.where(first, 0.0, d_pre)
    for i, part in blocks_of(rows):
        opre_ref[part, :] = pre_ref[part, :] + gain[i : i + 1] * other_ref[part, :].astype(F32)
    odpre_ref[...] = jnp.where(first, d_pre, d_pre * d_other)


def start_kernel(mine_ref, other_ref, after_ref, out_ref, opre_ref, odpre_ref, *, bit):
    device = lax.axis_index(SEQ)
    rows = mine_ref.shape[0] - 16
    first = (device // bit) % 2 == 0
    join_totals(mine_ref, other_ref, first, out_ref, rows)
    d_other = unpack_decay(other_ref[rows:, :])
    opre_ref[...] = jnp.where(first, 0.0, other_ref[:rows, :].astype(F32))
    odpre_ref[...] = jnp.where(first, 1.0, d_other)


def enter_kernel(
    mine_ref,
    other_ref,
    pre_ref,
    dpre_ref,
    cache_ref,
    own_ref,
    recv_ref,
    after_ref,
    send_ref,
    stay_ref,
    fin_ref,
    *,
    bit,
):
    device = lax.axis_index(SEQ)
    side = (device // 2) % 2
    rows = mine_ref.shape[0] - 16
    first = (device // bit) % 2 == 0
    d_mine = unpack_decay(mine_ref[rows:, :])
    d_other = unpack_decay(other_ref[rows:, :])
    d_later = jnp.where(first, d_other, d_mine)
    f_mine = jnp.where(first, d_later, 1.0)
    f_other = jnp.where(first, 1.0, d_later)
    d_all = d_mine * d_other
    d_pre = dpre_ref[...]
    gain = jnp.where(first, 0.0, d_pre)
    d_before = jnp.where(first, d_pre, d_pre * d_other)
    d_first = jnp.where(side == 0, unpack_decay(own_ref[rows:, :]), unpack_decay(recv_ref[rows:, :]))
    for i, part in blocks_of(rows):
        cache = cache_ref[part, :]
        other = other_ref[part, :].astype(F32)
        mine = mine_ref[part, :].astype(F32)
        row = slice(i, i + 1)
        fin_ref[part, :] = d_all[row] * cache + mine * f_mine[row] + other * f_other[row]
        plane = d_before[row] * cache + pre_ref[part, :] + gain[row] * other
        t_first = jnp.where(side == 0, own_ref[part, :].astype(F32), recv_ref[part, :].astype(F32))
        second = d_first[row] * plane + t_first
        send_ref[part, :] = jnp.where(side == 0, second, plane).astype(BF16)
        stay_ref[part, :] = jnp.where(side == 0, plane, second).astype(BF16)


def chip_kernel(stay_ref, recv_ref, keep_ref, part_ref, gate_ref, grow_ref, send_ref):
    enter_block(stay_ref, recv_ref, keep_ref, part_ref, send_ref, lax.axis_index(SEQ) % 2 == 1)


def enter_block(stay_ref, recv_ref, keep_ref, part_ref, out_ref, first):
    device = lax.axis_index(SEQ)
    core, side = device % 2, (device // 2) % 2
    rows = stay_ref.shape[0]

    def fill(values):
        for y in range(PAIR):
            for mine, source in ((True, stay_ref), (False, recv_ref)):

                @pl.when((side == y) == mine)
                def _(y=y, source=source):
                    values(y, source)

    @pl.when(first)
    def _():
        def values(y, source):
            out_ref[y] = source[...]

        fill(values)

    for kept, local in ((0, keep_ref), (1, part_ref)):

        @pl.when(jnp.logical_not(first) & (core == kept))
        def _(local=local):
            def values(y, source):
                decay = unpack_decay(local[y, rows:, :])
                for i, part in blocks_of(rows):
                    entered = decay[i : i + 1] * source[part, :].astype(F32)
                    out_ref[y, part, :] = (entered + local[y, part, :].astype(F32)).astype(BF16)

            fill(values)


def diag_kernel(
    xc_ref,
    xfix_ref,
    b_ref,
    bfix_ref,
    c_ref,
    cum_ref,
    row_ref,
    skip_ref,
    after_ref,
    out_ref,
    *,
    head_dim,
    first,
):
    rows = xc_ref.shape[0]
    heads = cum_ref.shape[1]
    per_group = heads // GROUPS
    below = lax.broadcasted_iota(jnp.int32, (rows, rows), 0)
    across = lax.broadcasted_iota(jnp.int32, (rows, rows), 1)
    mask = below >= across
    quad = 128 // head_dim
    lane = lax.broadcasted_iota(jnp.int32, (rows, 128), 1) // head_dim
    for g in range(out_ref.shape[1] // (per_group * head_dim)):
        part = slice((first + g) * STATE, (first + g + 1) * STATE)
        b_all = jnp.concatenate([bfix_ref[:, part], b_ref[TOP:, part]], axis=0)
        c_dot_b = lax.dot_general(
            c_ref[:, part], b_all, (((1,), (1,)), ((), ())), preferred_element_type=F32
        )
        for q in range(per_group // quad):
            base = (first + g) * per_group + q * quad
            cols = pl.ds(base * head_dim, 128)
            x_quad = jnp.concatenate([xfix_ref[:, cols], xc_ref[TOP:, cols]], axis=0)
            lhs, rhs = [], []
            for k in range(quad):
                head = base + k
                gap = cum_ref[:, head : head + 1] - row_ref[head : head + 1, :]
                decay = jnp.exp2(jnp.where(mask, gap, -1e30))
                lhs.append((c_dot_b * decay).astype(BF16))
                rhs.append(jnp.where(lane == k, x_quad, jnp.zeros_like(x_quad)))
            skip = skip_ref[:, base : base + 1]
            for k in range(1, quad):
                skip = jnp.where(lane[0:1] == k, skip_ref[:, base + k : base + k + 1], skip)
            inner = jnp.dot(
                jnp.concatenate(lhs, axis=1),
                jnp.concatenate(rhs, axis=0),
                preferred_element_type=F32,
            )
            out = pl.ds((g * per_group + q * quad) * head_dim, 128)
            out_ref[:, out] = inner + skip * x_quad.astype(F32)


def gate_kernel(len_ref, z_ref, after_ref, gate_ref):
    rows, width = z_ref.shape
    first = lax.axis_index(SEQ) * rows
    live = first + lax.broadcasted_iota(jnp.int32, (rows, 128), 0) < len_ref[0]
    for j in range(width // 128):
        cols = pl.ds(128 * j, 128)
        gate_ref[:, cols] = jnp.where(live, silu(z_ref[:, cols].astype(F32)), 0.0)


def grow_kernel(ecum_ref, final_ref, grow_ref, mine_ref, *, head_dim):
    steps = ecum_ref.shape[0]
    per_step = ecum_ref.shape[2] // 2
    width = per_step * head_dim
    head = lax.broadcasted_iota(jnp.int32, (2 * per_step, width), 0) % per_step
    lane = lax.broadcasted_iota(jnp.int32, (2 * per_step, width), 1)
    spread = jnp.where(head == lane // head_dim, 1.0, 0.0).astype(BF16)
    for i in range(steps):
        grow_ref[:, i * width : (i + 1) * width] = jnp.dot(
            ecum_ref[i], spread, preferred_element_type=F32
        )
    step = (lax.axis_index(SEQ) // (2 * PAIR)) % (final_ref.shape[0] // STATE)
    mine = final_ref[pl.ds(pl.multiple_of(step * STATE, STATE), STATE), :]
    mine_ref[...] = mine.T


def gated_part(parts, gate_ref, grow_ref, c_ref, state, group, half):
    width = gate_ref.shape[1] // GROUPS
    unit = width // 2
    per_part = GROUPS // len(parts)
    inside = pl.ds(pl.multiple_of((group % per_part) * width + half * unit, 128), unit)
    cols = pl.ds(pl.multiple_of(group * width + half * unit, 128), unit)
    entering = jnp.dot(
        c_ref[:, group * STATE : (group + 1) * STATE], state, preferred_element_type=F32
    )
    y_all = parts[group // per_part][:, inside] + grow_ref[:, cols] * entering
    return y_all.astype(BF16).astype(F32) * gate_ref[:, cols], cols


def sum_lanes(value):
    return sum(value[:, j : j + 128] for j in range(0, value.shape[1], 128))


def own_kernel(*refs, parts):
    diag_refs, refs = refs[:parts], refs[parts:]
    gate_ref, grow_ref, c_ref, gain_ref, stay_ref, recv_ref, keep_ref, part_ref = refs[:8]
    out_ref, sums_ref, own_ref = refs[9:]
    core = lax.axis_index(SEQ) % 2
    enter_block(stay_ref, recv_ref, keep_ref, part_ref, own_ref, core == 0)
    for g in range(GROUPS):
        i, y = g // PAIR, g % PAIR
        state = own_ref[y, i * STATE : (i + 1) * STATE, :]
        gated, cols = gated_part(diag_refs, gate_ref, grow_ref, c_ref, state, g, core)
        sums_ref[g] = sum_lanes(gated * gated)
        out_ref[g] = gated * gain_ref[:, cols]


def out_kernel(*refs, parts):
    diag_refs, refs = refs[:parts], refs[parts:]
    gate_ref, grow_ref, c_ref, own_ref, sums_ref, recv_ref, gain_ref, out_ref, held, sems = refs
    core = lax.axis_index(SEQ) % 2
    unit = own_ref.shape[2]
    width = 2 * unit
    copies = []
    for g in range(GROUPS):
        i, y = g // PAIR, g % PAIR
        state = recv_ref[y, i * STATE : (i + 1) * STATE, :]
        other, cols = gated_part(diag_refs, gate_ref, grow_ref, c_ref, state, g, 1 - core)
        squares = jnp.sum(sums_ref[g] + sum_lanes(other * other), axis=1, keepdims=True)
        scale = lax.rsqrt(squares * (1.0 / width) + 1e-05)
        for half, value in ((core, own_ref[g]), (1 - core, other * gain_ref[:, cols])):
            lanes = pl.ds(pl.multiple_of(half * unit, 128), unit)
            held[g, :, lanes] = (value * scale).astype(BF16)
        copy = pltpu.make_async_copy(
            held.at[g], out_ref.at[:, pl.ds(g * width, width)], sems.at[g]
        )
        copy.start()
        copies.append(copy)
    for copy in copies:
        copy.wait()


def swap(value, mask):
    devices = range(lax.axis_size(SEQ))
    return lax.ppermute(value, SEQ, [(i, i ^ mask) for i in devices])


def chip_route(count):
    route = {i: i + 1 for i in range(1, count - 1, 2)}
    route.update({i: i - 1 for i in range(4, count - 2, 2)})
    route.update({2: 0, 0: 1, count - 2: count - 1, count - 1: count - 3})
    return sorted(route.items())


def near(shape, dtype):
    return pltpu.VMEM(shape, dtype)


VMEM_SPEC = pl.BlockSpec(memory_space=pltpu.VMEM)
ANY_SPEC = pl.BlockSpec(memory_space=pl.ANY)


def plain_call(
    body, out_shape, *args, smem=(), far=(), after=(), mib=12, nbytes=2**20, scratch=(), out_specs=None
):
    return pl.pallas_call(
        body,
        out_shape=out_shape,
        in_specs=[pl.BlockSpec(memory_space=pltpu.SMEM)] * len(smem)
        + [ANY_SPEC] * len(far)
        + [VMEM_SPEC] * len(args) + [ANY_SPEC] * len(after),
        out_specs=out_specs or jax.tree.map(lambda _: VMEM_SPEC, out_shape),
        scratch_shapes=list(scratch),
        compiler_params=pltpu.CompilerParams(vmem_limit_bytes=mib * 2**20),
        cost_estimate=pl.CostEstimate(flops=0, bytes_accessed=nbytes, transcendentals=0),
    )(*smem, *[pltpu.with_memory_space_constraint(a, pltpu.HBM) for a in far], *args, *after)


def body(
    x_in,
    bc_in,
    z_in,
    dt_in,
    conv_weight,
    conv_bias,
    dt_bias,
    a_log,
    d_skip,
    norm_gain,
    conv_cache,
    cache_state,
    lengths,
):
    rows, inner = x_in.shape
    heads = dt_in.shape[1]
    head_dim = inner // heads
    devices = lax.axis_size(SEQ)
    index = lax.axis_index(SEQ)
    share = heads // devices
    steps = GROUPS // PAIR
    per_step = heads // steps
    width = inner // steps
    side = GROUPS * STATE
    unit = width // (2 * PAIR)
    unit_heads = unit // head_dim
    state_rows = steps * STATE
    msg_rows = state_rows + 16
    dma = pltpu.SemaphoreType.DMA

    fetched = [
        x_in,
        bc_in,
        conv_weight,
        conv_bias.reshape(1, -1),
        dt_in,
        dt_bias.reshape(1, -1),
        a_log.reshape(1, -1),
        norm_gain.reshape(1, -1),
    ]
    rim, *ready = plain_call(
        functools.partial(rim_kernel, count=len(fetched)),
        [near((RIM, inner + 2 * side), BF16)] + [near(a.shape, a.dtype) for a in fetched],
        far=fetched,
        mib=4,
        scratch=[
            pltpu.VMEM((TOP, inner), BF16),
            pltpu.VMEM((TOP, 2 * side), BF16),
            dma((2 + len(fetched),)),
        ],
    )
    near_rim = lax.ppermute(rim, SEQ, chip_route(devices))
    core_rim = swap(rim, 1)

    xc, bc, prex, preb, cum, step_size, dec, top, local = plain_call(
        functools.partial(conv_kernel, heads=heads, head_dim=head_dim),
        (
            near((rows, inner), BF16),
            near((rows, side), BF16),
            near((8, inner), F32),
            near((8, side), F32),
            near((rows, heads), F32),
            near((rows, heads), F32),
            near((2 * PAIR, 16, unit), BF16),
            near((8, inner), F32),
            near((GROUPS, STATE, width // PAIR), F32),
        ),
        *ready[:-1],
        smem=(lengths,),
        after=(rim,),
        scratch=[
            pltpu.VMEM((4, 8 + rows, 128), F32),
            pltpu.VMEM((2, rows, width), F32),
            pltpu.VMEM((2, rows, width), BF16),
        ],
        mib=16,
        nbytes=4 * 2**20,
    )

    pair_msg = near((PAIR, msg_rows, unit), BF16)
    send, keep, xfix, bfix = plain_call(
        fix_kernel,
        (pair_msg, pair_msg, near((TOP, inner), BF16), near((TOP, side), BF16)),
        near_rim,
        core_rim,
        conv_cache,
        ready[2],
        prex,
        preb,
        xc,
        bc,
        top,
        local,
        dec,
        scratch=[pltpu.VMEM((16, inner + side), F32)],
    )

    message = near((msg_rows, unit), BF16)
    part = swap(send, 1)
    send_y, own = plain_call(core_kernel, (message, message), keep, part)
    recv = swap(send_y, 2)
    chunks = 4
    cache = plain_call(
        functools.partial(cache_kernel, unit_heads=unit_heads),
        near((state_rows, unit), F32),
        far=(cache_state.transpose(1, 2, 0),),
        after=(own,),
        scratch=[
            pltpu.VMEM((head_dim, STATE, heads), F32),
            pltpu.VMEM((unit // 128, steps, STATE, 128), F32),
            dma((chunks,)),
        ],
        nbytes=2 * 2**20,
    )
    cc, log_cum, row, ecum = plain_call(
        side_kernel,
        (
            near((rows, side), BF16),
            near((rows, heads), F32),
            near((heads, rows), F32),
            near((steps, rows, 2 * per_step), BF16),
        ),
        ready[1],
        ready[2],
        ready[3],
        near_rim,
        core_rim,
        conv_cache,
        cum,
        step_size,
        after=(own,),
        scratch=[pltpu.VMEM((4, 8 + rows, 128), F32)],
    )
    total = plain_call(
        functools.partial(total_kernel, bit=2), message, own, recv, after=(cache, cc)
    )

    def diag_part(k, order):
        return plain_call(
            functools.partial(diag_kernel, head_dim=head_dim, first=k * GROUPS // 2),
            near((rows, inner // 2), F32),
            xc,
            xfix,
            bc,
            bfix,
            cc,
            log_cum,
            row,
            d_skip.reshape(1, -1),
            after=(order,),
            nbytes=4 * 2**20,
        )

    diags = [diag_part(0, total)]
    pre = None
    bit = 4
    pre_shape = (near((state_rows, unit), F32), near((8, unit), F32))
    while 2 * bit < devices:
        other = swap(total, 2 * bit - 4)
        if pre is None:
            total, *pre = plain_call(
                functools.partial(start_kernel, bit=bit),
                (message,) + pre_shape,
                total,
                other,
                after=(diags[0],),
            )
        else:
            total, *pre = plain_call(
                functools.partial(prefix_kernel, bit=bit), (message,) + pre_shape, total, other, *pre
            )
        bit *= 2
    if pre is None:
        pre = [jnp.zeros((state_rows, unit), F32), jnp.ones((8, unit), F32)]
    last = total
    other = swap(last, 2 * bit - 4)
    diags.append(diag_part(1, last))
    state_out = near((state_rows, unit), BF16)
    send_y, stay, final = plain_call(
        functools.partial(enter_kernel, bit=bit),
        (state_out, state_out, near((state_rows, unit), F32)),
        total,
        other,
        *pre,
        cache,
        own,
        recv,
        after=(diags[1],),
    )
    recv_y = swap(send_y, 2)
    grow, mine = plain_call(
        functools.partial(grow_kernel, head_dim=head_dim),
        (near((rows, inner), F32), jax.ShapeDtypeStruct((unit, STATE), F32)),
        ecum,
        final,
        nbytes=5 * 2**20,
    )
    gate = plain_call(
        gate_kernel, near((rows, inner), F32), z_in, smem=(lengths,), after=(final,)
    )
    half = near((PAIR, state_rows, unit), BF16)
    send_c = plain_call(chip_kernel, half, stay, recv_y, keep, part, after=(gate, grow))
    enter_recv = swap(send_c, 1)
    gain = ready[-1]
    gated_own, own_sums = plain_call(
        functools.partial(own_kernel, parts=len(diags)),
        (near((GROUPS, rows, unit), F32), near((GROUPS, rows, 128), F32)),
        *diags,
        gate,
        grow,
        cc,
        gain,
        stay,
        recv_y,
        keep,
        part,
        after=(send_c,),
        scratch=[pltpu.VMEM((PAIR, state_rows, unit), BF16)],
    )

    mixed = plain_call(
        functools.partial(out_kernel, parts=len(diags)),
        jax.ShapeDtypeStruct((rows, inner), BF16),
        *diags,
        gate,
        grow,
        cc,
        gated_own,
        own_sums,
        enter_recv,
        gain,
        out_specs=ANY_SPEC,
        scratch=[pltpu.VMEM((GROUPS, rows, 2 * unit), BF16), dma((GROUPS,))],
        mib=16,
        nbytes=4 * 2**20,
    )

    if share * head_dim == unit and devices == 2 * PAIR * steps:
        mine = mine.reshape(share, head_dim, STATE)
    else:
        around = [[4 * i + j for j in range(4)] for i in range(devices // 4)]
        every = final.reshape(steps, STATE, unit)
        every = lax.all_gather(every, SEQ, axis=1, axis_index_groups=around)
        every = every.reshape(steps * 2 * PAIR, STATE, unit).transpose(0, 2, 1)
        every = every.reshape(heads, head_dim, STATE)
        mine = lax.dynamic_slice_in_dim(every, index * share, share, 0)
    return (mixed, mine)


def solution(mesh):
    in_specs = (
        P(("groups", "seq"), None),
        P(("groups", "seq"), None),
        P(("groups", "seq"), None),
        P(("groups", "seq"), None),
        P(),
        P(),
        P(),
        P(),
        P(),
        P(),
        P("groups", None),
        P("groups", None, None),
        P("groups"),
    )
    out_specs = (P(("groups", "seq"), None), P(("groups", "seq"), None, None))
    return jax.shard_map(body, mesh=mesh, in_specs=in_specs, out_specs=out_specs, check_vma=False)
```

```python
import functools

import jax
import jax.numpy as jnp
from jax import lax
from jax.experimental import pallas as pl
from jax.experimental.pallas import tpu as pltpu
from jax.sharding import PartitionSpec as P

STATE = 64
GROUPS = 8
CONV_W = 4
RIM = CONV_W - 1
LOG2E = 1.4426950408889634
BF16 = jnp.bfloat16
F32 = jnp.float32
HI = lax.Precision.HIGHEST
SEQ = "seq"
PAIR = 2
TOP = 16


def silu(v):
    return silu_of_twice(0.5 * v)


def silu_of_twice(half):
    return half + half * jnp.tanh(half)


def split2(v):
    hi = v.astype(BF16)
    return hi, (v - hi.astype(F32)).astype(BF16)


def rim_kernel(*refs, count):
    x_ref, bc_ref = refs[:2]
    sources, out_ref, refs = refs[:count], refs[count], refs[count + 1 :]
    targets, (x_rows, bc_rows, sems) = refs[:count], refs[count:]
    rows, inner = x_ref.shape
    pairs = [
        (x_ref.at[pl.ds(rows - TOP, TOP), :], x_rows),
        (bc_ref.at[pl.ds(rows - TOP, TOP), :], bc_rows),
    ] + list(zip(sources, targets))
    copies = [pltpu.make_async_copy(a, b, sems.at[k]) for k, (a, b) in enumerate(pairs)]
    for copy in copies:
        copy.start()
    for copy in copies[:2]:
        copy.wait()
    out_ref[:, :inner] = x_rows[...].astype(F32)[TOP - RIM :, :].astype(BF16)
    out_ref[:, inner:] = bc_rows[...].astype(F32)[TOP - RIM :, :].astype(BF16)
    for copy in copies[2:]:
        copy.wait()


def pack_decay(dec):
    hi, lo = split2(dec)
    return jnp.concatenate([hi.astype(F32), lo.astype(F32)], axis=0).astype(BF16)


def unpack_decay(rows):
    both = rows.astype(F32)
    return both[0:8] + both[8:16]


def convolve(values, w_ref, bias_ref, first, ext, rows):
    cols = pl.ds(first, 128)
    ext[8:, :] = values.astype(F32)
    total = jnp.broadcast_to(0.5 * bias_ref[:, cols], (rows, 128))
    for k in range(CONV_W):
        total = total + ext[pl.ds(8 + k - RIM, rows), :] * (0.5 * w_ref[k : k + 1, cols])
    return total


def conv_kernel(
    len_ref,
    x_ref,
    bc_ref,
    w_ref,
    bias_ref,
    dt_ref,
    dtb_ref,
    alog_ref,
    after_ref,
    xo_ref,
    bo_ref,
    prex_ref,
    preb_ref,
    cum_ref,
    step_ref,
    dec_ref,
    top_ref,
    local_ref,
    ext,
    tails,
    scaled,
    *,
    heads,
    head_dim,
):
    _, rows, width = tails.shape
    side = bo_ref.shape[1]
    inner = x_ref.shape[1]
    steps = inner // width
    per_step = heads // steps
    spare = ext.shape[0]
    for k in range(spare):
        ext[k, 0:8, :] = jnp.zeros((8, 128), F32)

    raw = dt_ref[...].astype(F32) + dtb_ref[...]
    soft = jnp.maximum(raw, 0.0) + jnp.log1p(jnp.exp(-jnp.abs(raw)))
    token = lax.axis_index(SEQ) * rows + lax.broadcasted_iota(jnp.int32, (rows, heads), 0)
    dt = jnp.where(token < len_ref[0], soft, 0.0)
    step_ref[...] = dt
    rate = -jnp.exp(alog_ref[...]) * dt
    below = lax.broadcasted_iota(jnp.int32, (rows, rows), 0)
    across = lax.broadcasted_iota(jnp.int32, (rows, rows), 1)
    tri = jnp.where(below >= across, 1.0, 0.0).astype(BF16)
    hi, rest = split2(rate)
    mid, low = split2(rate - hi.astype(F32))
    sums = jnp.dot(tri, jnp.concatenate([hi, mid, low], axis=1), preferred_element_type=F32)
    cum = sums[:, :heads] + (sums[:, heads : 2 * heads] + sums[:, 2 * heads :])
    cum_ref[...] = cum

    for j in range(side // 128):
        cols = pl.ds(128 * j, 128)
        total = convolve(bc_ref[:, cols], w_ref, bias_ref, inner + 128 * j, ext.at[j % spare], rows)
        preb_ref[:, cols] = total[0:8]
        bo_ref[:, cols] = silu_of_twice(total).astype(BF16)

    last = cum[rows - 1 : rows, :]
    tail_hi, tail_lo = split2(jnp.exp(last - cum) * dt)
    unit_heads = per_step // (2 * PAIR)
    unit_cols = unit_heads * head_dim
    owner = lax.broadcasted_iota(jnp.int32, (8, heads), 0)
    head = lax.broadcasted_iota(jnp.int32, (8, heads), 1)
    dec_hi, dec_lo = split2(jnp.exp(last))
    chosen = jnp.concatenate(
        [jnp.where(head // per_step == owner, v.astype(F32), 0.0) for v in (dec_hi, dec_lo)], axis=0
    ).astype(BF16)
    head = lax.broadcasted_iota(jnp.int32, (heads, unit_cols), 0)
    lane = lax.broadcasted_iota(jnp.int32, (heads, unit_cols), 1)
    same = head % unit_heads == lane // head_dim
    for q in range(2 * PAIR):
        spread = jnp.where(same & ((head % per_step) // unit_heads == q), 1.0, 0.0).astype(BF16)
        dec_ref[q] = jnp.dot(chosen, spread, preferred_element_type=F32).astype(BF16)

    head = lax.broadcasted_iota(jnp.int32, (2 * per_step, width), 0) % per_step
    lane = lax.broadcasted_iota(jnp.int32, (2 * per_step, width), 1) // head_dim
    spread = jnp.where(head == lane, 1.0, 0.0).astype(BF16)

    def widen(i):
        part = slice(i * per_step, (i + 1) * per_step)
        both = jnp.concatenate([tail_hi[:, part], tail_lo[:, part]], axis=1)
        tails[i % 2] = jnp.dot(both, spread, preferred_element_type=F32)

    early = lax.broadcasted_iota(jnp.int32, (8, 128), 0) < RIM
    group = width // PAIR
    widen(0)
    for i in range(steps):
        if i + 1 < steps:
            widen(i + 1)
        for j in range(width // 128):
            cols, lanes = pl.ds(i * width + 128 * j, 128), slice(128 * j, 128 * (j + 1))
            total = convolve(
                x_ref[:, cols], w_ref, bias_ref, i * width + 128 * j, ext.at[j % spare], rows
            )
            prex_ref[:, cols] = total[0:8]
            xj = silu_of_twice(total).astype(BF16)
            xo_ref[:, cols] = xj
            tail = tails[i % 2, :, lanes]
            top_ref[:, cols] = jnp.where(early, tail[0:8], 0.0)
            tail = jnp.concatenate([jnp.where(early, 0.0, tail[0:8]), tail[8:]], axis=0)
            scaled[i % 2, :, lanes] = (xj.astype(F32) * tail).astype(BF16)
        b_turned = bo_ref[:, i * PAIR * STATE : (i + 1) * PAIR * STATE].T
        for y in range(PAIR):
            local_ref[PAIR * i + y] = jnp.dot(
                b_turned[y * STATE : (y + 1) * STATE, :],
                scaled[i % 2, :, y * group : (y + 1) * group],
                preferred_element_type=F32,
            )


def before_block(near_rim, core_rim, cache):
    device = lax.axis_index(SEQ)
    rim = jnp.where(device % 2 == 1, core_rim.astype(F32), near_rim.astype(F32))
    return jnp.where(device == 0, cache.astype(F32), rim)


def side_kernel(
    bc_ref,
    w_ref,
    bias_ref,
    near_ref,
    core_ref,
    cache_ref,
    cum_ref,
    step_ref,
    after_ref,
    co_ref,
    log_ref,
    row_ref,
    ecum_ref,
    ext,
):
    rows, heads = cum_ref.shape
    side = co_ref.shape[1]
    first = w_ref.shape[1] - side
    spare = ext.shape[0]
    for j in range(side // 128):
        cols = pl.ds(first + 128 * j, 128)
        ext[j % spare, 8 - RIM : 8, :] = before_block(
            near_ref[:, cols], core_ref[:, cols], cache_ref[:, cols]
        )
        values = bc_ref[:, pl.ds(side + 128 * j, 128)]
        total = convolve(values, w_ref, bias_ref, first + 128 * j, ext.at[j % spare], rows)
        co_ref[:, pl.ds(128 * j, 128)] = silu_of_twice(total).astype(BF16)
    cum, dt = cum_ref[...], step_ref[...]
    log_ref[...] = cum * LOG2E
    log_dt = jnp.where(dt > 0.0, jnp.log(jnp.maximum(dt, 1e-38)) * LOG2E, -1e30)
    row_ref[...] = (cum * LOG2E - log_dt).T
    ecum_hi, ecum_lo = split2(jnp.exp(cum))
    steps, _, twice = ecum_ref.shape
    for i in range(steps):
        part = slice(i * twice // 2, (i + 1) * twice // 2)
        ecum_ref[i] = jnp.concatenate([ecum_hi[:, part], ecum_lo[:, part]], axis=1)


def fix_kernel(
    near_ref,
    core_ref,
    cache_ref,
    w_ref,
    prex_ref,
    preb_ref,
    xc_ref,
    bc_ref,
    top_ref,
    local_ref,
    dec_ref,
    far_ref,
    near_out_ref,
    keep_ref,
    xfix_ref,
    bfix_ref,
    ext,
):
    device = lax.axis_index(SEQ)
    core = device % 2
    inner = xc_ref.shape[1]
    side = bc_ref.shape[1]
    ext[8:, :] = jnp.zeros((8, ext.shape[1]), F32)
    cols = pl.ds(0, ext.shape[1])
    ext[8 - RIM : 8, :] = before_block(near_ref[:, cols], core_ref[:, cols], cache_ref[:, cols])

    def fix(pre, old, dst, first, count):
        cols = pl.ds(first, count)
        total = pre[...]
        for k in range(RIM):
            total = total + ext[pl.ds(8 - RIM + k, 8), cols] * (0.5 * w_ref[k : k + 1, cols])
        fixed = silu_of_twice(total)
        dst[...] = jnp.concatenate([fixed, old[0:TOP, :].astype(F32)[8:, :]], axis=0).astype(BF16)
        return fixed.astype(BF16).astype(F32)

    x_top = fix(prex_ref, xc_ref, xfix_ref, 0, inner)
    b_top = fix(preb_ref, bc_ref, bfix_ref, inner, side)
    scaled = x_top * top_ref[...]
    scaled = jnp.concatenate([scaled, jnp.zeros_like(scaled)], axis=0).astype(BF16)
    b_top = jnp.concatenate([b_top, jnp.zeros_like(b_top)], axis=0)
    b_turned = b_top.T.astype(BF16)
    groups, _, width = local_ref.shape
    unit = width // 2
    side_bit = (device // 2) % 2
    for i in range(groups // PAIR):
        where = pl.ds(i * STATE, STATE)
        sends = []
        for y in range(PAIR):
            g = PAIR * i + y
            extra = jnp.dot(
                b_turned[g * STATE : (g + 1) * STATE, :],
                scaled[:, g * width : (g + 1) * width],
                preferred_element_type=F32,
            )
            whole_state = local_ref[g] + extra
            low, high = whole_state[:, :unit], whole_state[:, unit:]
            sends.append(jnp.where(core == 0, high, low))
            keep_ref[y, where, :] = jnp.where(core == 0, low, high).astype(BF16)
        far_ref[where, :] = jnp.where(side_bit == 0, sends[1], sends[0]).astype(BF16)
        near_out_ref[where, :] = jnp.where(side_bit == 0, sends[0], sends[1]).astype(BF16)
    where = pl.ds(groups // PAIR * STATE, 16)
    far_ref[where, :] = dec_ref[2 * (1 - side_bit) + 1 - core]
    near_out_ref[where, :] = dec_ref[2 * side_bit + 1 - core]
    for y in range(PAIR):
        keep_ref[y, where, :] = dec_ref[2 * y + core]


def cache_kernel(state_hbm, after_ref, out_ref, state_ref, held, sems, *, unit_heads):
    channels, size, heads = state_hbm.shape
    chunks = sems.shape[0]
    count = channels // chunks
    copies = []
    for c in range(chunks):
        part = pl.ds(c * count, count)
        copies.append(pltpu.make_async_copy(state_hbm.at[part], state_ref.at[part], sems.at[c]))
        copies[c].start()
    per_tile = 128 // unit_heads
    quarters = 2 * PAIR
    steps = heads // (quarters * unit_heads)
    quarter = lax.axis_index(SEQ) % quarters
    lane = lax.broadcasted_iota(jnp.int32, (size, 128), 1) // unit_heads
    for channel in range(channels):
        if channel % count == 0:
            copies[channel // count].wait()
        tile, place = channel // per_tile, channel % per_tile
        value = state_ref[channel]
        for i in range(steps):
            start = (i * quarters + quarter) * unit_heads
            moved = pltpu.roll(value, (place * unit_heads - start + heads) % heads, axis=1)
            if place == 0:
                held[tile, i] = moved
            else:
                held[tile, i] = jnp.where(lane == place, moved, held[tile, i])
    unit = out_ref.shape[1]
    dim = unit // unit_heads
    source = lax.broadcasted_iota(jnp.int32, (unit, unit), 0)
    target = lax.broadcasted_iota(jnp.int32, (unit, unit), 1)
    chosen = source == (target % dim) * unit_heads + target // dim
    order = jnp.where(chosen, 1.0, 0.0).astype(BF16)
    for i in range(steps):
        value = jnp.concatenate([held[t, i] for t in range(unit // 128)], axis=1)
        hi = value.astype(BF16)
        rest = value - hi.astype(F32)
        mid = rest.astype(BF16)
        low = (rest - mid.astype(F32)).astype(BF16)
        parts = jnp.dot(
            jnp.concatenate([hi, mid, low], axis=0), order, preferred_element_type=F32
        )
        out_ref[i * size : (i + 1) * size, :] = (
            parts[:size] + parts[size : 2 * size] + parts[2 * size :]
        )


def blocks_of(rows):
    return [(i, slice(i * STATE, (i + 1) * STATE)) for i in range(rows // STATE)]


def core_kernel(keep_ref, recv_ref, *rest, own):
    device = lax.axis_index(SEQ)
    core, side = device % 2, (device // 2) % 2
    out_ref = rest[-1]
    pick = side if own else 1 - side
    join_totals(keep_ref.at[pick], recv_ref, core == 0, out_ref, recv_ref.shape[0] - 16)


def join_totals(mine, other, mine_first, out, rows):
    d_mine = unpack_decay(mine[rows:, :])
    d_other = unpack_decay(other[rows:, :])
    d_later = jnp.where(mine_first, d_other, d_mine)
    f_mine = jnp.where(mine_first, d_later, 1.0)
    f_other = jnp.where(mine_first, 1.0, d_later)
    for i, part in blocks_of(rows):
        total = mine[part, :].astype(F32) * f_mine[i : i + 1] + other[part, :].astype(F32) * f_other[
            i : i + 1
        ]
        out[part, :] = total.astype(BF16)
    out[rows:, :] = pack_decay(d_mine * d_other)


def total_kernel(mine_ref, other_ref, cache_ref, c_ref, out_ref, *, bit):
    device = lax.axis_index(SEQ)
    rows = mine_ref.shape[0] - 16
    join_totals(mine_ref, other_ref, (device // bit) % 2 == 0, out_ref, rows)


def prefix_kernel(mine_ref, other_ref, pre_ref, dpre_ref, out_ref, opre_ref, odpre_ref, *, bit):
    device = lax.axis_index(SEQ)
    rows = mine_ref.shape[0] - 16
    first = (device // bit) % 2 == 0
    join_totals(mine_ref, other_ref, first, out_ref, rows)
    d_other = unpack_decay(other_ref[rows:, :])
    d_pre = dpre_ref[...]
    gain = jnp.where(first, 0.0, d_pre)
    for i, part in blocks_of(rows):
        opre_ref[part, :] = pre_ref[part, :] + gain[i : i + 1] * other_ref[part, :].astype(F32)
    odpre_ref[...] = jnp.where(first, d_pre, d_pre * d_other)


def start_kernel(mine_ref, other_ref, after_ref, out_ref, opre_ref, odpre_ref, *, bit):
    device = lax.axis_index(SEQ)
    rows = mine_ref.shape[0] - 16
    first = (device // bit) % 2 == 0
    join_totals(mine_ref, other_ref, first, out_ref, rows)
    d_other = unpack_decay(other_ref[rows:, :])
    opre_ref[...] = jnp.where(first, 0.0, other_ref[:rows, :].astype(F32))
    odpre_ref[...] = jnp.where(first, 1.0, d_other)


def enter_kernel(
    mine_ref,
    other_ref,
    pre_ref,
    dpre_ref,
    cache_ref,
    own_ref,
    recv_ref,
    after_ref,
    send_ref,
    stay_ref,
    fin_ref,
    *,
    bit,
):
    device = lax.axis_index(SEQ)
    side = (device // 2) % 2
    rows = mine_ref.shape[0] - 16
    first = (device // bit) % 2 == 0
    d_mine = unpack_decay(mine_ref[rows:, :])
    d_other = unpack_decay(other_ref[rows:, :])
    d_later = jnp.where(first, d_other, d_mine)
    f_mine = jnp.where(first, d_later, 1.0)
    f_other = jnp.where(first, 1.0, d_later)
    d_all = d_mine * d_other
    d_pre = dpre_ref[...]
    gain = jnp.where(first, 0.0, d_pre)
    d_before = jnp.where(first, d_pre, d_pre * d_other)
    d_first = jnp.where(side == 0, unpack_decay(own_ref[rows:, :]), unpack_decay(recv_ref[rows:, :]))
    for i, part in blocks_of(rows):
        cache = cache_ref[part, :]
        other = other_ref[part, :].astype(F32)
        mine = mine_ref[part, :].astype(F32)
        row = slice(i, i + 1)
        fin_ref[part, :] = d_all[row] * cache + mine * f_mine[row] + other * f_other[row]
        plane = d_before[row] * cache + pre_ref[part, :] + gain[row] * other
        t_first = jnp.where(side == 0, own_ref[part, :].astype(F32), recv_ref[part, :].astype(F32))
        second = d_first[row] * plane + t_first
        send_ref[part, :] = jnp.where(side == 0, second, plane).astype(BF16)
        stay_ref[part, :] = jnp.where(side == 0, plane, second).astype(BF16)


def chip_kernel(stay_ref, recv_ref, keep_ref, far_ref, near_ref, gate_ref, grow_ref, send_ref):
    parts = (far_ref, near_ref)
    enter_block(stay_ref, recv_ref, keep_ref, parts, send_ref, lax.axis_index(SEQ) % 2 == 1)


def enter_block(stay_ref, recv_ref, keep_ref, parts, out_ref, first):
    device = lax.axis_index(SEQ)
    core, side = device % 2, (device // 2) % 2
    rows = stay_ref.shape[0]

    def fill(values):
        for y in range(PAIR):
            for mine, source in ((True, stay_ref), (False, recv_ref)):

                @pl.when((side == y) == mine)
                def _(y=y, source=source, mine=mine):
                    values(y, source, mine)

    @pl.when(first)
    def _():
        def values(y, source, mine):
            out_ref[y] = source[...]

        fill(values)

    for kept in range(2):

        @pl.when(jnp.logical_not(first) & (core == kept))
        def _(kept=kept):
            def values(y, source, mine):
                local = parts[mine] if kept else keep_ref.at[y]
                decay = unpack_decay(local[rows:, :])
                for i, part in blocks_of(rows):
                    entered = decay[i : i + 1] * source[part, :].astype(F32)
                    out_ref[y, part, :] = (entered + local[part, :].astype(F32)).astype(BF16)

            fill(values)


def diag_kernel(
    xc_ref,
    xfix_ref,
    b_ref,
    bfix_ref,
    c_ref,
    cum_ref,
    row_ref,
    skip_ref,
    after_ref,
    out_ref,
    *,
    head_dim,
    first,
):
    rows = xc_ref.shape[0]
    heads = cum_ref.shape[1]
    per_group = heads // GROUPS
    below = lax.broadcasted_iota(jnp.int32, (rows, rows), 0)
    across = lax.broadcasted_iota(jnp.int32, (rows, rows), 1)
    mask = below >= across
    quad = 128 // head_dim
    lane = lax.broadcasted_iota(jnp.int32, (rows, 128), 1) // head_dim
    for g in range(out_ref.shape[1] // (per_group * head_dim)):
        part = slice((first + g) * STATE, (first + g + 1) * STATE)
        b_all = jnp.concatenate([bfix_ref[:, part], b_ref[TOP:, part]], axis=0)
        c_dot_b = lax.dot_general(
            c_ref[:, part], b_all, (((1,), (1,)), ((), ())), preferred_element_type=F32
        )
        for q in range(per_group // quad):
            base = (first + g) * per_group + q * quad
            cols = pl.ds(base * head_dim, 128)
            x_quad = jnp.concatenate([xfix_ref[:, cols], xc_ref[TOP:, cols]], axis=0)
            lhs, rhs = [], []
            for k in range(quad):
                head = base + k
                gap = cum_ref[:, head : head + 1] - row_ref[head : head + 1, :]
                decay = jnp.exp2(jnp.where(mask, gap, -1e30))
                lhs.append((c_dot_b * decay).astype(BF16))
                rhs.append(jnp.where(lane == k, x_quad, jnp.zeros_like(x_quad)))
            skip = skip_ref[:, base : base + 1]
            for k in range(1, quad):
                skip = jnp.where(lane[0:1] == k, skip_ref[:, base + k : base + k + 1], skip)
            inner = jnp.dot(
                jnp.concatenate(lhs, axis=1),
                jnp.concatenate(rhs, axis=0),
                preferred_element_type=F32,
            )
            out = pl.ds((g * per_group + q * quad) * head_dim, 128)
            out_ref[:, out] = inner + skip * x_quad.astype(F32)


def gate_kernel(len_ref, z_ref, after_ref, gate_ref):
    rows, width = z_ref.shape
    first = lax.axis_index(SEQ) * rows
    live = first + lax.broadcasted_iota(jnp.int32, (rows, 128), 0) < len_ref[0]
    for j in range(width // 128):
        cols = pl.ds(128 * j, 128)
        gate_ref[:, cols] = jnp.where(live, silu(z_ref[:, cols].astype(F32)), 0.0)


def grow_kernel(ecum_ref, final_ref, grow_ref, mine_ref, *, head_dim):
    steps = ecum_ref.shape[0]
    per_step = ecum_ref.shape[2] // 2
    width = per_step * head_dim
    head = lax.broadcasted_iota(jnp.int32, (2 * per_step, width), 0) % per_step
    lane = lax.broadcasted_iota(jnp.int32, (2 * per_step, width), 1)
    spread = jnp.where(head == lane // head_dim, 1.0, 0.0).astype(BF16)
    for i in range(steps):
        grow_ref[:, i * width : (i + 1) * width] = jnp.dot(
            ecum_ref[i], spread, preferred_element_type=F32
        )
    step = (lax.axis_index(SEQ) // (2 * PAIR)) % (final_ref.shape[0] // STATE)
    mine = final_ref[pl.ds(pl.multiple_of(step * STATE, STATE), STATE), :]
    mine_ref[...] = mine.T


def gated_part(parts, gate_ref, grow_ref, c_ref, state, group, half):
    width = gate_ref.shape[1] // GROUPS
    unit = width // 2
    per_part = GROUPS // len(parts)
    inside = pl.ds(pl.multiple_of((group % per_part) * width + half * unit, 128), unit)
    cols = pl.ds(pl.multiple_of(group * width + half * unit, 128), unit)
    entering = jnp.dot(
        c_ref[:, group * STATE : (group + 1) * STATE], state, preferred_element_type=F32
    )
    y_all = parts[group // per_part][:, inside] + grow_ref[:, cols] * entering
    return y_all.astype(BF16).astype(F32) * gate_ref[:, cols], cols


def sum_lanes(value):
    return sum(value[:, j : j + 128] for j in range(0, value.shape[1], 128))


def own_kernel(*refs, parts):
    diag_refs, refs = refs[:parts], refs[parts:]
    gate_ref, grow_ref, c_ref, gain_ref, stay_ref, recv_ref, keep_ref, *parts_in = refs[:9]
    out_ref, sums_ref, own_ref = refs[10:]
    core = lax.axis_index(SEQ) % 2
    enter_block(stay_ref, recv_ref, keep_ref, parts_in, own_ref, core == 0)
    for g in range(GROUPS):
        i, y = g // PAIR, g % PAIR
        state = own_ref[y, i * STATE : (i + 1) * STATE, :]
        gated, cols = gated_part(diag_refs, gate_ref, grow_ref, c_ref, state, g, core)
        sums_ref[g] = sum_lanes(gated * gated)
        out_ref[g] = gated * gain_ref[:, cols]


def out_kernel(*refs, parts):
    diag_refs, refs = refs[:parts], refs[parts:]
    gate_ref, grow_ref, c_ref, own_ref, sums_ref, recv_ref, gain_ref, out_ref, held, sems = refs
    core = lax.axis_index(SEQ) % 2
    unit = own_ref.shape[2]
    width = 2 * unit
    copies = []
    for g in range(GROUPS):
        i, y = g // PAIR, g % PAIR
        state = recv_ref[y, i * STATE : (i + 1) * STATE, :]
        other, cols = gated_part(diag_refs, gate_ref, grow_ref, c_ref, state, g, 1 - core)
        squares = jnp.sum(sums_ref[g] + sum_lanes(other * other), axis=1, keepdims=True)
        scale = lax.rsqrt(squares * (1.0 / width) + 1e-05)
        for half, value in ((core, own_ref[g]), (1 - core, other * gain_ref[:, cols])):
            lanes = pl.ds(pl.multiple_of(half * unit, 128), unit)
            held[g, :, lanes] = (value * scale).astype(BF16)
        copy = pltpu.make_async_copy(
            held.at[g], out_ref.at[:, pl.ds(g * width, width)], sems.at[g]
        )
        copy.start()
        copies.append(copy)
    for copy in copies:
        copy.wait()


def swap(value, mask):
    devices = range(lax.axis_size(SEQ))
    return lax.ppermute(value, SEQ, [(i, i ^ mask) for i in devices])


def chip_route(count):
    route = {i: i + 1 for i in range(1, count - 1, 2)}
    route.update({i: i - 1 for i in range(4, count - 2, 2)})
    route.update({2: 0, 0: 1, count - 2: count - 1, count - 1: count - 3})
    return sorted(route.items())


def near(shape, dtype):
    return pltpu.VMEM(shape, dtype)


VMEM_SPEC = pl.BlockSpec(memory_space=pltpu.VMEM)
ANY_SPEC = pl.BlockSpec(memory_space=pl.ANY)


def plain_call(
    body, out_shape, *args, smem=(), far=(), after=(), mib=12, nbytes=2**20, scratch=(), out_specs=None
):
    return pl.pallas_call(
        body,
        out_shape=out_shape,
        in_specs=[pl.BlockSpec(memory_space=pltpu.SMEM)] * len(smem)
        + [ANY_SPEC] * len(far)
        + [VMEM_SPEC] * len(args) + [ANY_SPEC] * len(after),
        out_specs=out_specs or jax.tree.map(lambda _: VMEM_SPEC, out_shape),
        scratch_shapes=list(scratch),
        compiler_params=pltpu.CompilerParams(vmem_limit_bytes=mib * 2**20),
        cost_estimate=pl.CostEstimate(flops=0, bytes_accessed=nbytes, transcendentals=0),
    )(*smem, *[pltpu.with_memory_space_constraint(a, pltpu.HBM) for a in far], *args, *after)


def body(
    x_in,
    bc_in,
    z_in,
    dt_in,
    conv_weight,
    conv_bias,
    dt_bias,
    a_log,
    d_skip,
    norm_gain,
    conv_cache,
    cache_state,
    lengths,
):
    rows, inner = x_in.shape
    heads = dt_in.shape[1]
    head_dim = inner // heads
    devices = lax.axis_size(SEQ)
    index = lax.axis_index(SEQ)
    share = heads // devices
    steps = GROUPS // PAIR
    per_step = heads // steps
    width = inner // steps
    side = GROUPS * STATE
    unit = width // (2 * PAIR)
    unit_heads = unit // head_dim
    state_rows = steps * STATE
    msg_rows = state_rows + 16
    dma = pltpu.SemaphoreType.DMA

    fetched = [
        x_in,
        bc_in,
        conv_weight,
        conv_bias.reshape(1, -1),
        dt_in,
        dt_bias.reshape(1, -1),
        a_log.reshape(1, -1),
        norm_gain.reshape(1, -1),
    ]
    rim, *ready = plain_call(
        functools.partial(rim_kernel, count=len(fetched)),
        [near((RIM, inner + 2 * side), BF16)] + [near(a.shape, a.dtype) for a in fetched],
        far=fetched,
        mib=4,
        scratch=[
            pltpu.VMEM((TOP, inner), BF16),
            pltpu.VMEM((TOP, 2 * side), BF16),
            dma((2 + len(fetched),)),
        ],
    )
    near_rim = lax.ppermute(rim, SEQ, chip_route(devices))
    core_rim = swap(rim, 1)

    xc, bc, prex, preb, cum, step_size, dec, top, local = plain_call(
        functools.partial(conv_kernel, heads=heads, head_dim=head_dim),
        (
            near((rows, inner), BF16),
            near((rows, side), BF16),
            near((8, inner), F32),
            near((8, side), F32),
            near((rows, heads), F32),
            near((rows, heads), F32),
            near((2 * PAIR, 16, unit), BF16),
            near((8, inner), F32),
            near((GROUPS, STATE, width // PAIR), F32),
        ),
        *ready[:-1],
        smem=(lengths,),
        after=(rim,),
        scratch=[
            pltpu.VMEM((4, 8 + rows, 128), F32),
            pltpu.VMEM((2, rows, width), F32),
            pltpu.VMEM((2, rows, width), BF16),
        ],
        mib=16,
        nbytes=4 * 2**20,
    )

    pair_msg = near((PAIR, msg_rows, unit), BF16)
    message = near((msg_rows, unit), BF16)
    send_far, send_near, keep, xfix, bfix = plain_call(
        fix_kernel,
        (message, message, pair_msg, near((TOP, inner), BF16), near((TOP, side), BF16)),
        near_rim,
        core_rim,
        conv_cache,
        ready[2],
        prex,
        preb,
        xc,
        bc,
        top,
        local,
        dec,
        scratch=[pltpu.VMEM((16, inner + side), F32)],
    )

    part_far = swap(send_far, 1)
    part_near = swap(send_near, 1)
    send_y = plain_call(functools.partial(core_kernel, own=False), message, keep, part_far)
    recv = swap(send_y, 2)
    own = plain_call(
        functools.partial(core_kernel, own=True), message, keep, part_near, after=(send_y,)
    )
    chunks = 4
    cache = plain_call(
        functools.partial(cache_kernel, unit_heads=unit_heads),
        near((state_rows, unit), F32),
        far=(cache_state.transpose(1, 2, 0),),
        after=(own,),
        scratch=[
            pltpu.VMEM((head_dim, STATE, heads), F32),
            pltpu.VMEM((unit // 128, steps, STATE, 128), F32),
            dma((chunks,)),
        ],
        nbytes=2 * 2**20,
    )
    cc, log_cum, row, ecum = plain_call(
        side_kernel,
        (
            near((rows, side), BF16),
            near((rows, heads), F32),
            near((heads, rows), F32),
            near((steps, rows, 2 * per_step), BF16),
        ),
        ready[1],
        ready[2],
        ready[3],
        near_rim,
        core_rim,
        conv_cache,
        cum,
        step_size,
        after=(own,),
        scratch=[pltpu.VMEM((4, 8 + rows, 128), F32)],
    )
    total = plain_call(
        functools.partial(total_kernel, bit=2), message, own, recv, after=(cache, cc)
    )

    def diag_part(k, order):
        return plain_call(
            functools.partial(diag_kernel, head_dim=head_dim, first=k * GROUPS // 2),
            near((rows, inner // 2), F32),
            xc,
            xfix,
            bc,
            bfix,
            cc,
            log_cum,
            row,
            d_skip.reshape(1, -1),
            after=(order,),
            nbytes=4 * 2**20,
        )

    diags = [diag_part(0, total)]
    pre = None
    bit = 4
    pre_shape = (near((state_rows, unit), F32), near((8, unit), F32))
    while 2 * bit < devices:
        other = swap(total, 2 * bit - 4)
        if pre is None:
            total, *pre = plain_call(
                functools.partial(start_kernel, bit=bit),
                (message,) + pre_shape,
                total,
                other,
                after=(diags[0],),
            )
        else:
            total, *pre = plain_call(
                functools.partial(prefix_kernel, bit=bit), (message,) + pre_shape, total, other, *pre
            )
        bit *= 2
    if pre is None:
        pre = [jnp.zeros((state_rows, unit), F32), jnp.ones((8, unit), F32)]
    last = total
    other = swap(last, 2 * bit - 4)
    diags.append(diag_part(1, last))
    state_out = near((state_rows, unit), BF16)
    send_y, stay, final = plain_call(
        functools.partial(enter_kernel, bit=bit),
        (state_out, state_out, near((state_rows, unit), F32)),
        total,
        other,
        *pre,
        cache,
        own,
        recv,
        after=(diags[1],),
    )
    recv_y = swap(send_y, 2)
    grow, mine = plain_call(
        functools.partial(grow_kernel, head_dim=head_dim),
        (near((rows, inner), F32), jax.ShapeDtypeStruct((unit, STATE), F32)),
        ecum,
        final,
        nbytes=5 * 2**20,
    )
    gate = plain_call(
        gate_kernel, near((rows, inner), F32), z_in, smem=(lengths,), after=(final,)
    )
    half = near((PAIR, state_rows, unit), BF16)
    send_c = plain_call(chip_kernel, half, stay, recv_y, keep, part_far, part_near, after=(gate, grow))
    enter_recv = swap(send_c, 1)
    gain = ready[-1]
    gated_own, own_sums = plain_call(
        functools.partial(own_kernel, parts=len(diags)),
        (near((GROUPS, rows, unit), F32), near((GROUPS, rows, 128), F32)),
        *diags,
        gate,
        grow,
        cc,
        gain,
        stay,
        recv_y,
        keep,
        part_far,
        part_near,
        after=(send_c,),
        scratch=[pltpu.VMEM((PAIR, state_rows, unit), BF16)],
    )

    mixed = plain_call(
        functools.partial(out_kernel, parts=len(diags)),
        jax.ShapeDtypeStruct((rows, inner), BF16),
        *diags,
        gate,
        grow,
        cc,
        gated_own,
        own_sums,
        enter_recv,
        gain,
        out_specs=ANY_SPEC,
        scratch=[pltpu.VMEM((GROUPS, rows, 2 * unit), BF16), dma((GROUPS,))],
        mib=16,
        nbytes=4 * 2**20,
    )

    if share * head_dim == unit and devices == 2 * PAIR * steps:
        mine = mine.reshape(share, head_dim, STATE)
    else:
        around = [[4 * i + j for j in range(4)] for i in range(devices // 4)]
        every = final.reshape(steps, STATE, unit)
        every = lax.all_gather(every, SEQ, axis=1, axis_index_groups=around)
        every = every.reshape(steps * 2 * PAIR, STATE, unit).transpose(0, 2, 1)
        every = every.reshape(heads, head_dim, STATE)
        mine = lax.dynamic_slice_in_dim(every, index * share, share, 0)
    return (mixed, mine)


def solution(mesh):
    in_specs = (
        P(("groups", "seq"), None),
        P(("groups", "seq"), None),
        P(("groups", "seq"), None),
        P(("groups", "seq"), None),
        P(),
        P(),
        P(),
        P(),
        P(),
        P(),
        P("groups", None),
        P("groups", None, None),
        P("groups"),
    )
    out_specs = (P(("groups", "seq"), None), P(("groups", "seq"), None, None))
    return jax.shard_map(body, mesh=mesh, in_specs=in_specs, out_specs=out_specs, check_vma=False)
```

```python
import functools

import jax
import jax.numpy as jnp
from jax import lax
from jax.experimental import pallas as pl
from jax.experimental.pallas import tpu as pltpu
from jax.sharding import PartitionSpec as P

STATE = 64
GROUPS = 8
CONV_W = 4
RIM = CONV_W - 1
LOG2E = 1.4426950408889634
BF16 = jnp.bfloat16
F32 = jnp.float32
HI = lax.Precision.HIGHEST
SEQ = "seq"
PAIR = 2
TOP = 16


def silu(v):
    return silu_of_twice(0.5 * v)


def silu_of_twice(half):
    return half + half * jnp.tanh(half)


def split2(v):
    hi = v.astype(BF16)
    return hi, (v - hi.astype(F32)).astype(BF16)


def rim_kernel(*refs, count):
    x_ref, bc_ref = refs[:2]
    sources, out_ref, refs = refs[:count], refs[count], refs[count + 1 :]
    targets, (x_rows, bc_rows, sems) = refs[:count], refs[count:]
    rows, inner = x_ref.shape
    pairs = [
        (x_ref.at[pl.ds(rows - TOP, TOP), :], x_rows),
        (bc_ref.at[pl.ds(rows - TOP, TOP), :], bc_rows),
    ] + list(zip(sources, targets))
    copies = [pltpu.make_async_copy(a, b, sems.at[k]) for k, (a, b) in enumerate(pairs)]
    for copy in copies:
        copy.start()
    for copy in copies[:2]:
        copy.wait()
    out_ref[:, :inner] = x_rows[...].astype(F32)[TOP - RIM :, :].astype(BF16)
    out_ref[:, inner:] = bc_rows[...].astype(F32)[TOP - RIM :, :].astype(BF16)
    for copy in copies[2:]:
        copy.wait()


def pack_decay(dec):
    hi, lo = split2(dec)
    return jnp.concatenate([hi.astype(F32), lo.astype(F32)], axis=0).astype(BF16)


def unpack_decay(rows):
    both = rows.astype(F32)
    return both[0:8] + both[8:16]


def convolve(values, w_ref, bias_ref, first, ext, rows):
    cols = pl.ds(first, 128)
    ext[8:, :] = values.astype(F32)
    total = jnp.broadcast_to(0.5 * bias_ref[:, cols], (rows, 128))
    for k in range(CONV_W):
        total = total + ext[pl.ds(8 + k - RIM, rows), :] * (0.5 * w_ref[k : k + 1, cols])
    return total


def conv_kernel(
    len_ref,
    x_ref,
    bc_ref,
    w_ref,
    bias_ref,
    dt_ref,
    dtb_ref,
    alog_ref,
    after_ref,
    xo_ref,
    bo_ref,
    prex_ref,
    preb_ref,
    cum_ref,
    step_ref,
    dec_ref,
    top_ref,
    local_ref,
    ext,
    tails,
    scaled,
    *,
    heads,
    head_dim,
):
    _, rows, width = tails.shape
    side = bo_ref.shape[1]
    inner = x_ref.shape[1]
    steps = inner // width
    per_step = heads // steps
    spare = ext.shape[0]
    for k in range(spare):
        ext[k, 0:8, :] = jnp.zeros((8, 128), F32)

    raw = dt_ref[...].astype(F32) + dtb_ref[...]
    soft = jnp.maximum(raw, 0.0) + jnp.log1p(jnp.exp(-jnp.abs(raw)))
    token = lax.axis_index(SEQ) * rows + lax.broadcasted_iota(jnp.int32, (rows, heads), 0)
    dt = jnp.where(token < len_ref[0], soft, 0.0)
    step_ref[...] = dt
    rate = -jnp.exp(alog_ref[...]) * dt
    below = lax.broadcasted_iota(jnp.int32, (rows, rows), 0)
    across = lax.broadcasted_iota(jnp.int32, (rows, rows), 1)
    tri = jnp.where(below >= across, 1.0, 0.0).astype(BF16)
    hi, rest = split2(rate)
    mid, low = split2(rate - hi.astype(F32))
    sums = jnp.dot(tri, jnp.concatenate([hi, mid, low], axis=1), preferred_element_type=F32)
    cum = sums[:, :heads] + (sums[:, heads : 2 * heads] + sums[:, 2 * heads :])
    cum_ref[...] = cum

    for j in range(side // 128):
        cols = pl.ds(128 * j, 128)
        total = convolve(bc_ref[:, cols], w_ref, bias_ref, inner + 128 * j, ext.at[j % spare], rows)
        preb_ref[:, cols] = total[0:8]
        bo_ref[:, cols] = silu_of_twice(total).astype(BF16)

    last = cum[rows - 1 : rows, :]
    tail_hi, tail_lo = split2(jnp.exp(last - cum) * dt)
    unit_heads = per_step // (2 * PAIR)
    unit_cols = unit_heads * head_dim
    owner = lax.broadcasted_iota(jnp.int32, (8, heads), 0)
    head = lax.broadcasted_iota(jnp.int32, (8, heads), 1)
    dec_hi, dec_lo = split2(jnp.exp(last))
    chosen = jnp.concatenate(
        [jnp.where(head // per_step == owner, v.astype(F32), 0.0) for v in (dec_hi, dec_lo)], axis=0
    ).astype(BF16)
    head = lax.broadcasted_iota(jnp.int32, (heads, unit_cols), 0)
    lane = lax.broadcasted_iota(jnp.int32, (heads, unit_cols), 1)
    same = head % unit_heads == lane // head_dim
    for q in range(2 * PAIR):
        spread = jnp.where(same & ((head % per_step) // unit_heads == q), 1.0, 0.0).astype(BF16)
        dec_ref[q] = jnp.dot(chosen, spread, preferred_element_type=F32).astype(BF16)

    head = lax.broadcasted_iota(jnp.int32, (2 * per_step, width), 0) % per_step
    lane = lax.broadcasted_iota(jnp.int32, (2 * per_step, width), 1) // head_dim
    spread = jnp.where(head == lane, 1.0, 0.0).astype(BF16)

    def widen(i):
        part = slice(i * per_step, (i + 1) * per_step)
        both = jnp.concatenate([tail_hi[:, part], tail_lo[:, part]], axis=1)
        tails[i % 2] = jnp.dot(both, spread, preferred_element_type=F32)

    early = lax.broadcasted_iota(jnp.int32, (8, 128), 0) < RIM
    group = width // PAIR
    widen(0)
    for i in range(steps):
        if i + 1 < steps:
            widen(i + 1)
        for j in range(width // 128):
            cols, lanes = pl.ds(i * width + 128 * j, 128), slice(128 * j, 128 * (j + 1))
            total = convolve(
                x_ref[:, cols], w_ref, bias_ref, i * width + 128 * j, ext.at[j % spare], rows
            )
            prex_ref[:, cols] = total[0:8]
            xj = silu_of_twice(total).astype(BF16)
            xo_ref[:, cols] = xj
            tail = tails[i % 2, :, lanes]
            top_ref[:, cols] = jnp.where(early, tail[0:8], 0.0)
            tail = jnp.concatenate([jnp.where(early, 0.0, tail[0:8]), tail[8:]], axis=0)
            scaled[i % 2, :, lanes] = (xj.astype(F32) * tail).astype(BF16)
        b_turned = bo_ref[:, i * PAIR * STATE : (i + 1) * PAIR * STATE].T
        for y in range(PAIR):
            local_ref[PAIR * i + y] = jnp.dot(
                b_turned[y * STATE : (y + 1) * STATE, :],
                scaled[i % 2, :, y * group : (y + 1) * group],
                preferred_element_type=F32,
            )


def before_block(near_rim, core_rim, cache):
    device = lax.axis_index(SEQ)
    rim = jnp.where(device % 2 == 1, core_rim.astype(F32), near_rim.astype(F32))
    return jnp.where(device == 0, cache.astype(F32), rim)


def side_kernel(
    bc_ref,
    w_ref,
    bias_ref,
    near_ref,
    core_ref,
    cache_ref,
    cum_ref,
    step_ref,
    after_ref,
    co_ref,
    log_ref,
    row_ref,
    ecum_ref,
    ext,
):
    rows, heads = cum_ref.shape
    side = co_ref.shape[1]
    first = w_ref.shape[1] - side
    spare = ext.shape[0]
    for j in range(side // 128):
        cols = pl.ds(first + 128 * j, 128)
        ext[j % spare, 8 - RIM : 8, :] = before_block(
            near_ref[:, cols], core_ref[:, cols], cache_ref[:, cols]
        )
        values = bc_ref[:, pl.ds(side + 128 * j, 128)]
        total = convolve(values, w_ref, bias_ref, first + 128 * j, ext.at[j % spare], rows)
        co_ref[:, pl.ds(128 * j, 128)] = silu_of_twice(total).astype(BF16)
    cum, dt = cum_ref[...], step_ref[...]
    log_ref[...] = cum * LOG2E
    log_dt = jnp.where(dt > 0.0, jnp.log(jnp.maximum(dt, 1e-38)) * LOG2E, -1e30)
    row_ref[...] = (cum * LOG2E - log_dt).T
    ecum_hi, ecum_lo = split2(jnp.exp(cum))
    steps, _, twice = ecum_ref.shape
    for i in range(steps):
        part = slice(i * twice // 2, (i + 1) * twice // 2)
        ecum_ref[i] = jnp.concatenate([ecum_hi[:, part], ecum_lo[:, part]], axis=1)


def fix_kernel(
    near_ref,
    core_ref,
    cache_ref,
    w_ref,
    prex_ref,
    preb_ref,
    xc_ref,
    bc_ref,
    top_ref,
    local_ref,
    dec_ref,
    far_ref,
    near_out_ref,
    keep_ref,
    xfix_ref,
    bfix_ref,
    ext,
):
    device = lax.axis_index(SEQ)
    core = device % 2
    inner = xc_ref.shape[1]
    side = bc_ref.shape[1]
    ext[8:, :] = jnp.zeros((8, ext.shape[1]), F32)
    cols = pl.ds(0, ext.shape[1])
    ext[8 - RIM : 8, :] = before_block(near_ref[:, cols], core_ref[:, cols], cache_ref[:, cols])

    def fix(pre, old, dst, first, count):
        cols = pl.ds(first, count)
        total = pre[...]
        for k in range(RIM):
            total = total + ext[pl.ds(8 - RIM + k, 8), cols] * (0.5 * w_ref[k : k + 1, cols])
        fixed = silu_of_twice(total)
        dst[...] = jnp.concatenate([fixed, old[0:TOP, :].astype(F32)[8:, :]], axis=0).astype(BF16)
        return fixed.astype(BF16).astype(F32)

    x_top = fix(prex_ref, xc_ref, xfix_ref, 0, inner)
    b_top = fix(preb_ref, bc_ref, bfix_ref, inner, side)
    scaled = x_top * top_ref[...]
    scaled = jnp.concatenate([scaled, jnp.zeros_like(scaled)], axis=0).astype(BF16)
    b_top = jnp.concatenate([b_top, jnp.zeros_like(b_top)], axis=0)
    b_turned = b_top.T.astype(BF16)
    groups, _, width = local_ref.shape
    unit = width // 2
    side_bit = (device // 2) % 2
    for i in range(groups // PAIR):
        where = pl.ds(i * STATE, STATE)
        sends = []
        for y in range(PAIR):
            g = PAIR * i + y
            extra = jnp.dot(
                b_turned[g * STATE : (g + 1) * STATE, :],
                scaled[:, g * width : (g + 1) * width],
                preferred_element_type=F32,
            )
            whole_state = local_ref[g] + extra
            low, high = whole_state[:, :unit], whole_state[:, unit:]
            sends.append(jnp.where(core == 0, high, low))
            keep_ref[y, where, :] = jnp.where(core == 0, low, high).astype(BF16)
        far_ref[where, :] = jnp.where(side_bit == 0, sends[1], sends[0]).astype(BF16)
        near_out_ref[where, :] = jnp.where(side_bit == 0, sends[0], sends[1]).astype(BF16)
    where = pl.ds(groups // PAIR * STATE, 16)
    far_ref[where, :] = dec_ref[2 * (1 - side_bit) + 1 - core]
    near_out_ref[where, :] = dec_ref[2 * side_bit + 1 - core]
    for y in range(PAIR):
        keep_ref[y, where, :] = dec_ref[2 * y + core]


def cache_kernel(state_hbm, after_ref, out_ref, state_ref, held, sems, *, unit_heads):
    channels, size, heads = state_hbm.shape
    chunks = sems.shape[0]
    count = channels // chunks
    copies = []
    for c in range(chunks):
        part = pl.ds(c * count, count)
        copies.append(pltpu.make_async_copy(state_hbm.at[part], state_ref.at[part], sems.at[c]))
        copies[c].start()
    per_tile = 128 // unit_heads
    quarters = 2 * PAIR
    steps = heads // (quarters * unit_heads)
    quarter = lax.axis_index(SEQ) % quarters
    lane = lax.broadcasted_iota(jnp.int32, (size, 128), 1) // unit_heads
    for channel in range(channels):
        if channel % count == 0:
            copies[channel // count].wait()
        tile, place = channel // per_tile, channel % per_tile
        value = state_ref[channel]
        for i in range(steps):
            start = (i * quarters + quarter) * unit_heads
            moved = pltpu.roll(value, (place * unit_heads - start + heads) % heads, axis=1)
            if place == 0:
                held[tile, i] = moved
            else:
                held[tile, i] = jnp.where(lane == place, moved, held[tile, i])
    unit = out_ref.shape[1]
    dim = unit // unit_heads
    source = lax.broadcasted_iota(jnp.int32, (unit, unit), 0)
    target = lax.broadcasted_iota(jnp.int32, (unit, unit), 1)
    chosen = source == (target % dim) * unit_heads + target // dim
    order = jnp.where(chosen, 1.0, 0.0).astype(BF16)
    for i in range(steps):
        value = jnp.concatenate([held[t, i] for t in range(unit // 128)], axis=1)
        hi = value.astype(BF16)
        rest = value - hi.astype(F32)
        mid = rest.astype(BF16)
        low = (rest - mid.astype(F32)).astype(BF16)
        parts = jnp.dot(
            jnp.concatenate([hi, mid, low], axis=0), order, preferred_element_type=F32
        )
        out_ref[i * size : (i + 1) * size, :] = (
            parts[:size] + parts[size : 2 * size] + parts[2 * size :]
        )


def blocks_of(rows):
    return [(i, slice(i * STATE, (i + 1) * STATE)) for i in range(rows // STATE)]


def core_kernel(keep_ref, recv_ref, *rest, own):
    device = lax.axis_index(SEQ)
    core, side = device % 2, (device // 2) % 2
    out_ref = rest[-1]
    pick = side if own else 1 - side
    join_totals(keep_ref.at[pick], recv_ref, core == 0, out_ref, recv_ref.shape[0] - 16)


def join_totals(mine, other, mine_first, out, rows):
    d_mine = unpack_decay(mine[rows:, :])
    d_other = unpack_decay(other[rows:, :])
    d_later = jnp.where(mine_first, d_other, d_mine)
    f_mine = jnp.where(mine_first, d_later, 1.0)
    f_other = jnp.where(mine_first, 1.0, d_later)
    for i, part in blocks_of(rows):
        total = mine[part, :].astype(F32) * f_mine[i : i + 1] + other[part, :].astype(F32) * f_other[
            i : i + 1
        ]
        out[part, :] = total.astype(BF16)
    out[rows:, :] = pack_decay(d_mine * d_other)


def total_kernel(mine_ref, other_ref, cache_ref, c_ref, out_ref, *, bit):
    device = lax.axis_index(SEQ)
    rows = mine_ref.shape[0] - 16
    join_totals(mine_ref, other_ref, (device // bit) % 2 == 0, out_ref, rows)


def prefix_kernel(mine_ref, other_ref, pre_ref, dpre_ref, out_ref, opre_ref, odpre_ref, *, bit):
    device = lax.axis_index(SEQ)
    rows = mine_ref.shape[0] - 16
    first = (device // bit) % 2 == 0
    join_totals(mine_ref, other_ref, first, out_ref, rows)
    d_other = unpack_decay(other_ref[rows:, :])
    d_pre = dpre_ref[...]
    gain = jnp.where(first, 0.0, d_pre)
    for i, part in blocks_of(rows):
        opre_ref[part, :] = pre_ref[part, :] + gain[i : i + 1] * other_ref[part, :].astype(F32)
    odpre_ref[...] = jnp.where(first, d_pre, d_pre * d_other)


def start_kernel(mine_ref, other_ref, after_ref, out_ref, opre_ref, odpre_ref, *, bit):
    device = lax.axis_index(SEQ)
    rows = mine_ref.shape[0] - 16
    first = (device // bit) % 2 == 0
    join_totals(mine_ref, other_ref, first, out_ref, rows)
    d_other = unpack_decay(other_ref[rows:, :])
    opre_ref[...] = jnp.where(first, 0.0, other_ref[:rows, :].astype(F32))
    odpre_ref[...] = jnp.where(first, 1.0, d_other)


def enter_kernel(
    mine_ref,
    other_ref,
    pre_ref,
    dpre_ref,
    cache_ref,
    own_ref,
    recv_ref,
    after_ref,
    send_ref,
    stay_ref,
    fin_ref,
    *,
    bit,
):
    device = lax.axis_index(SEQ)
    side = (device // 2) % 2
    rows = mine_ref.shape[0] - 16
    first = (device // bit) % 2 == 0
    d_mine = unpack_decay(mine_ref[rows:, :])
    d_other = unpack_decay(other_ref[rows:, :])
    d_later = jnp.where(first, d_other, d_mine)
    f_mine = jnp.where(first, d_later, 1.0)
    f_other = jnp.where(first, 1.0, d_later)
    d_all = d_mine * d_other
    d_pre = dpre_ref[...]
    gain = jnp.where(first, 0.0, d_pre)
    d_before = jnp.where(first, d_pre, d_pre * d_other)
    d_first = jnp.where(side == 0, unpack_decay(own_ref[rows:, :]), unpack_decay(recv_ref[rows:, :]))
    for i, part in blocks_of(rows):
        cache = cache_ref[part, :]
        other = other_ref[part, :].astype(F32)
        mine = mine_ref[part, :].astype(F32)
        row = slice(i, i + 1)
        fin_ref[part, :] = d_all[row] * cache + mine * f_mine[row] + other * f_other[row]
        plane = d_before[row] * cache + pre_ref[part, :] + gain[row] * other
        t_first = jnp.where(side == 0, own_ref[part, :].astype(F32), recv_ref[part, :].astype(F32))
        second = d_first[row] * plane + t_first
        send_ref[part, :] = jnp.where(side == 0, second, plane).astype(BF16)
        stay_ref[part, :] = jnp.where(side == 0, plane, second).astype(BF16)


def chip_kernel(source_ref, keep_ref, part_ref, *rest, own):
    core, side = lax.axis_index(SEQ) % 2, (lax.axis_index(SEQ) // 2) % 2
    enter_block(source_ref, keep_ref, part_ref, rest[-1], core == 1, side if own else 1 - side)


def enter_block(source_ref, keep_ref, part_ref, out_ref, first, slot):
    core = lax.axis_index(SEQ) % 2
    rows = source_ref.shape[0]

    @pl.when(first)
    def _():
        out_ref[...] = source_ref[...]

    for kept, local in ((0, keep_ref.at[slot]), (1, part_ref)):

        @pl.when(jnp.logical_not(first) & (core == kept))
        def _(local=local):
            decay = unpack_decay(local[rows:, :])
            for i, part in blocks_of(rows):
                entered = decay[i : i + 1] * source_ref[part, :].astype(F32)
                out_ref[part, :] = (entered + local[part, :].astype(F32)).astype(BF16)


def diag_kernel(
    xc_ref,
    xfix_ref,
    b_ref,
    bfix_ref,
    c_ref,
    cum_ref,
    row_ref,
    skip_ref,
    after_ref,
    out_ref,
    *,
    head_dim,
    first,
):
    rows = xc_ref.shape[0]
    heads = cum_ref.shape[1]
    per_group = heads // GROUPS
    below = lax.broadcasted_iota(jnp.int32, (rows, rows), 0)
    across = lax.broadcasted_iota(jnp.int32, (rows, rows), 1)
    mask = below >= across
    quad = 128 // head_dim
    lane = lax.broadcasted_iota(jnp.int32, (rows, 128), 1) // head_dim
    for g in range(out_ref.shape[1] // (per_group * head_dim)):
        part = slice((first + g) * STATE, (first + g + 1) * STATE)
        b_all = jnp.concatenate([bfix_ref[:, part], b_ref[TOP:, part]], axis=0)
        c_dot_b = lax.dot_general(
            c_ref[:, part], b_all, (((1,), (1,)), ((), ())), preferred_element_type=F32
        )
        for q in range(per_group // quad):
            base = (first + g) * per_group + q * quad
            cols = pl.ds(base * head_dim, 128)
            x_quad = jnp.concatenate([xfix_ref[:, cols], xc_ref[TOP:, cols]], axis=0)
            lhs, rhs = [], []
            for k in range(quad):
                head = base + k
                gap = cum_ref[:, head : head + 1] - row_ref[head : head + 1, :]
                decay = jnp.exp2(jnp.where(mask, gap, -1e30))
                lhs.append((c_dot_b * decay).astype(BF16))
                rhs.append(jnp.where(lane == k, x_quad, jnp.zeros_like(x_quad)))
            skip = skip_ref[:, base : base + 1]
            for k in range(1, quad):
                skip = jnp.where(lane[0:1] == k, skip_ref[:, base + k : base + k + 1], skip)
            inner = jnp.dot(
                jnp.concatenate(lhs, axis=1),
                jnp.concatenate(rhs, axis=0),
                preferred_element_type=F32,
            )
            out = pl.ds((g * per_group + q * quad) * head_dim, 128)
            out_ref[:, out] = inner + skip * x_quad.astype(F32)


def gate_kernel(len_ref, z_ref, after_ref, gate_ref):
    rows, width = z_ref.shape
    first = lax.axis_index(SEQ) * rows
    live = first + lax.broadcasted_iota(jnp.int32, (rows, 128), 0) < len_ref[0]
    for j in range(width // 128):
        cols = pl.ds(128 * j, 128)
        gate_ref[:, cols] = jnp.where(live, silu(z_ref[:, cols].astype(F32)), 0.0)


def grow_kernel(ecum_ref, final_ref, grow_ref, mine_ref, *, head_dim):
    steps = ecum_ref.shape[0]
    per_step = ecum_ref.shape[2] // 2
    width = per_step * head_dim
    head = lax.broadcasted_iota(jnp.int32, (2 * per_step, width), 0) % per_step
    lane = lax.broadcasted_iota(jnp.int32, (2 * per_step, width), 1)
    spread = jnp.where(head == lane // head_dim, 1.0, 0.0).astype(BF16)
    for i in range(steps):
        grow_ref[:, i * width : (i + 1) * width] = jnp.dot(
            ecum_ref[i], spread, preferred_element_type=F32
        )
    step = (lax.axis_index(SEQ) // (2 * PAIR)) % (final_ref.shape[0] // STATE)
    mine = final_ref[pl.ds(pl.multiple_of(step * STATE, STATE), STATE), :]
    mine_ref[...] = mine.T


def gated_part(parts, gate_ref, grow_ref, c_ref, state, i, y, half):
    width = gate_ref.shape[1] // GROUPS
    unit = width // 2
    per_part = GROUPS // len(parts)
    offset = y * width + half * unit
    inside = pl.ds(pl.multiple_of(PAIR * i % per_part * width + offset, 128), unit)
    cols = pl.ds(pl.multiple_of(PAIR * i * width + offset, 128), unit)
    both = c_ref[:, PAIR * i * STATE : PAIR * (i + 1) * STATE]
    c_group = jnp.where(y == 0, both[:, :STATE], both[:, STATE:])
    entering = jnp.dot(c_group, state, preferred_element_type=F32)
    y_all = parts[PAIR * i // per_part][:, inside] + grow_ref[:, cols] * entering
    return y_all.astype(BF16).astype(F32) * gate_ref[:, cols], cols


def sum_lanes(value):
    return sum(value[:, j : j + 128] for j in range(0, value.shape[1], 128))


def finish_group(held, i, y, halves, squares, out_ref, sems):
    unit = halves[0][1].shape[1]
    scale = lax.rsqrt(jnp.sum(squares, axis=1, keepdims=True) * (0.5 / unit) + 1e-05)
    for half, value in halves:
        held[i, :, pl.ds(pl.multiple_of(half * unit, 128), unit)] = (value * scale).astype(BF16)
    first = pl.multiple_of((PAIR * i + y) * 2 * unit, 128)
    copy = pltpu.make_async_copy(held.at[i], out_ref.at[:, pl.ds(first, 2 * unit)], sems.at[i])
    copy.start()
    return copy


def own_kernel(*refs, parts):
    diag_refs, refs = refs[:parts], refs[parts:]
    gate_ref, grow_ref, c_ref, gain_ref, stay_ref, recv_ref, keep_ref, far_ref, near_ref, enter_ref = refs[:10]
    out_ref, gated_ref, sums_ref, own_ref, held, sems = refs[11:]
    core, side = lax.axis_index(SEQ) % 2, (lax.axis_index(SEQ) // 2) % 2
    steps = held.shape[0]
    given = (diag_refs, gate_ref, grow_ref, c_ref)
    enter_block(stay_ref, keep_ref, near_ref, own_ref.at[0], core == 0, side)
    copies = []
    for i in range(steps):
        part = slice(i * STATE, (i + 1) * STATE)
        own, own_cols = gated_part(*given, own_ref[0, part, :], i, side, core)
        other, cols = gated_part(*given, enter_ref[part, :], i, side, 1 - core)
        squares = sum_lanes(own * own) + sum_lanes(other * other)
        halves = ((core, own * gain_ref[:, own_cols]), (1 - core, other * gain_ref[:, cols]))
        copies.append(finish_group(held, i, side, halves, squares, out_ref, sems))
    enter_block(recv_ref, keep_ref, far_ref, own_ref.at[1], core == 0, 1 - side)
    for i in range(steps):
        part = slice(i * STATE, (i + 1) * STATE)
        own, own_cols = gated_part(*given, own_ref[1, part, :], i, 1 - side, core)
        sums_ref[i] = sum_lanes(own * own)
        gated_ref[i] = own * gain_ref[:, own_cols]
    for copy in copies:
        copy.wait()


def out_kernel(*refs, parts):
    diag_refs, refs = refs[:parts], refs[parts:]
    gate_ref, grow_ref, c_ref, gated_ref, sums_ref, enter_ref, gain_ref = refs[:7]
    out_ref, held, sems = refs[8:]
    core, side = lax.axis_index(SEQ) % 2, (lax.axis_index(SEQ) // 2) % 2
    given = (diag_refs, gate_ref, grow_ref, c_ref)
    copies = []
    for i in range(held.shape[0]):
        part = slice(i * STATE, (i + 1) * STATE)
        other, cols = gated_part(*given, enter_ref[part, :], i, 1 - side, 1 - core)
        squares = sums_ref[i] + sum_lanes(other * other)
        halves = ((core, gated_ref[i]), (1 - core, other * gain_ref[:, cols]))
        copies.append(finish_group(held, i, 1 - side, halves, squares, out_ref, sems))
    for copy in copies:
        copy.wait()


def swap(value, mask):
    devices = range(lax.axis_size(SEQ))
    return lax.ppermute(value, SEQ, [(i, i ^ mask) for i in devices])


def chip_route(count):
    route = {i: i + 1 for i in range(1, count - 1, 2)}
    route.update({i: i - 1 for i in range(4, count - 2, 2)})
    route.update({2: 0, 0: 1, count - 2: count - 1, count - 1: count - 3})
    return sorted(route.items())


def near(shape, dtype):
    return pltpu.VMEM(shape, dtype)


VMEM_SPEC = pl.BlockSpec(memory_space=pltpu.VMEM)
ANY_SPEC = pl.BlockSpec(memory_space=pl.ANY)


def plain_call(
    body, out_shape, *args, smem=(), far=(), after=(), mib=12, nbytes=2**20, scratch=(), out_specs=None, aliases=None
):
    return pl.pallas_call(
        body,
        out_shape=out_shape,
        in_specs=[pl.BlockSpec(memory_space=pltpu.SMEM)] * len(smem)
        + [ANY_SPEC] * len(far)
        + [VMEM_SPEC] * len(args) + [ANY_SPEC] * len(after),
        out_specs=out_specs or jax.tree.map(lambda _: VMEM_SPEC, out_shape),
        scratch_shapes=list(scratch),
        input_output_aliases=aliases or {},
        compiler_params=pltpu.CompilerParams(vmem_limit_bytes=mib * 2**20),
        cost_estimate=pl.CostEstimate(flops=0, bytes_accessed=nbytes, transcendentals=0),
    )(*smem, *[pltpu.with_memory_space_constraint(a, pltpu.HBM) for a in far], *args, *after)


def body(
    x_in,
    bc_in,
    z_in,
    dt_in,
    conv_weight,
    conv_bias,
    dt_bias,
    a_log,
    d_skip,
    norm_gain,
    conv_cache,
    cache_state,
    lengths,
):
    rows, inner = x_in.shape
    heads = dt_in.shape[1]
    head_dim = inner // heads
    devices = lax.axis_size(SEQ)
    index = lax.axis_index(SEQ)
    share = heads // devices
    steps = GROUPS // PAIR
    per_step = heads // steps
    width = inner // steps
    side = GROUPS * STATE
    unit = width // (2 * PAIR)
    unit_heads = unit // head_dim
    state_rows = steps * STATE
    msg_rows = state_rows + 16
    dma = pltpu.SemaphoreType.DMA

    fetched = [
        x_in,
        bc_in,
        conv_weight,
        conv_bias.reshape(1, -1),
        dt_in,
        dt_bias.reshape(1, -1),
        a_log.reshape(1, -1),
        norm_gain.reshape(1, -1),
    ]
    rim, *ready = plain_call(
        functools.partial(rim_kernel, count=len(fetched)),
        [near((RIM, inner + 2 * side), BF16)] + [near(a.shape, a.dtype) for a in fetched],
        far=fetched,
        mib=4,
        scratch=[
            pltpu.VMEM((TOP, inner), BF16),
            pltpu.VMEM((TOP, 2 * side), BF16),
            dma((2 + len(fetched),)),
        ],
    )
    near_rim = lax.ppermute(rim, SEQ, chip_route(devices))
    core_rim = swap(rim, 1)

    xc, bc, prex, preb, cum, step_size, dec, top, local = plain_call(
        functools.partial(conv_kernel, heads=heads, head_dim=head_dim),
        (
            near((rows, inner), BF16),
            near((rows, side), BF16),
            near((8, inner), F32),
            near((8, side), F32),
            near((rows, heads), F32),
            near((rows, heads), F32),
            near((2 * PAIR, 16, unit), BF16),
            near((8, inner), F32),
            near((GROUPS, STATE, width // PAIR), F32),
        ),
        *ready[:-1],
        smem=(lengths,),
        after=(rim,),
        scratch=[
            pltpu.VMEM((4, 8 + rows, 128), F32),
            pltpu.VMEM((2, rows, width), F32),
            pltpu.VMEM((2, rows, width), BF16),
        ],
        mib=16,
        nbytes=4 * 2**20,
    )

    pair_msg = near((PAIR, msg_rows, unit), BF16)
    message = near((msg_rows, unit), BF16)
    send_far, send_near, keep, xfix, bfix = plain_call(
        fix_kernel,
        (message, message, pair_msg, near((TOP, inner), BF16), near((TOP, side), BF16)),
        near_rim,
        core_rim,
        conv_cache,
        ready[2],
        prex,
        preb,
        xc,
        bc,
        top,
        local,
        dec,
        scratch=[pltpu.VMEM((16, inner + side), F32)],
    )

    part_far = swap(send_far, 1)
    part_near = swap(send_near, 1)
    send_y = plain_call(functools.partial(core_kernel, own=False), message, keep, part_far)
    recv = swap(send_y, 2)
    own = plain_call(
        functools.partial(core_kernel, own=True), message, keep, part_near, after=(send_y,)
    )
    chunks = 4
    cache = plain_call(
        functools.partial(cache_kernel, unit_heads=unit_heads),
        near((state_rows, unit), F32),
        far=(cache_state.transpose(1, 2, 0),),
        after=(own,),
        scratch=[
            pltpu.VMEM((head_dim, STATE, heads), F32),
            pltpu.VMEM((unit // 128, steps, STATE, 128), F32),
            dma((chunks,)),
        ],
        nbytes=2 * 2**20,
    )
    cc, log_cum, row, ecum = plain_call(
        side_kernel,
        (
            near((rows, side), BF16),
            near((rows, heads), F32),
            near((heads, rows), F32),
            near((steps, rows, 2 * per_step), BF16),
        ),
        ready[1],
        ready[2],
        ready[3],
        near_rim,
        core_rim,
        conv_cache,
        cum,
        step_size,
        after=(own,),
        scratch=[pltpu.VMEM((4, 8 + rows, 128), F32)],
    )
    total = plain_call(
        functools.partial(total_kernel, bit=2), message, own, recv, after=(cache, cc)
    )

    def diag_part(k, order):
        return plain_call(
            functools.partial(diag_kernel, head_dim=head_dim, first=k * GROUPS // 2),
            near((rows, inner // 2), F32),
            xc,
            xfix,
            bc,
            bfix,
            cc,
            log_cum,
            row,
            d_skip.reshape(1, -1),
            after=(order,),
            nbytes=4 * 2**20,
        )

    diags = [diag_part(0, total)]
    pre = None
    bit = 4
    pre_shape = (near((state_rows, unit), F32), near((8, unit), F32))
    while 2 * bit < devices:
        other = swap(total, 2 * bit - 4)
        if pre is None:
            total, *pre = plain_call(
                functools.partial(start_kernel, bit=bit),
                (message,) + pre_shape,
                total,
                other,
                after=(diags[0],),
            )
        else:
            total, *pre = plain_call(
                functools.partial(prefix_kernel, bit=bit), (message,) + pre_shape, total, other, *pre
            )
        bit *= 2
    if pre is None:
        pre = [jnp.zeros((state_rows, unit), F32), jnp.ones((8, unit), F32)]
    last = total
    other = swap(last, 2 * bit - 4)
    diags.append(diag_part(1, last))
    state_out = near((state_rows, unit), BF16)
    send_y, stay, final = plain_call(
        functools.partial(enter_kernel, bit=bit),
        (state_out, state_out, near((state_rows, unit), F32)),
        total,
        other,
        *pre,
        cache,
        own,
        recv,
        after=(diags[1],),
    )
    recv_y = swap(send_y, 2)
    grow, mine = plain_call(
        functools.partial(grow_kernel, head_dim=head_dim),
        (near((rows, inner), F32), jax.ShapeDtypeStruct((unit, STATE), F32)),
        ecum,
        final,
        nbytes=5 * 2**20,
    )
    gate = plain_call(
        gate_kernel, near((rows, inner), F32), z_in, smem=(lengths,), after=(final,)
    )
    send_near = plain_call(
        functools.partial(chip_kernel, own=True),
        state_out,
        stay,
        keep,
        part_near,
        after=(gate, grow),
    )
    enter_near = swap(send_near, 1)
    send_far = plain_call(
        functools.partial(chip_kernel, own=False),
        state_out,
        recv_y,
        keep,
        part_far,
        after=(send_near,),
    )
    enter_far = swap(send_far, 1)
    gain = ready[-1]
    held = [pltpu.VMEM((steps, rows, 2 * unit), BF16), dma((steps,))]
    shared = (*diags, gate, grow, cc)
    mixed, gated_own, own_sums = plain_call(
        functools.partial(own_kernel, parts=len(diags)),
        (
            pltpu.HBM((rows, inner), BF16),
            near((steps, rows, unit), F32),
            near((steps, rows, 128), F32),
        ),
        *shared,
        gain,
        stay,
        recv_y,
        keep,
        part_far,
        part_near,
        enter_near,
        after=(send_far,),
        out_specs=(ANY_SPEC, VMEM_SPEC, VMEM_SPEC),
        scratch=[pltpu.VMEM((2, state_rows, unit), BF16)] + held,
    )
    operands = (*shared, gated_own, own_sums, enter_far, gain)
    mixed = plain_call(
        functools.partial(out_kernel, parts=len(diags)),
        pltpu.HBM((rows, inner), BF16),
        *operands,
        after=(mixed,),
        out_specs=ANY_SPEC,
        scratch=held,
        aliases={len(operands): 0},
        nbytes=4 * 2**20,
    )

    if share * head_dim == unit and devices == 2 * PAIR * steps:
        mine = mine.reshape(share, head_dim, STATE)
    else:
        around = [[4 * i + j for j in range(4)] for i in range(devices // 4)]
        every = final.reshape(steps, STATE, unit)
        every = lax.all_gather(every, SEQ, axis=1, axis_index_groups=around)
        every = every.reshape(steps * 2 * PAIR, STATE, unit).transpose(0, 2, 1)
        every = every.reshape(heads, head_dim, STATE)
        mine = lax.dynamic_slice_in_dim(every, index * share, share, 0)
    return (mixed, mine)


def solution(mesh):
    in_specs = (
        P(("groups", "seq"), None),
        P(("groups", "seq"), None),
        P(("groups", "seq"), None),
        P(("groups", "seq"), None),
        P(),
        P(),
        P(),
        P(),
        P(),
        P(),
        P("groups", None),
        P("groups", None, None),
        P("groups"),
    )
    out_specs = (P(("groups", "seq"), None), P(("groups", "seq"), None, None))
    return jax.shard_map(body, mesh=mesh, in_specs=in_specs, out_specs=out_specs, check_vma=False)
```
